32 devices in a mesh: tri: 8 (over z, x), rhs: 2 (over y), split: 2 (over core).
Axes of the slice: x: 2, y: 2, z: 4, core: 2. Of those that a mesh axis runs over, the one named last changes fastest.
Arguments:
- residual: float32 [256, 16384], P('rhs', ('tri', 'split')), may hold values from -6 to 6
- attach: int32 [256], P('rhs'), may hold values from 0 to 16383
- vertices: float32 [3, 8192], replicated, may hold values from -3 to 3
- corners: int32 [3, 16384], replicated, may hold values from 0 to 8191
- layers: int32 [16384], replicated, may hold values from 0 to 2
Outputs:
- solution: float32 [256, 16384], P('rhs', ('tri', 'split'))
- remainder: float32 [256, 16384], P('rhs', ('tri', 'split'))
- direction: float32 [256, 16384], P('rhs', ('tri', 'split'))
The draws below stay inside these ranges and needn't reach their ends.
All inputs are finite; a program needn't handle non-finite values.
Results may differ from the reference program's by a relative error of at most 0.011.
Values may be sent and summed in bfloat16 or wider, within the bound.
No kernel may reach another device: no remote copies, remote signals or barrier semaphores. Data moves between devices by JAX's collectives and lax.ppermute only.
A program may use at most 192 MiB of HBM per device.

```python
import math
import jax
import jax.numpy as jnp
from jax import lax

R = 256
TRI_DEV = 1024
TRIS = 16384
VERTS = 8192


def touch_ends(values, own_key, low, largest):
    dims = values.shape
    place = [jax.random.randint(jax.random.fold_in(own_key, axis), (), 0, dims[axis]) for axis in range(len(dims))]
    values = values.at[tuple(place)].set(low)
    longest = dims.index(max(dims))
    place[longest] = (place[longest] + 1) % dims[longest]
    return values.at[tuple(place)].set(largest)


def levels(key, shape, cuts, low, top_value):
    loudness, own = 1.0, jax.random.fold_in(key, 6)
    for axis_at, parts in cuts:
        heights = jnp.exp(jax.random.uniform(jax.random.fold_in(own, axis_at), (parts,), jnp.float32, low / len(cuts), top_value / len(cuts)))
        loudness = loudness * jnp.repeat(heights, shape[axis_at] // parts).reshape([-1 if axis == axis_at else 1 for axis in range(len(shape))])
    return loudness


def scatter_about(key, extent, deviation, reach, cuts=(), kind=jnp.bfloat16):
    result = jax.random.normal(key, extent, jnp.float32) * deviation
    if len(cuts) > 0:
        result = levels(key, extent, cuts, -0.22, 0.18) * result
    return jnp.clip(result, min=-reach, max=reach).astype(kind)


def setup_inputs(seed: int = 0) -> dict:
    arg_keys = jax.random.split(jax.random.key(seed), 6)
    return {
        "residual": scatter_about(arg_keys[0], (R, TRIS), 1.0, 6.0, ((0, 2), (1, 16)), jnp.float32),
        "attach": touch_ends(jax.random.randint(arg_keys[1], (R,), 0, TRIS), jax.random.fold_in(arg_keys[1], 1), 0, TRIS - 1).astype(jnp.int32),
        "vertices": scatter_about(arg_keys[2], (3, VERTS), 0.5, 3.0, (), jnp.float32),
        "corners": touch_ends(jax.random.randint(arg_keys[3], (3, TRIS), 0, VERTS), jax.random.fold_in(arg_keys[3], 1), 0, VERTS - 1).astype(jnp.int32),
        "layers": touch_ends(jax.random.randint(arg_keys[4], (TRIS,), 0, 3), jax.random.fold_in(arg_keys[4], 1), 0, 2).astype(jnp.int32),
    }


smooth_sq = 0.01
self_term = 1.0
inject = 3.0

def geometry(vertices, corners, layers):
    points = vertices[:, corners]
    centre = (points[:, 0] + points[:, 1] + points[:, 2]) / 3.0
    edge_one = points[:, 1] - points[:, 0]
    edge_two = points[:, 2] - points[:, 0]
    cross_x = edge_one[1] * edge_two[2] - edge_one[2] * edge_two[1]
    cross_y = edge_one[2] * edge_two[0] - edge_one[0] * edge_two[2]
    cross_z = edge_one[0] * edge_two[1] - edge_one[1] * edge_two[0]
    area_sq = cross_x * cross_x + cross_y * cross_y + cross_z * cross_z
    factor = jnp.where(layers == 0, 1.0, jnp.where(layers == 1, 0.3, 0.8)).astype(jnp.float32)
    weight = factor * (0.5 + area_sq / (1.0 + area_sq))
    return (centre, weight)

def kernel_tile(cent_rows, weight_rows, ids_rows, cent_cols, weight_cols, ids_cols, scale):
    delta = cent_rows[0][:, None] - cent_cols[0][None, :]
    dist_sq = delta * delta
    delta = cent_rows[1][:, None] - cent_cols[1][None, :]
    dist_sq = dist_sq + delta * delta
    delta = cent_rows[2][:, None] - cent_cols[2][None, :]
    dist_sq = dist_sq + delta * delta
    inverse = lax.rsqrt(dist_sq + smooth_sq)
    same = jnp.where(ids_rows[:, None] == ids_cols[None, :], self_term, 0.0)
    value = weight_rows[:, None] * weight_cols[None, :] * (inverse * scale + same)
    return value.astype(jnp.bfloat16)

def reference(residual, attach, vertices, corners, layers):
    highest = lax.Precision.HIGHEST
    centre, weight = geometry(vertices, corners, layers)
    ids_all = jnp.arange(TRIS, dtype=jnp.int32)
    current = residual + inject * (attach[:, None] == ids_all[None, :]).astype(jnp.float32)
    packed = current.astype(jnp.bfloat16)
    scale = 1.0 / math.sqrt(TRIS)

    def one_block(index):
        begin = (index * TRI_DEV).astype(jnp.int32)
        cent_rows = lax.dynamic_slice_in_dim(centre, begin, TRI_DEV, 1)
        weight_rows = lax.dynamic_slice_in_dim(weight, begin, TRI_DEV, 0)
        ids_rows = begin + jnp.arange(TRI_DEV, dtype=jnp.int32)
        tile = kernel_tile(cent_rows, weight_rows, ids_rows, centre, weight, ids_all, scale)
        return jnp.dot(packed.astype(jnp.float32), tile.T.astype(jnp.float32), preferred_element_type=jnp.float32)
    pieces = lax.map(one_block, jnp.arange(TRIS // TRI_DEV, dtype=jnp.int32))
    image = jnp.transpose(pieces, (1, 0, 2)).reshape(R, TRIS)
    gram = jnp.dot(current, image.T, precision=highest)
    gram = 0.5 * (gram + gram.T)
    square = jnp.dot(current, current.T, precision=highest)
    step = jax.scipy.linalg.cho_solve((jnp.linalg.cholesky(gram), True), square)
    solution = jnp.dot(step.T, current, precision=highest)
    remainder = current - jnp.dot(step.T, image, precision=highest)
    square_next = jnp.dot(remainder, remainder.T, precision=highest)
    turn = jax.scipy.linalg.cho_solve((jnp.linalg.cholesky(square), True), square_next)
    direction = remainder + jnp.dot(turn.T, current, precision=highest)
    return (solution, remainder, direction)
```

```python
import functools
import math

import jax
import jax.numpy as jnp
from jax import lax
from jax.experimental import pallas as pl
from jax.experimental.pallas import tpu as pltpu
from jax.sharding import PartitionSpec as P

smooth_sq = 0.01
self_term = 1.0
inject = 3.0
f32 = jnp.float32
bf16 = jnp.bfloat16
LANES = 128
FEATURES = 32
PAIRS = ((0, 0), (0, 1), (1, 0), (1, 1), (0, 2), (2, 0))
VMEM = pl.BlockSpec(memory_space=pltpu.VMEM)
SMEM = pl.BlockSpec(memory_space=pltpu.SMEM)


def dot(a, b, ca, cb, precision=None):
    return lax.dot_general(
        a, b, (((ca,), (cb,)), ((), ())), precision=precision, preferred_element_type=f32
    )


def exact_dot(a, b, ca, cb):
    return dot(a, b, ca, cb, lax.Precision.HIGHEST)


def params():
    return pltpu.CompilerParams(vmem_limit_bytes=48 * 1024 * 1024)


def pieces_of(value):
    high = value.astype(bf16).astype(f32)
    rest = value - high
    middle = rest.astype(bf16).astype(f32)
    return (high, middle, rest - middle)


def geometry_kernel(scale, blocks_ref, table_ref, corners_ref, layers_ref, a_ref, b_ref, diag_ref, a_rows, b_rows):
    count = corners_ref.shape[1]
    tops = table_ref.shape[1]
    table = [[part.astype(bf16) for part in pieces_of(table_ref[axis])] for axis in range(3)]
    top_iota = lax.broadcasted_iota(jnp.int32, (tops, count), 0)
    low_iota = lax.broadcasted_iota(jnp.int32, (LANES, count), 0)
    points = []
    for corner in range(3):
        index = corners_ref[corner : corner + 1, :]
        top = jnp.where(top_iota == (index >> 7), 1.0, 0.0).astype(bf16)
        low = low_iota == (index & (LANES - 1))
        point = []
        for axis in range(3):
            high, middle, rest = (dot(part, top, 0, 0) for part in table[axis])
            point.append(jnp.sum(jnp.where(low, (high + middle) + rest, 0.0), axis=0, keepdims=True))
        points.append(point)
    p0, p1, p2 = points
    centre = [(p0[k] + p1[k] + p2[k]) / 3.0 for k in range(3)]
    e1 = [p1[k] - p0[k] for k in range(3)]
    e2 = [p2[k] - p0[k] for k in range(3)]
    cross_x = e1[1] * e2[2] - e1[2] * e2[1]
    cross_y = e1[2] * e2[0] - e1[0] * e2[2]
    cross_z = e1[0] * e2[1] - e1[1] * e2[0]
    area_sq = cross_x * cross_x + cross_y * cross_y + cross_z * cross_z
    layers = layers_ref[...]
    factor = jnp.where(layers == 0, 1.0, jnp.where(layers == 1, 0.3, 0.8)).astype(f32)
    weight = factor * (0.5 + area_sq / (1.0 + area_sq))
    unit = 1.0 / (scale * (weight * weight))
    norm = centre[0] * centre[0] + centre[1] * centre[1] + centre[2] * centre[2]
    a_side = [unit * norm, unit] + [unit * c for c in centre]
    b_side = [unit, unit * (norm + smooth_sq)] + [-2.0 * unit * c for c in centre]
    a_parts = [pieces_of(value) for value in a_side]
    b_parts = [pieces_of(value) for value in b_side]
    row = 0
    for a_piece, b_piece in PAIRS:
        for term in range(5):
            a_rows[row : row + 1, :] = a_parts[term][a_piece]
            b_rows[row : row + 1, :] = b_parts[term][b_piece]
            row += 1
    blank = jnp.zeros((FEATURES - row, count), f32)
    a_rows[row:, :] = blank
    b_rows[row:, :] = blank
    a_ref[...] = a_rows[...].astype(bf16)
    b_ref[...] = b_rows[...].astype(bf16)
    diag_ref[...] = weight * weight * (lax.rsqrt(jnp.full_like(weight, smooth_sq)) * scale + self_term)


def geometry(blocks, table, corners, layers, count, scale):
    n = blocks.shape[0]
    tops = table.shape[1]
    feature = jax.ShapeDtypeStruct((n, FEATURES, count), bf16)
    return pl.pallas_call(
        functools.partial(geometry_kernel, scale),
        grid_spec=pltpu.PrefetchScalarGridSpec(
            num_scalar_prefetch=1,
            grid=(n,),
            in_specs=[
                pl.BlockSpec((3, tops, LANES), lambda g, blk: (0, 0, 0)),
                pl.BlockSpec((3, count), lambda g, blk: (0, blk[g])),
                pl.BlockSpec((1, count), lambda g, blk: (0, blk[g])),
            ],
            out_specs=[
                pl.BlockSpec((None, FEATURES, count), lambda g, blk: (g, 0, 0)),
                pl.BlockSpec((None, FEATURES, count), lambda g, blk: (g, 0, 0)),
                pl.BlockSpec((None, 1, count), lambda g, blk: (g, 0, 0)),
            ],
            scratch_shapes=[pltpu.VMEM((FEATURES, count), f32), pltpu.VMEM((FEATURES, count), f32)],
        ),
        out_shape=(feature, feature, jax.ShapeDtypeStruct((n, 1, count), f32)),
        compiler_params=params(),
        name="geometry",
    )(blocks, table, corners, layers[None, :])


def image_kernel(sources, has_start, has_diag, *refs):
    refs = list(refs)
    densities = [refs.pop(0) for _ in range(sources)]
    a_refs = [refs.pop(0) for _ in range(sources)]
    b_ref = refs.pop(0)
    diag_ref = refs.pop(0) if has_diag else None
    start_ref = refs.pop(0) if has_start else None
    out_ref = refs.pop(0)
    targets, columns, count = out_ref.shape
    chunk = min(512, count)

    def one(target, with_diag):
        b = b_ref[target]
        acc = start_ref[target] if has_start else jnp.zeros((columns, count), f32)
        for density, a_ref in zip(densities, a_refs):
            for begin in range(0, count, chunk):
                tile = lax.rsqrt(dot(a_ref[:, begin : begin + chunk], b, 0, 0))
                if with_diag:
                    rows = begin + lax.broadcasted_iota(jnp.int32, tile.shape, 0)
                    cols = lax.broadcasted_iota(jnp.int32, tile.shape, 1)
                    tile = jnp.where(rows == cols, diag_ref[...], tile)
                acc = acc + dot(density[:, begin : begin + chunk], tile.astype(bf16), 1, 0)
        out_ref[target] = acc

    if has_diag:
        one(0, True)
    if targets > int(has_diag):

        @pl.loop(int(has_diag), targets)
        def _(target):
            one(target, False)


def image_part(densities, a_side, b_side, start=None, diag=None):
    columns, count = densities[0].shape
    targets = b_side.shape[0]
    operands = [*densities, *a_side, b_side]
    if diag is not None:
        operands.append(diag)
    if start is not None:
        operands.append(start)
    entries = len(densities) * count * targets * count
    return pl.pallas_call(
        functools.partial(image_kernel, len(densities), start is not None, diag is not None),
        in_specs=[VMEM] * len(operands),
        out_specs=VMEM,
        out_shape=jax.ShapeDtypeStruct((targets, columns, count), f32),
        compiler_params=params(),
        cost_estimate=pl.CostEstimate(
            flops=2 * entries * (columns + FEATURES), bytes_accessed=8 * targets * columns * count, transcendentals=entries
        ),
        name="image_part",
    )(*operands)


def gram_kernel(ranks, place_ref, *refs):
    currents, images = refs[:ranks], refs[ranks : 2 * ranks]
    current_ref, image_ref, sums_ref = refs[2 * ranks :]
    columns, count = currents[0].shape
    for rank in range(ranks):
        at = pl.ds(pl.multiple_of(place_ref[rank] * columns, columns), columns)
        current_ref[at, :] = currents[rank][...]
        image_ref[at, :] = images[rank][...]
    width = count // ranks
    mine = pl.ds(pl.multiple_of(place_ref[0] * width, width), width)
    current = current_ref[:, mine]
    image = image_ref[:, mine]
    total = ranks * columns
    sums_ref[:total] = exact_dot(current, image, 1, 1)
    sums_ref[total : 2 * total] = exact_dot(current, current, 1, 1)
    sums_ref[2 * total :] = exact_dot(image, image, 1, 1)


def gram_sums(places, currents, images):
    ranks = len(currents)
    columns, count = currents[0].shape
    whole = jax.ShapeDtypeStruct((ranks * columns, count), f32)
    return pl.pallas_call(
        functools.partial(gram_kernel, ranks),
        in_specs=[SMEM] + [VMEM] * (2 * ranks),
        out_specs=[VMEM] * 3,
        out_shape=(whole, whole, jax.ShapeDtypeStruct((3 * ranks * columns, ranks * columns), f32)),
        compiler_params=params(),
        name="gram",
    )(places, *currents, *images)


def invert_small(block):
    size = block.shape[0]
    row_at = lax.broadcasted_iota(jnp.int32, block.shape, 0)
    col_at = lax.broadcasted_iota(jnp.int32, block.shape, 1)
    for step in range(size):
        inverse = 1.0 / block[step : step + 1, step : step + 1]
        row = jnp.where(col_at[:1] == step, 1.0, block[step : step + 1, :]) * inverse
        col = block[:, step : step + 1]
        block = jnp.where(row_at == step, row, jnp.where(col_at == step, 0.0, block) - col * row)
    return block


def sweep(ref, begin, size):
    total = ref.shape[0]
    panel = ref[begin : begin + size, :]
    inverse = invert_small(panel[:, begin : begin + size])
    row_at = lax.broadcasted_iota(jnp.int32, panel.shape, 0)
    col_at = lax.broadcasted_iota(jnp.int32, panel.shape, 1)
    inside = (col_at >= begin) & (col_at < begin + size)
    eye = jnp.where(col_at == row_at + begin, 1.0, 0.0)
    row = exact_dot(inverse, jnp.where(inside, eye, panel), 1, 0)
    signed = jnp.where(col_at < begin, -panel, panel)
    update = exact_dot(signed, row, 0, 0)
    lanes = lax.broadcasted_iota(jnp.int32, (total, total), 1)
    ref[...] = jnp.where((lanes >= begin) & (lanes < begin + size), 0.0, ref[...]) - update
    ref[begin : begin + size, :] = row


def solve_kernel(columns, size, place_ref, sums_ref, step_ref, turn_ref, gram_inv, square_inv, step_all):
    total = sums_ref.shape[1]
    cross = sums_ref[:total]
    gram_inv[...] = 0.5 * (cross + cross.T)
    square_inv[...] = sums_ref[total : 2 * total]
    for begin in range(0, total, size):
        sweep(gram_inv, begin, size)
        sweep(square_inv, begin, size)
    mine = pl.ds(pl.multiple_of(place_ref[0] * columns, columns), columns)
    step_all[...] = exact_dot(sums_ref[total : 2 * total], gram_inv[...], 1, 0)
    step = step_all[mine, :]
    step_ref[...] = step
    square_rows = sums_ref[pl.ds(pl.multiple_of(total + place_ref[0] * columns, columns), columns), :]
    cross_rows = sums_ref[mine, :]
    left = exact_dot(step, sums_ref[2 * total :], 1, 0) - cross_rows
    following = square_rows - exact_dot(step, sums_ref[:total], 1, 1) + exact_dot(left, step_all[...], 1, 1)
    turn_ref[...] = exact_dot(following, square_inv[...], 1, 0)


def solve(places, sums, columns):
    total = sums.shape[1]
    square = pltpu.VMEM((total, total), f32)
    rows = jax.ShapeDtypeStruct((columns, total), f32)
    return pl.pallas_call(
        functools.partial(solve_kernel, columns, 32),
        in_specs=[SMEM, VMEM],
        out_specs=[VMEM] * 2,
        out_shape=(rows, rows),
        scratch_shapes=[square, square, square],
        compiler_params=params(),
        name="solve",
    )(places, sums)


def finish_kernel(mine_ref, current_ref, image_ref, step_ref, turn_ref, solution_ref, remainder_ref, direction_ref):
    current = current_ref[...]
    step = step_ref[...]
    solution_ref[...] = exact_dot(step, current, 1, 0)
    remainder = mine_ref[...] - exact_dot(step, image_ref[...], 1, 0)
    remainder_ref[...] = remainder
    direction_ref[...] = remainder + exact_dot(turn_ref[...], current, 1, 0)


def finish(mine, current, image, step, turn):
    out = jax.ShapeDtypeStruct(mine.shape, f32)
    return pl.pallas_call(
        finish_kernel,
        in_specs=[VMEM] * 5,
        out_specs=[VMEM] * 3,
        out_shape=(out, out, out),
        compiler_params=params(),
        name="finish",
    )(mine, current, image, step, turn)


def swap(value, axis, bits):
    size = lax.axis_size(axis)
    return lax.ppermute(value, axis, [(at, at ^ bits) for at in range(size)])


def in_order(parts, place):
    bit = 1
    while bit < len(parts):
        flip = (place & bit) != 0
        parts = [jnp.where(flip, parts[at ^ bit], parts[at]) for at in range(len(parts))]
        bit *= 2
    return parts


def all_sum(value, ranks, groups, near, core, place):
    rows = value.shape[0]
    half = rows // 2
    keep = lax.dynamic_slice_in_dim(value, core * half, half, 0)
    give = lax.dynamic_slice_in_dim(value, (1 - core) * half, half, 0)
    value = keep + swap(give, "split", 1)
    cuts = 2 * ranks
    share = half // cuts
    got = []
    for bits in range(1, cuts):
        give = lax.dynamic_slice_in_dim(value, (place ^ bits) * share, share, 0)
        got.append(pair_swap(give, bits, ranks))
    value = sum(got, lax.dynamic_slice_in_dim(value, place * share, share, 0))
    value = sum([swap(value, "tri", 2 * k) for k in range(1, groups)], value)
    parts = [value] + [pair_swap(value, bits, ranks) for bits in range(1, cuts)]
    value = jnp.concatenate(in_order(parts, place), axis=0)
    return jnp.concatenate(in_order([value, swap(value, "split", 1)], core), axis=0)


def pair_swap(value, bits, ranks):
    rank_bits, tri_bit = bits % ranks, bits // ranks
    if tri_bit == 0:
        return swap(value, "rhs", rank_bits)
    if rank_bits == 0:
        return swap(value, "tri", 1)
    count = lax.axis_size("tri")
    perm = [
        (tri * ranks + rank, (tri ^ 1) * ranks + (rank ^ rank_bits)) for tri in range(count) for rank in range(ranks)
    ]
    return lax.ppermute(value, ("tri", "rhs"), perm)


def body(residual, attach, vertices, corners, layers):
    columns, count = residual.shape
    tris, ranks, cores = lax.axis_size("tri"), lax.axis_size("rhs"), lax.axis_size("split")
    tri, rank, core = lax.axis_index("tri"), lax.axis_index("rhs"), lax.axis_index("split")
    near = min(4, tris)
    groups = tris // near
    scale = 1.0 / math.sqrt(corners.shape[1])

    my_ids = (tri * cores + core) * count + jnp.arange(count, dtype=jnp.int32)
    current = residual + inject * (attach[:, None] == my_ids[None, :]).astype(f32)
    packed = current.astype(bf16)
    packed_near = [swap(packed, "tri", bits) for bits in range(1, near)]
    currents = [current] + [swap(current, "rhs", bits) for bits in range(1, ranks)]

    sources = [(tri ^ bits) * cores + core for bits in range(near)]
    targets = [(tri ^ (near * far)) * cores + (core ^ other) for far in range(groups) for other in range(cores)]
    blocks = jnp.stack([*sources, *targets]).astype(jnp.int32)
    table = vertices.reshape(3, vertices.shape[1] // LANES, LANES)
    a_all, b_all, diag = geometry(blocks, table, corners, layers, count, scale)
    a_side = [a_all[bits] for bits in range(near)]
    b_side = b_all[near:]

    first = image_part([packed], a_side[:1], b_side, diag=diag[0])
    image_far = []
    if groups > 1:
        far = image_part(packed_near, a_side[1:], b_side[cores:], start=first[cores:])
        far = far.reshape(groups - 1, cores, columns, count)
        for at in range(1, groups):
            part = far[at - 1, 0] + swap(far[at - 1, 1].astype(bf16), "split", 1).astype(f32)
            image_far.append(swap(part.astype(bf16), "tri", near * at))
    own = image_part(packed_near, a_side[1:], b_side[:cores], start=first[:cores])
    image = own[0] + swap(own[1], "split", 1)
    for part in image_far:
        image = image + part.astype(f32)

    images = [image] + [swap(image, "rhs", bits) for bits in range(1, ranks)]
    places = jnp.stack([rank ^ bits for bits in range(ranks)]).astype(jnp.int32)
    every_current, every_image, sums = gram_sums(places, currents, images)
    sums = all_sum(sums, ranks, tris // 2, near, core, (tri & 1) * ranks + rank)
    step, turn = solve(places, sums, columns)
    return finish(current, every_current, every_image, step, turn)


def solution(mesh):
    return jax.shard_map(
        body,
        mesh=mesh,
        in_specs=(P("rhs", ("tri", "split")), P("rhs"), P(), P(), P()),
        out_specs=(
            P("rhs", ("tri", "split")),
            P("rhs", ("tri", "split")),
            P("rhs", ("tri", "split")),
        ),
        check_vma=False,
    )
```

```python
import functools
import math

import jax
import jax.numpy as jnp
from jax import lax
from jax.experimental import pallas as pl
from jax.experimental.pallas import tpu as pltpu
from jax.sharding import PartitionSpec as P

smooth_sq = 0.01
self_term = 1.0
inject = 3.0
f32 = jnp.float32
bf16 = jnp.bfloat16
LANES = 128
FEATURES = 32
PAIRS = ((0, 0), (0, 1), (1, 0), (1, 1), (0, 2), (2, 0))
VMEM = pl.BlockSpec(memory_space=pltpu.VMEM)
SMEM = pl.BlockSpec(memory_space=pltpu.SMEM)


def dot(a, b, ca, cb, precision=None):
    return lax.dot_general(
        a, b, (((ca,), (cb,)), ((), ())), precision=precision, preferred_element_type=f32
    )


def exact_dot(a, b, ca, cb):
    return dot(a, b, ca, cb, lax.Precision.HIGHEST)


def close_dot(a, b, ca, cb):
    a_high, b_high = a.astype(bf16), b.astype(bf16)
    a_low = (a - a_high.astype(f32)).astype(bf16)
    b_low = (b - b_high.astype(f32)).astype(bf16)
    return (dot(a_low, b_high, ca, cb) + dot(a_high, b_low, ca, cb)) + dot(a_high, b_high, ca, cb)


def params(mebibytes=16):
    return pltpu.CompilerParams(vmem_limit_bytes=mebibytes * 1024 * 1024)


def pieces_of(value):
    high = value.astype(bf16).astype(f32)
    rest = value - high
    middle = rest.astype(bf16).astype(f32)
    return (high, middle, rest - middle)


def geometry_kernel(
    scale, blocks_ref, vertices_ref, corners_ref, layers_ref, a_ref, b_ref, diag_ref, plain, table, a_rows, b_rows
):
    count = corners_ref.shape[1]
    tops = plain.shape[0]

    @pl.when(pl.program_id(0) == 0)
    def _():
        for axis in range(3):
            for top in range(tops):
                plain[top : top + 1, axis * LANES : (axis + 1) * LANES] = vertices_ref[
                    axis : axis + 1, top * LANES : (top + 1) * LANES
                ]
        for at, part in enumerate(pieces_of(plain[...])):
            table[at * tops : (at + 1) * tops, :] = part.astype(bf16)

    top_iota = lax.broadcasted_iota(jnp.int32, (tops, count), 0)
    low_iota = lax.broadcasted_iota(jnp.int32, (LANES, count), 0)
    points = []
    for corner in range(3):
        index = corners_ref[corner : corner + 1, :]
        top = jnp.where(top_iota == (index >> 7), 1.0, 0.0).astype(bf16)
        low = low_iota == (index & (LANES - 1))
        found = dot(table[...], jnp.concatenate([top, top, top], axis=0), 0, 0)
        points.append(
            [
                jnp.sum(jnp.where(low, found[axis * LANES : (axis + 1) * LANES], 0.0), axis=0, keepdims=True)
                for axis in range(3)
            ]
        )
    p0, p1, p2 = points
    centre = [(p0[k] + p1[k] + p2[k]) / 3.0 for k in range(3)]
    e1 = [p1[k] - p0[k] for k in range(3)]
    e2 = [p2[k] - p0[k] for k in range(3)]
    cross_x = e1[1] * e2[2] - e1[2] * e2[1]
    cross_y = e1[2] * e2[0] - e1[0] * e2[2]
    cross_z = e1[0] * e2[1] - e1[1] * e2[0]
    area_sq = cross_x * cross_x + cross_y * cross_y + cross_z * cross_z
    layers = layers_ref[...]
    factor = jnp.where(layers == 0, 1.0, jnp.where(layers == 1, 0.3, 0.8)).astype(f32)
    weight = factor * (0.5 + area_sq / (1.0 + area_sq))
    unit = 1.0 / (scale * (weight * weight))
    norm = centre[0] * centre[0] + centre[1] * centre[1] + centre[2] * centre[2]
    a_side = [unit * norm, unit] + [unit * c for c in centre]
    b_side = [unit, unit * (norm + smooth_sq)] + [-2.0 * unit * c for c in centre]
    a_parts = [pieces_of(value) for value in a_side]
    b_parts = [pieces_of(value) for value in b_side]
    row = 0
    for a_piece, b_piece in PAIRS:
        for term in range(5):
            a_rows[row : row + 1, :] = a_parts[term][a_piece]
            b_rows[row : row + 1, :] = b_parts[term][b_piece]
            row += 1
    blank = jnp.zeros((FEATURES - row, count), f32)
    a_rows[row:, :] = blank
    b_rows[row:, :] = blank
    a_ref[...] = a_rows[...].astype(bf16)
    b_ref[...] = b_rows[...].astype(bf16)
    diag_ref[...] = weight * weight * (lax.rsqrt(jnp.full_like(weight, smooth_sq)) * scale + self_term)


def geometry(blocks, vertices, corners, layers, count, scale):
    n = blocks.shape[0]
    points = vertices.shape[1]
    tops = points // LANES
    feature = jax.ShapeDtypeStruct((n, FEATURES, count), bf16)
    return pl.pallas_call(
        functools.partial(geometry_kernel, scale),
        grid_spec=pltpu.PrefetchScalarGridSpec(
            num_scalar_prefetch=1,
            grid=(n,),
            in_specs=[
                pl.BlockSpec((3, points), lambda g, blk: (0, 0)),
                pl.BlockSpec((3, count), lambda g, blk: (0, blk[g])),
                pl.BlockSpec((1, count), lambda g, blk: (0, blk[g])),
            ],
            out_specs=[
                pl.BlockSpec((None, FEATURES, count), lambda g, blk: (g, 0, 0)),
                pl.BlockSpec((None, FEATURES, count), lambda g, blk: (g, 0, 0)),
                pl.BlockSpec((None, 1, count), lambda g, blk: (g, 0, 0)),
            ],
            scratch_shapes=[
                pltpu.VMEM((tops, 3 * LANES), f32),
                pltpu.VMEM((3 * tops, 3 * LANES), bf16),
                pltpu.VMEM((FEATURES, count), f32),
                pltpu.VMEM((FEATURES, count), f32),
            ],
        ),
        out_shape=(feature, feature, jax.ShapeDtypeStruct((n, 1, count), f32)),
        compiler_params=params(),
        name="geometry",
    )(blocks, vertices, corners, layers[None, :])


def image_kernel(sources, has_start, has_diag, *refs):
    refs = list(refs)
    densities = [refs.pop(0) for _ in range(sources)]
    a_refs = [refs.pop(0) for _ in range(sources)]
    b_ref = refs.pop(0)
    start_ref = refs.pop(0) if has_start else None
    out_ref = refs.pop(0)
    targets, columns, count = out_ref.shape
    chunk = min(512, count)

    def one(target, with_diag):
        b = b_ref[target]
        acc = start_ref[target] if has_start else jnp.zeros((columns, count), f32)
        for density, a_ref in zip(densities, a_refs):
            for begin in range(0, count, chunk):
                tile = lax.rsqrt(dot(a_ref[:, begin : begin + chunk], b, 0, 0))
                if with_diag:
                    rows = begin + lax.broadcasted_iota(jnp.int32, tile.shape, 0)
                    cols = lax.broadcasted_iota(jnp.int32, tile.shape, 1)
                    tile = jnp.where(rows == cols, 0.0, tile)
                acc = acc + dot(density[:, begin : begin + chunk], tile.astype(bf16), 1, 0)
        out_ref[target] = acc

    if has_diag:
        one(0, True)
    if targets > int(has_diag):

        @pl.loop(int(has_diag), targets)
        def _(target):
            one(target, False)


def image_part(densities, a_side, b_side, start=None, own_first=False):
    columns, count = densities[0].shape
    targets = b_side.shape[0]
    operands = [*densities, *a_side, b_side]
    if start is not None:
        operands.append(start)
    entries = len(densities) * count * targets * count
    return pl.pallas_call(
        functools.partial(image_kernel, len(densities), start is not None, own_first),
        in_specs=[VMEM] * len(operands),
        out_specs=VMEM,
        out_shape=jax.ShapeDtypeStruct((targets, columns, count), f32),
        compiler_params=params(24),
        cost_estimate=pl.CostEstimate(
            flops=2 * entries * (columns + FEATURES), bytes_accessed=8 * targets * columns * count, transcendentals=entries
        ),
        name="image_part",
    )(*operands)


def combine_kernel(ranks, place_ref, *refs):
    parts, smooth_ref = refs[: -2 * ranks + 1], refs[-2 * ranks + 1]
    gives, rests = refs[-2 * ranks + 2 : -ranks + 1], refs[-ranks + 1 :]
    count = smooth_ref.shape[1]
    width = count // ranks
    smooth = parts[0][...].astype(f32)
    for part in parts[1:]:
        smooth = smooth + part[...].astype(f32)
    smooth_ref[...] = smooth
    for at in range(1, ranks):
        place = place_ref[at]
        gives[at - 1][...] = smooth_ref[:, pl.ds(pl.multiple_of(place * width, width), width)].astype(bf16)
        for chunk in range(ranks - 1):
            begin = lax.rem(place + 1 + chunk, ranks) * width
            rests[at - 1][:, chunk * width : (chunk + 1) * width] = smooth_ref[
                :, pl.ds(pl.multiple_of(begin, width), width)
            ].astype(bf16)


def combine(places, parts):
    ranks = places.shape[0]
    columns, count = parts[0].shape
    width = count // ranks
    out_shape = [jax.ShapeDtypeStruct((columns, count), f32)]
    out_shape += [jax.ShapeDtypeStruct((columns, width), bf16)] * (ranks - 1)
    out_shape += [jax.ShapeDtypeStruct((columns, count - width), bf16)] * (ranks - 1)
    outs = pl.pallas_call(
        functools.partial(combine_kernel, ranks),
        in_specs=[SMEM] + [VMEM] * len(parts),
        out_specs=[VMEM] * len(out_shape),
        out_shape=out_shape,
        compiler_params=params(),
        name="combine",
    )(places, *parts)
    return outs[0], outs[1:ranks], outs[ranks:]


def gram_kernel(ranks, place_ref, core_ref, smooth_ref, diag_ref, *refs):
    currents, gots = refs[:ranks], refs[ranks : 2 * ranks - 1]
    keep_ref, give_ref, current_all, image_all, sums = refs[2 * ranks - 1 :]
    columns, count = smooth_ref.shape
    width = count // ranks
    mine = pl.ds(pl.multiple_of(place_ref[0] * width, width), width)
    diag = diag_ref[:, mine].astype(bf16).astype(f32)
    for rank in range(ranks):
        at = pl.ds(pl.multiple_of(place_ref[rank] * columns, columns), columns)
        current = currents[rank][:, mine]
        smooth = smooth_ref[:, mine] if rank == 0 else gots[rank - 1][...].astype(f32)
        current_all[at, :] = current
        image_all[at, :] = smooth + diag * current.astype(bf16).astype(f32)
    current = current_all[...]
    image = image_all[...]
    total = ranks * columns
    sums[:total] = close_dot(current, image, 1, 1)
    sums[total : 2 * total] = close_dot(current, current, 1, 1)
    sums[2 * total :] = close_dot(image, image, 1, 1)
    half = keep_ref.shape[0]
    keep_ref[...] = sums[pl.ds(pl.multiple_of(core_ref[0] * half, half), half), :]
    give_ref[...] = sums[pl.ds(pl.multiple_of((1 - core_ref[0]) * half, half), half), :]


def gram_sums(places, core, smooth, diag, currents, gots):
    ranks = len(currents)
    columns, count = smooth.shape
    total = ranks * columns
    half = jax.ShapeDtypeStruct((3 * total // 2, total), f32)
    return pl.pallas_call(
        functools.partial(gram_kernel, ranks),
        in_specs=[SMEM, SMEM] + [VMEM] * (2 * ranks + 1),
        out_specs=[VMEM] * 2,
        out_shape=(half, half),
        scratch_shapes=[
            pltpu.VMEM((total, count // ranks), f32),
            pltpu.VMEM((total, count // ranks), f32),
            pltpu.VMEM((3 * total, total), f32),
        ],
        compiler_params=params(),
        name="gram",
    )(places, core, smooth, diag, *currents, *gots)


def shares_kernel(place_ref, keep_ref, got_ref, *shares):
    size = shares[0].shape[0]
    for at, share in enumerate(shares):
        rows = pl.ds(pl.multiple_of(place_ref[at] * size, size), size)
        share[...] = keep_ref[rows, :] + got_ref[rows, :]


def cut(places, keep, got):
    rows, lanes = keep.shape
    cuts = places.shape[0]
    return pl.pallas_call(
        shares_kernel,
        in_specs=[SMEM, VMEM, VMEM],
        out_specs=[VMEM] * cuts,
        out_shape=[jax.ShapeDtypeStruct((rows // cuts, lanes), f32)] * cuts,
        compiler_params=params(),
        name="shares",
    )(places, keep, got)


def reciprocal(value):
    guess = pl.reciprocal(value, approx=True)
    return guess * (2.0 - value * guess)


def eliminate(panel, begin, width):
    size, total = panel.shape
    parts = [panel[:, at : at + LANES] for at in range(0, total, LANES)]
    row_at = lax.broadcasted_iota(jnp.int32, (size, LANES), 0)
    col_at = lax.broadcasted_iota(jnp.int32, (size, LANES), 1)
    for group in range(0, size, width):
        own = parts[(begin + group) // LANES]
        first = (begin + group) % LANES
        cols = [jnp.broadcast_to(own[:, first + at : first + at + 1], (size, LANES)) for at in range(width)]
        for at in range(width):
            pivot = group + at
            inverse = reciprocal(cols[at][pivot : pivot + 1, :])
            is_row = row_at == pivot
            col = jnp.where(is_row, -1.0, cols[at])
            for part in range(len(parts)):
                row, gone = parts[part][pivot : pivot + 1, :], is_row
                if part == (begin + pivot) // LANES:
                    is_col = col_at == (begin + pivot) % LANES
                    row, gone = jnp.where(is_col[:1], 1.0, row), is_row | is_col
                parts[part] = jnp.where(gone, 0.0, parts[part]) - col * (row * inverse)
            for later in range(at + 1, width):
                factor = cols[later][pivot : pivot + 1, :] * inverse
                cols[later] = jnp.where(is_row, 0.0, cols[later]) - col * factor
    return jnp.concatenate(parts, axis=1)


def sweep(ref, begin, size):
    total = ref.shape[0]
    panel = ref[begin : begin + size, :]
    row = eliminate(panel, begin, 8)
    col_at = lax.broadcasted_iota(jnp.int32, panel.shape, 1)
    left = [part.astype(bf16) for part in pieces_of(jnp.where(col_at < begin, -panel, panel))]
    right = [part.astype(bf16) for part in pieces_of(row)]
    update = dot(
        jnp.concatenate([left[at] for at, _ in PAIRS], axis=0),
        jnp.concatenate([right[at] for _, at in PAIRS], axis=0),
        0,
        0,
    )
    lanes = lax.broadcasted_iota(jnp.int32, (total, total), 1)
    ref[...] = jnp.where((lanes >= begin) & (lanes < begin + size), 0.0, ref[...]) - update
    ref[begin : begin + size, :] = row


def solve_kernel(columns, size, cuts, place_ref, share_ref, *refs):
    shares = refs[: 2 * cuts]
    step_ref, turn_ref, sums, gram_inv, square_inv, step_all = refs[2 * cuts :]
    rows, total = shares[0].shape
    for at, share in enumerate(shares):
        sums[pl.ds(pl.multiple_of(share_ref[at] * rows, rows), rows), :] = share[...]
    cross = sums[:total]
    gram_inv[...] = 0.5 * (cross + cross.T)
    square_inv[...] = sums[total : 2 * total]
    for begin in range(0, total, size):
        sweep(gram_inv, begin, size)
        sweep(square_inv, begin, size)
    mine = pl.ds(pl.multiple_of(place_ref[0] * columns, columns), columns)
    step_all[...] = close_dot(sums[total : 2 * total], gram_inv[...], 1, 0)
    step = step_all[mine, :]
    step_ref[...] = step
    square_rows = sums[pl.ds(pl.multiple_of(total + place_ref[0] * columns, columns), columns), :]
    cross_rows = sums[mine, :]
    left = close_dot(step, sums[2 * total :], 1, 0) - cross_rows
    following = square_rows - close_dot(step, sums[:total], 1, 1) + close_dot(left, step_all[...], 1, 1)
    turn_ref[...] = close_dot(following, square_inv[...], 1, 0)


def solve(places, share_places, shares, columns):
    total = shares[0].shape[1]
    square = pltpu.VMEM((total, total), f32)
    rows = jax.ShapeDtypeStruct((columns, total), f32)
    return pl.pallas_call(
        functools.partial(solve_kernel, columns, 32, len(shares) // 2),
        in_specs=[SMEM, SMEM] + [VMEM] * len(shares),
        out_specs=[VMEM] * 2,
        out_shape=(rows, rows),
        scratch_shapes=[pltpu.VMEM((3 * total, total), f32), square, square, square],
        compiler_params=params(),
        name="solve",
    )(places, share_places, *shares)


def finish_kernel(ranks, place_ref, smooth_ref, diag_ref, step_ref, turn_ref, *refs):
    currents, gots, rests = refs[:ranks], refs[ranks : 2 * ranks - 1], refs[2 * ranks - 1 : 3 * ranks - 2]
    solution_ref, remainder_ref, direction_ref, current_all, image_all = refs[3 * ranks - 2 :]
    columns, count = smooth_ref.shape
    width = count // ranks
    diag = diag_ref[...].astype(bf16).astype(f32)
    for rank in range(ranks):
        at = pl.ds(pl.multiple_of(place_ref[rank] * columns, columns), columns)
        current = currents[rank][...]
        current_all[at, :] = current
        fixed = diag * current.astype(bf16).astype(f32)
        if rank == 0:
            image_all[at, :] = smooth_ref[...] + fixed
            continue
        for chunk in range(ranks):
            begin = lax.rem(place_ref[0] + chunk, ranks) * width
            lanes = pl.ds(pl.multiple_of(begin, width), width)
            if chunk == 0:
                image_all[at, lanes] = gots[rank - 1][...].astype(f32)
            else:
                image_all[at, lanes] = rests[rank - 1][:, (chunk - 1) * width : chunk * width].astype(f32)
        image_all[at, :] = image_all[at, :] + fixed
    step = step_ref[...]
    solution_ref[...] = close_dot(step, current_all[...], 1, 0)
    remainder = currents[0][...] - close_dot(step, image_all[...], 1, 0)
    remainder_ref[...] = remainder
    direction_ref[...] = remainder + close_dot(turn_ref[...], current_all[...], 1, 0)


def finish(places, smooth, diag, step, turn, currents, gots, rests):
    ranks = len(currents)
    columns, count = smooth.shape
    out = jax.ShapeDtypeStruct((columns, count), f32)
    every = pltpu.VMEM((ranks * columns, count), f32)
    return pl.pallas_call(
        functools.partial(finish_kernel, ranks),
        in_specs=[SMEM] + [VMEM] * (3 * ranks + 2),
        out_specs=[VMEM] * 3,
        out_shape=(out, out, out),
        scratch_shapes=[every, every],
        compiler_params=params(),
        name="finish",
    )(places, smooth, diag, step, turn, *currents, *gots, *rests)


def swap(value, axis, bits):
    size = lax.axis_size(axis)
    return lax.ppermute(value, axis, [(at, at ^ bits) for at in range(size)])


def pair_swap(value, bits, ranks):
    rank_bits, tri_bit = bits % ranks, bits // ranks
    if tri_bit == 0:
        return swap(value, "rhs", rank_bits)
    if rank_bits == 0:
        return swap(value, "tri", 1)
    count = lax.axis_size("tri")
    perm = [
        (tri * ranks + rank, (tri ^ 1) * ranks + (rank ^ rank_bits)) for tri in range(count) for rank in range(ranks)
    ]
    return lax.ppermute(value, ("tri", "rhs"), perm)


def indices(*values):
    return jnp.stack(values).astype(jnp.int32)


def all_sum(keep, give, ranks, tris, place, core):
    cuts = 2 * ranks
    cut_places = indices(*[place ^ bits for bits in range(cuts)])
    value, *gives = cut(cut_places, keep, swap(give, "split", 1))
    value = sum([pair_swap(part, bits, ranks) for bits, part in enumerate(gives, 1)], value)
    value = sum([swap(value, "tri", 2 * far) for far in range(1, tris // 2)], value)
    shares = [value] + [pair_swap(value, bits, ranks) for bits in range(1, cuts)]
    others = [swap(share, "split", 1) for share in shares]
    return shares + others, jnp.concatenate([cut_places + core * cuts, cut_places + (1 - core) * cuts])


def body(residual, attach, vertices, corners, layers):
    columns, count = residual.shape
    tris, ranks, cores = lax.axis_size("tri"), lax.axis_size("rhs"), lax.axis_size("split")
    tri, rank, core = lax.axis_index("tri"), lax.axis_index("rhs"), lax.axis_index("split")
    near = min(4, tris)
    groups = tris // near
    scale = 1.0 / math.sqrt(corners.shape[1])

    my_ids = (tri * cores + core) * count + jnp.arange(count, dtype=jnp.int32)
    current = residual + inject * (attach[:, None] == my_ids[None, :]).astype(f32)
    packed = current.astype(bf16)
    packed_near = [swap(packed, "tri", bits) for bits in range(1, near)]
    currents = [current] + [swap(current, "rhs", bits) for bits in range(1, ranks)]

    own_blocks = [(tri ^ (near * far)) * cores + core for far in range(groups)]
    near_blocks = [(tri ^ bits) * cores + core for bits in range(1, near)]
    a_all, b_all, diag = geometry(indices(*own_blocks, *near_blocks), vertices, corners, layers, count, scale)
    a_near = [a_all[groups + bits] for bits in range(near - 1)]
    b_own, diag = b_all[:groups], diag[0]
    b_other = swap(b_own, "split", 1)

    first_own = image_part([packed], [a_all[0]], b_own, own_first=True)
    first_other = image_part([packed], [a_all[0]], b_other)
    parts_far = []
    if groups > 1:
        far_other = image_part(packed_near, a_near, b_other[1:], start=first_other[1:])
        far_other = swap(far_other.astype(bf16), "split", 1)
        far_own = image_part(packed_near, a_near, b_own[1:], start=first_own[1:])
        far = (far_own + far_other.astype(f32)).astype(bf16)
        parts_far = [swap(far[at - 1], "tri", near * at) for at in range(1, groups)]
    own_other = image_part(packed_near, a_near, b_other[:1], start=first_other[:1])
    own_other = swap(own_other[0], "split", 1)
    own = image_part(packed_near, a_near, b_own[:1], start=first_own[:1])

    places = indices(*[rank ^ bits for bits in range(ranks)])
    smooth, gives, rests = combine(places, [own[0], own_other, *parts_far])
    gots = [swap(give, "rhs", bits) for bits, give in enumerate(gives, 1)]
    keep, give = gram_sums(places, indices(core), smooth, diag, currents, gots)
    keep, give, *rests = lax.optimization_barrier((keep, give, *rests))
    rests = [swap(rest, "rhs", bits) for bits, rest in enumerate(rests, 1)]
    shares, share_places = all_sum(keep, give, ranks, tris, (tri & 1) * ranks + rank, core)
    step, turn = solve(places, share_places, shares, columns)
    return finish(places, smooth, diag, step, turn, currents, gots, rests)


def solution(mesh):
    return jax.shard_map(
        body,
        mesh=mesh,
        in_specs=(P("rhs", ("tri", "split")), P("rhs"), P(), P(), P()),
        out_specs=(
            P("rhs", ("tri", "split")),
            P("rhs", ("tri", "split")),
            P("rhs", ("tri", "split")),
        ),
        check_vma=False,
    )
```

```python
import functools
import math

import jax
import jax.numpy as jnp
from jax import lax
from jax.experimental import pallas as pl
from jax.experimental.pallas import tpu as pltpu
from jax.sharding import PartitionSpec as P

smooth_sq = 0.01
self_term = 1.0
inject = 3.0
f32 = jnp.float32
bf16 = jnp.bfloat16
LANES = 128
FEATURES = 32
PAIRS = ((0, 0), (0, 1), (1, 0), (1, 1), (0, 2), (2, 0))
VMEM = pl.BlockSpec(memory_space=pltpu.VMEM)
SMEM = pl.BlockSpec(memory_space=pltpu.SMEM)
SMALL = pl.CostEstimate(flops=1024, bytes_accessed=1024, transcendentals=0)


def dot(a, b, ca, cb, precision=None):
    return lax.dot_general(
        a, b, (((ca,), (cb,)), ((), ())), precision=precision, preferred_element_type=f32
    )


def exact_dot(a, b, ca, cb):
    return dot(a, b, ca, cb, lax.Precision.HIGHEST)


def close_dot(a, b, ca, cb):
    a_high, b_high = a.astype(bf16), b.astype(bf16)
    a_low = (a - a_high.astype(f32)).astype(bf16)
    b_low = (b - b_high.astype(f32)).astype(bf16)
    return (dot(a_low, b_high, ca, cb) + dot(a_high, b_low, ca, cb)) + dot(a_high, b_high, ca, cb)


def params(mebibytes=16):
    return pltpu.CompilerParams(vmem_limit_bytes=mebibytes * 1024 * 1024)


def pieces_of(value):
    high = value.astype(bf16).astype(f32)
    rest = value - high
    middle = rest.astype(bf16).astype(f32)
    return (high, middle, rest - middle)


def geometry_kernel(
    scale, blocks_ref, vertices_ref, corners_ref, layers_ref, a_ref, b_ref, diag_ref, plain, table, a_rows, b_rows
):
    count = corners_ref.shape[1]
    tops = plain.shape[0]

    @pl.when(pl.program_id(0) == 0)
    def _():
        for axis in range(3):
            for top in range(tops):
                plain[top : top + 1, axis * LANES : (axis + 1) * LANES] = vertices_ref[
                    axis : axis + 1, top * LANES : (top + 1) * LANES
                ]
        for at, part in enumerate(pieces_of(plain[...])):
            table[at * tops : (at + 1) * tops, :] = part.astype(bf16)

    top_iota = lax.broadcasted_iota(jnp.int32, (tops, count), 0)
    low_iota = lax.broadcasted_iota(jnp.int32, (LANES, count), 0)
    points = []
    for corner in range(3):
        index = corners_ref[corner : corner + 1, :]
        top = jnp.where(top_iota == (index >> 7), 1.0, 0.0).astype(bf16)
        low = low_iota == (index & (LANES - 1))
        found = dot(table[...], jnp.concatenate([top, top, top], axis=0), 0, 0)
        points.append(
            [
                jnp.sum(jnp.where(low, found[axis * LANES : (axis + 1) * LANES], 0.0), axis=0, keepdims=True)
                for axis in range(3)
            ]
        )
    p0, p1, p2 = points
    centre = [(p0[k] + p1[k] + p2[k]) / 3.0 for k in range(3)]
    e1 = [p1[k] - p0[k] for k in range(3)]
    e2 = [p2[k] - p0[k] for k in range(3)]
    cross_x = e1[1] * e2[2] - e1[2] * e2[1]
    cross_y = e1[2] * e2[0] - e1[0] * e2[2]
    cross_z = e1[0] * e2[1] - e1[1] * e2[0]
    area_sq = cross_x * cross_x + cross_y * cross_y + cross_z * cross_z
    layers = layers_ref[...]
    factor = jnp.where(layers == 0, 1.0, jnp.where(layers == 1, 0.3, 0.8)).astype(f32)
    weight = factor * (0.5 + area_sq / (1.0 + area_sq))
    unit = 1.0 / (scale * (weight * weight))
    norm = centre[0] * centre[0] + centre[1] * centre[1] + centre[2] * centre[2]
    a_side = [unit * norm, unit] + [unit * c for c in centre]
    b_side = [unit, unit * (norm + smooth_sq)] + [-2.0 * unit * c for c in centre]
    a_parts = [pieces_of(value) for value in a_side]
    b_parts = [pieces_of(value) for value in b_side]
    row = 0
    for a_piece, b_piece in PAIRS:
        for term in range(5):
            a_rows[row : row + 1, :] = a_parts[term][a_piece]
            b_rows[row : row + 1, :] = b_parts[term][b_piece]
            row += 1
    blank = jnp.zeros((FEATURES - row, count), f32)
    a_rows[row:, :] = blank
    b_rows[row:, :] = blank
    a_ref[...] = a_rows[...].astype(bf16)
    b_ref[...] = b_rows[...].astype(bf16)
    diag_ref[...] = weight * weight * (lax.rsqrt(jnp.full_like(weight, smooth_sq)) * scale + self_term)


def geometry(blocks, vertices, corners, layers, count, scale):
    n = blocks.shape[0]
    points = vertices.shape[1]
    tops = points // LANES
    return pl.pallas_call(
        functools.partial(geometry_kernel, scale),
        grid_spec=pltpu.PrefetchScalarGridSpec(
            num_scalar_prefetch=1,
            grid=(n,),
            in_specs=[
                pl.BlockSpec((3, points), lambda g, blk: (0, 0)),
                pl.BlockSpec((3, count), lambda g, blk: (0, blk[g])),
                pl.BlockSpec((1, count), lambda g, blk: (0, blk[g])),
            ],
            out_specs=[
                pl.BlockSpec((None, FEATURES, count), lambda g, blk: (g, 0, 0)),
                pl.BlockSpec((None, FEATURES, count), lambda g, blk: (g, 0, 0)),
                pl.BlockSpec((None, 1, count), lambda g, blk: (g, 0, 0)),
            ],
            scratch_shapes=[
                pltpu.VMEM((tops, 3 * LANES), f32),
                pltpu.VMEM((3 * tops, 3 * LANES), bf16),
                pltpu.VMEM((FEATURES, count), f32),
                pltpu.VMEM((FEATURES, count), f32),
            ],
        ),
        out_shape=(
            jax.ShapeDtypeStruct((n, FEATURES, count), bf16),
            jax.ShapeDtypeStruct((n, FEATURES, count), bf16),
            jax.ShapeDtypeStruct((n, 1, count), f32),
        ),
        compiler_params=params(),
        name="geometry",
    )(blocks, vertices, corners, layers[None, :])


def image_kernel(sources, slots, targets, has_start, extras, first_ref, *refs):
    refs = list(refs)
    densities = [refs.pop(0) for _ in sources]
    sides = [refs.pop(0) for _ in range(1 + max(which for which, _ in [*slots, *[t[:2] for t in targets]]))]
    starts = [refs.pop(0) for _ in targets] if has_start else [None] * len(targets)
    more = [refs.pop(0) for _ in range(extras)]
    count = densities[0].shape[1]
    half = count // 2
    chunk = min(512, count)
    for at, (which, slot, part) in enumerate(targets):
        columns, width = refs[at].shape
        if part is None:
            lanes = slice(None)
        else:
            place = first_ref[0] if part == 0 else 1 - first_ref[0]
            lanes = pl.ds(pl.multiple_of(place * half, half), half)
        b = sides[which][slot, :, lanes]
        acc = starts[at][:, lanes] if has_start else jnp.zeros((columns, width), f32)
        for source, (density, (side, a_slot)) in enumerate(zip(densities, slots)):
            for begin in range(0, count, chunk):
                tile = lax.rsqrt(dot(sides[side][a_slot, :, begin : begin + chunk], b, 0, 0))
                acc = acc + dot(density[:, begin : begin + chunk], tile.astype(bf16), 1, 0)
        if at < extras:
            acc = acc + more[at][...].astype(f32)
        refs[at][...] = acc.astype(refs[at].dtype)


def image_part(first, densities, slots, sides, targets, starts=None, extras=(), kind=f32):
    columns, count = densities[0].shape
    sides = sides[: 1 + max(which for which, _ in [*slots, *[t[:2] for t in targets]])]
    operands = [first, *densities, *sides, *(starts or []), *extras]
    widths = [count if part is None else count // 2 for _, _, part in targets]
    return pl.pallas_call(
        functools.partial(image_kernel, range(len(densities)), slots, targets, bool(starts), len(extras)),
        in_specs=[SMEM] + [VMEM] * (len(operands) - 1),
        out_specs=[VMEM] * len(targets),
        out_shape=[jax.ShapeDtypeStruct((columns, width), kind) for width in widths],
        compiler_params=params(20),
        cost_estimate=SMALL,
        name="image_part",
    )(*operands)


def half_of(mine, other):
    return (mine > other).astype(jnp.int32)


def stack_kernel(near, *refs):
    a_ref, out_ref = refs[near:]
    columns = refs[0].shape[0]
    for source in range(near):
        out_ref[source * columns : (source + 1) * columns, :] = refs[source][...]
        side = near * columns + source * FEATURES
        out_ref[side : side + FEATURES, :] = a_ref[near - 1 - source]


def stack_rows(sources, a_side, near):
    columns, count = sources[0].shape
    return pl.pallas_call(
        functools.partial(stack_kernel, near),
        in_specs=[VMEM] * (near + 1),
        out_specs=VMEM,
        out_shape=jax.ShapeDtypeStruct((near * (columns + FEATURES), count), bf16),
        compiler_params=params(),
        cost_estimate=SMALL,
        name="stack_rows",
    )(*sources, a_side)


def own_kernel(near, mine_ref, theirs_ref, b_ref, out_ref):
    columns, count = out_ref.shape
    chunk = min(512, count)
    b = b_ref[0]
    acc = jnp.zeros((columns, count), f32)
    for ref in (mine_ref, theirs_ref):
        for source in range(near):
            side = near * columns + source * FEATURES
            for begin in range(0, count, chunk):
                lanes = slice(begin, begin + chunk)
                tile = lax.rsqrt(dot(ref[side : side + FEATURES, lanes], b, 0, 0))
                if ref is mine_ref and source == 0:
                    rows = begin + lax.broadcasted_iota(jnp.int32, tile.shape, 0)
                    cols = lax.broadcasted_iota(jnp.int32, tile.shape, 1)
                    tile = jnp.where(rows == cols, 0.0, tile)
                acc = acc + dot(ref[source * columns : (source + 1) * columns, lanes], tile.astype(bf16), 1, 0)
    out_ref[...] = acc


def own_image(mine, theirs, b_side, near):
    rows, count = mine.shape
    columns = rows // near - FEATURES
    return pl.pallas_call(
        functools.partial(own_kernel, near),
        in_specs=[VMEM] * 3,
        out_specs=VMEM,
        out_shape=jax.ShapeDtypeStruct((columns, count), f32),
        compiler_params=params(20),
        cost_estimate=SMALL,
        name="own_image",
    )(mine, theirs, b_side)


def combine_kernel(part, first_ref, own_ref, *refs):
    fars, (smooth_ref, low_ref) = refs[:-2], refs[-2:]
    width = smooth_ref.shape[1]
    place = first_ref[0] if part == 0 else 1 - first_ref[0]
    lanes = pl.ds(pl.multiple_of(place * width, width), width)
    smooth = own_ref[:, lanes]
    for far in fars:
        smooth = smooth + far[...].astype(f32)
    smooth_ref[...] = smooth
    low_ref[...] = smooth.astype(bf16)


def combine(part, first, own, fars):
    columns, count = own.shape
    return pl.pallas_call(
        functools.partial(combine_kernel, part),
        in_specs=[SMEM] + [VMEM] * (1 + len(fars)),
        out_specs=[VMEM] * 2,
        out_shape=[jax.ShapeDtypeStruct((columns, count // 2), kind) for kind in (f32, bf16)],
        compiler_params=params(),
        cost_estimate=SMALL,
        name="combine",
    )(first, own, *fars)


def full_image(first_ref, diag_ref, current_ref, smooth_refs, image_ref):
    half = smooth_refs[0].shape[1]
    for place, smooth in zip((first_ref[0], 1 - first_ref[0]), smooth_refs):
        lanes = pl.ds(pl.multiple_of(place * half, half), half)
        fixed = diag_ref[:, lanes].astype(bf16).astype(f32) * current_ref[:, lanes].astype(bf16).astype(f32)
        image_ref[:, lanes] = smooth[...] + fixed


def gram_kernel(ranks, first_ref, diag_ref, first_half, second_half, *refs):
    currents, (block, image) = refs[:ranks], refs[ranks:]
    columns = currents[0].shape[0]
    full_image(first_ref, diag_ref, currents[0], (first_half, second_half), image)
    for rank in range(ranks):
        current = currents[rank][...]
        block[rank, :columns] = close_dot(image[...], current, 1, 1)
        block[rank, columns : 2 * columns] = close_dot(currents[0][...], current, 1, 1)
    block[0, 2 * columns :] = close_dot(image[...], image[...], 1, 1)


def gram_sums(first, diag, smooths, currents):
    ranks = len(currents)
    columns, count = currents[0].shape
    return pl.pallas_call(
        functools.partial(gram_kernel, ranks),
        in_specs=[SMEM] + [VMEM] * (ranks + 3),
        out_specs=[VMEM] * 2,
        out_shape=(
            jax.ShapeDtypeStruct((ranks, 3 * columns, columns), f32),
            jax.ShapeDtypeStruct((columns, count), f32),
        ),
        compiler_params=params(),
        cost_estimate=SMALL,
        name="gram",
    )(first, diag, *smooths, *currents)


def cross_kernel(ranks, place_ref, core_ref, block_ref, image_ref, diag_ref, *refs):
    currents, gots = refs[: ranks - 1], refs[ranks - 1 : 2 * ranks - 2]
    keep_ref, give_ref, sums, block = refs[2 * ranks - 2 :]
    columns, count = image_ref.shape
    half = count // 2
    block[...] = block_ref[...]
    for rank in range(1, ranks):
        which = half_of(place_ref[0], place_ref[rank])
        lanes = pl.ds(pl.multiple_of(which * half, half), half)
        current = currents[rank - 1][:, lanes].astype(bf16).astype(f32)
        other = gots[rank - 1][...].astype(f32) + diag_ref[:, lanes].astype(bf16).astype(f32) * current
        block[rank, 2 * columns :] = close_dot(image_ref[:, lanes], other, 1, 1)
    for place in range(ranks):
        rank = jnp.bitwise_xor(place_ref[0], place)
        sums[:, place * columns : (place + 1) * columns] = block[rank]
    rows = keep_ref.shape[0]
    keep_ref[...] = sums[pl.ds(pl.multiple_of(core_ref[0] * rows, rows), rows), :]
    give_ref[...] = sums[pl.ds(pl.multiple_of((1 - core_ref[0]) * rows, rows), rows), :]


def cross_sums(places, core, blocks, image, diag, currents, gots):
    ranks = len(currents)
    columns, count = image.shape
    total = ranks * columns
    half = jax.ShapeDtypeStruct((3 * columns // 2, total), f32)
    return pl.pallas_call(
        functools.partial(cross_kernel, ranks),
        in_specs=[SMEM, SMEM] + [VMEM] * (2 * ranks + 1),
        out_specs=[VMEM] * 2,
        out_shape=(half, half),
        scratch_shapes=[
            pltpu.VMEM((3 * columns, total), f32),
            pltpu.VMEM((ranks, 3 * columns, columns), f32),
        ],
        compiler_params=params(),
        cost_estimate=SMALL,
        name="cross",
    )(places, core, blocks, image, diag, *currents[1:], *gots)


def shares_kernel(place_ref, keep_ref, got_ref, *shares):
    size = shares[0].shape[0]
    for at, share in enumerate(shares):
        rows = pl.ds(pl.multiple_of(place_ref[at] * size, size), size)
        share[...] = keep_ref[rows, :] + got_ref[rows, :]


def cut(places, keep, got):
    rows, lanes = keep.shape
    cuts = places.shape[0]
    return pl.pallas_call(
        shares_kernel,
        in_specs=[SMEM, VMEM, VMEM],
        out_specs=[VMEM] * cuts,
        out_shape=[jax.ShapeDtypeStruct((rows // cuts, lanes), f32)] * cuts,
        compiler_params=params(),
        name="shares",
    )(places, keep, got)


def reciprocal(value):
    guess = pl.reciprocal(value, approx=True)
    return guess * (2.0 - value * guess)


def eliminate(panel, begin, width):
    size, total = panel.shape
    parts = [panel[:, at : at + LANES] for at in range(0, total, LANES)]
    row_at = lax.broadcasted_iota(jnp.int32, (size, LANES), 0)
    col_at = lax.broadcasted_iota(jnp.int32, (1, LANES), 1)
    for group in range(0, size, width):
        own = parts[(begin + group) // LANES]
        first = (begin + group) % LANES
        cols = [jnp.broadcast_to(own[:, first + at : first + at + 1], (size, LANES)) for at in range(width)]
        for at in range(width):
            pivot = group + at
            value = cols[at][pivot : pivot + 1, :]
            inverse = reciprocal(value)
            col = jnp.where(row_at == pivot, cols[at] - 1.0, cols[at])
            for part in range(len(parts)):
                row = parts[part][pivot : pivot + 1, :]
                if part == (begin + pivot) // LANES:
                    row = jnp.where(col_at == (begin + pivot) % LANES, value + 1.0, row)
                parts[part] = parts[part] - col * (row * inverse)
            for later in range(at + 1, width):
                cols[later] = cols[later] - col * (cols[later][pivot : pivot + 1, :] * inverse)
    return jnp.concatenate(parts, axis=1)


def sweep(ref, begin, size):
    total = ref.shape[0]
    panel = ref[begin : begin + size, :]
    row = eliminate(panel, begin, 8)
    col_at = lax.broadcasted_iota(jnp.int32, panel.shape, 1)
    left = [part.astype(bf16) for part in pieces_of(jnp.where(col_at < begin, -panel, panel))]
    right = [part.astype(bf16) for part in pieces_of(row)]
    update = dot(
        jnp.concatenate([left[at] for at, _ in PAIRS], axis=0),
        jnp.concatenate([right[at] for _, at in PAIRS], axis=0),
        0,
        0,
    )
    lanes = lax.broadcasted_iota(jnp.int32, (total, total), 1)
    ref[...] = jnp.where((lanes >= begin) & (lanes < begin + size), 0.0, ref[...]) - update
    ref[begin : begin + size, :] = row


def solve_kernel(columns, size, place_ref, share_ref, *refs):
    shares = refs[:-7]
    step_ref, turn_ref, sums, grams, gram_inv, square_inv, step_all = refs[-7:]
    rows, total = shares[0].shape
    for at, share in enumerate(shares):
        sums[pl.ds(pl.multiple_of(share_ref[at] * rows, rows), rows), :] = share[...]
    for rank in range(total // columns):
        for which in range(3):
            begin = (rank * 3 + which) * columns
            grams[which, rank * columns : (rank + 1) * columns, :] = sums[begin : begin + columns, :]
    cross = grams[0]
    gram = 0.5 * (cross + cross.T)
    gram_scale = 1.0 / jnp.max(gram, keepdims=True)
    square_scale = 1.0 / jnp.max(grams[1], keepdims=True)
    gram_inv[...] = gram * gram_scale
    square_inv[...] = grams[1] * square_scale
    for begin in range(0, total, size):
        sweep(gram_inv, begin, size)
        sweep(square_inv, begin, size)
    mine = pl.ds(pl.multiple_of(place_ref[0] * columns, columns), columns)
    step_all[...] = close_dot(grams[1], gram_inv[...] * gram_scale, 1, 0)
    step = step_all[mine, :]
    step_ref[...] = step
    row_at = lax.broadcasted_iota(jnp.int32, (total, total), 0) // columns
    col_at = lax.broadcasted_iota(jnp.int32, (total, total), 1) // columns
    pairs = grams[2]
    images = pairs + jnp.where(row_at == col_at, 0.0, pairs.T)
    left = close_dot(step, images, 1, 0)
    across = close_dot(step, grams[0], 1, 0)
    grams[0] = grams[0].T
    left = left - grams[0, mine, :]
    following = grams[1, mine, :] - across + close_dot(left, step_all[...], 1, 1)
    turn_ref[...] = close_dot(following, square_inv[...] * square_scale, 1, 0)


def solve(places, share_places, shares, columns):
    total = shares[0].shape[1]
    square = pltpu.VMEM((total, total), f32)
    rows = jax.ShapeDtypeStruct((columns, total), f32)
    return pl.pallas_call(
        functools.partial(solve_kernel, columns, 32),
        in_specs=[SMEM, SMEM] + [VMEM] * len(shares),
        out_specs=[VMEM] * 2,
        out_shape=(rows, rows),
        scratch_shapes=[
            pltpu.VMEM((3 * total, total), f32),
            pltpu.VMEM((3, total, total), f32),
            square,
            square,
            square,
        ],
        compiler_params=params(),
        name="solve",
    )(places, share_places, *shares)


def others_kernel(ranks, place_ref, diag_ref, *refs):
    currents, gots, rests, outs = (refs[at * (ranks - 1) : (at + 1) * (ranks - 1)] for at in range(4))
    half = diag_ref.shape[1] // 2
    for at in range(ranks - 1):
        which = half_of(place_ref[0], place_ref[at + 1])
        for place, smooth in ((which, gots[at]), (1 - which, rests[at])):
            lanes = pl.ds(pl.multiple_of(place * half, half), half)
            fixed = diag_ref[:, lanes].astype(bf16).astype(f32) * currents[at][:, lanes].astype(bf16).astype(f32)
            outs[at][:, lanes] = smooth[...].astype(f32) + fixed


def other_images(places, diag, currents, gots, rests):
    ranks = len(currents)
    return pl.pallas_call(
        functools.partial(others_kernel, ranks),
        in_specs=[SMEM] + [VMEM] * (3 * ranks - 2),
        out_specs=[VMEM] * (ranks - 1),
        out_shape=[jax.ShapeDtypeStruct(currents[0].shape, f32)] * (ranks - 1),
        compiler_params=params(),
        cost_estimate=SMALL,
        name="other_images",
    )(places, diag, *currents[1:], *gots, *rests)


def finish_kernel(ranks, place_ref, step_ref, turn_ref, *refs):
    currents, images = refs[:ranks], refs[ranks : 2 * ranks]
    solution_ref, remainder_ref, direction_ref, current_all, image_all = refs[2 * ranks :]
    columns = currents[0].shape[0]
    for rank in range(ranks):
        at = pl.ds(pl.multiple_of(place_ref[rank] * columns, columns), columns)
        current_all[at, :] = currents[rank][...]
        image_all[at, :] = images[rank][...]
    current, step = current_all[...], step_ref[...]
    solution_ref[...] = close_dot(step, current, 1, 0)
    remainder = currents[0][...] - close_dot(step, image_all[...], 1, 0)
    remainder_ref[...] = remainder
    direction_ref[...] = remainder + close_dot(turn_ref[...], current, 1, 0)


def finish(places, step, turn, currents, images):
    ranks = len(currents)
    columns, count = currents[0].shape
    total = ranks * columns
    width = max(count // 4, LANES)
    out = jax.ShapeDtypeStruct((columns, count), f32)
    rows = pl.BlockSpec((columns, width), lambda at: (0, at))
    whole = pl.BlockSpec((columns, total), lambda at: (0, 0))
    return pl.pallas_call(
        functools.partial(finish_kernel, ranks),
        grid=(count // width,),
        in_specs=[SMEM, whole, whole] + [rows] * (2 * ranks),
        out_specs=[rows] * 3,
        out_shape=(out, out, out),
        scratch_shapes=[pltpu.VMEM((total, width), f32)] * 2,
        compiler_params=params(),
        cost_estimate=SMALL,
        name="finish",
    )(places, step, turn, *currents, *images)


def swap(value, axis, bits):
    size = lax.axis_size(axis)
    return lax.ppermute(value, axis, [(at, at ^ bits) for at in range(size)])


def pair_swap(value, bits, ranks):
    rank_bits, tri_bit = bits % ranks, bits // ranks
    if tri_bit == 0:
        return swap(value, "rhs", rank_bits)
    if rank_bits == 0:
        return swap(value, "tri", 1)
    count = lax.axis_size("tri")
    perm = [
        (tri * ranks + rank, (tri ^ 1) * ranks + (rank ^ rank_bits)) for tri in range(count) for rank in range(ranks)
    ]
    return lax.ppermute(value, ("tri", "rhs"), perm)


def indices(*values):
    return jnp.stack(values).astype(jnp.int32)


def all_sum(keep, give, beside, ranks, tris, tri, rank, core):
    low = tri & 1
    value, give = cut(indices(low, 1 - low), keep, swap(give, "split", 1))
    value = value + swap(give, "tri", 1)
    parts = [swap(value, "tri", 2 * far) for far in range(1, tris // 2)]
    parts, beside = lax.optimization_barrier((parts, beside))
    value = sum(parts, value)
    shares = [value] + [pair_swap(value, bits, ranks) for bits in range(1, 2 * ranks)]
    shares += [swap(share, "split", 1) for share in shares]
    places = [
        (rank ^ (bits % ranks)) * 4 + (core ^ other) * 2 + (low ^ (bits // ranks))
        for other in range(2)
        for bits in range(2 * ranks)
    ]
    return shares, indices(*places), beside


def body(residual, attach, vertices, corners, layers):
    columns, count = residual.shape
    tris, ranks, cores = lax.axis_size("tri"), lax.axis_size("rhs"), lax.axis_size("split")
    tri, rank, core = lax.axis_index("tri"), lax.axis_index("rhs"), lax.axis_index("split")
    near = min(4, tris)
    groups = tris // near
    scale = 1.0 / math.sqrt(corners.shape[1])

    my_ids = (tri * cores + core) * count + jnp.arange(count, dtype=jnp.int32)
    current = residual + inject * (attach[:, None] == my_ids[None, :]).astype(f32)
    packed = current.astype(bf16)
    currents = [current] + [swap(current, "rhs", bits) for bits in range(1, ranks)]
    sources = [packed] + [swap(packed, "tri", bits) for bits in range(1, near)]

    own_blocks = [(tri ^ (near * far)) * cores + core for far in range(groups)]
    near_blocks = [(tri ^ bits) * cores + core for bits in range(1, near)]
    vertices, packed = lax.optimization_barrier((vertices, packed))
    blocks = indices(*reversed(near_blocks), *own_blocks)
    a_side, b_side, diag = geometry(blocks, vertices, corners, layers, count, scale)
    diag = diag[near - 1]
    b_side = b_side[near - 1 :]
    slots = list(reversed(range(near)))
    sides = [a_side, b_side, swap(b_side, "split", 1)]
    half_place = half_of(rank ^ 1, rank) if ranks > 1 else jnp.int32(0)
    first = indices(half_place)

    def part(which, targets, starts=None, **more):
        return image_part(
            first, sources[which], [(0, slot) for slot in slots[which]], sides, targets, starts, **more
        )

    fars = range(1, groups)
    arrived = [[], []]
    last = slice(near - 1, near)
    far_sum = []
    if groups > 1:
        own_at, other_at = ([(side, far, None) for far in fars] for side in (1, 2))
        far_own = part(slice(0, 1), own_at)
        sides, far_own = lax.optimization_barrier((sides, far_own))
        far_other = part(slice(0, 1), other_at)
        for at in range(1, near - 1):
            both = part(slice(at, at + 1), other_at + own_at, [*far_other, *far_own])
            far_other, far_own = both[: len(other_at)], both[len(other_at) :]
        ready = []
        sides, currents = lax.optimization_barrier((sides, currents))
        for half in range(2):
            ready.append(part(last, [(*at[:2], half) for at in other_at], far_other, kind=bf16))
            sides, _ = lax.optimization_barrier((sides, ready))
        sent = [[swap(value, "split", 1) for value in values] for values in ready]
        for half in range(2):
            far_sum.append(
                part(last, [(*at[:2], half) for at in own_at], far_own, extras=sent[half], kind=bf16)
            )
            arrived[half] = [swap(value, "tri", near * far) for far, value in zip(fars, far_sum[half])]
            sides, _ = lax.optimization_barrier((sides, far_sum))
        sources, _ = lax.optimization_barrier((sources, sent))
    mine = stack_rows(sources, a_side, near)
    theirs = swap(mine, "split", 1)
    theirs, _ = lax.optimization_barrier((theirs, far_sum))
    own = own_image(mine, theirs, b_side, near)

    places = indices(*[rank ^ bits for bits in range(ranks)])
    smooth_first, low_first = combine(0, first, own, arrived[0])
    smooth_second, low_second = combine(1, first, own, arrived[1])
    gots, rests = [], []
    for bits in range(1, ranks):
        if bits == 1:
            give, rest = low_first, low_second
        else:
            is_first = half_of(rank ^ bits, rank) == half_place
            give = jnp.where(is_first, low_first, low_second)
            rest = jnp.where(is_first, low_second, low_first)
        gots.append(swap(give, "rhs", bits))
        rests.append(rest)
    blocks, image = gram_sums(first, diag, [smooth_first, smooth_second], currents)
    keep, give = cross_sums(places, indices(core), blocks, image, diag, currents, gots)
    rests, _ = lax.optimization_barrier((rests, gots))
    rests = [swap(rest, "rhs", bits) for bits, rest in enumerate(rests, 1)]
    beside = other_images(places, diag, currents, gots, rests)
    shares, share_places, beside = all_sum(keep, give, beside, ranks, tris, tri, rank, core)
    step, turn = solve(places, share_places, shares, columns)
    return finish(places, step, turn, currents, [image, *beside])


def solution(mesh):
    return jax.shard_map(
        body,
        mesh=mesh,
        in_specs=(P("rhs", ("tri", "split")), P("rhs"), P(), P(), P()),
        out_specs=(
            P("rhs", ("tri", "split")),
            P("rhs", ("tri", "split")),
            P("rhs", ("tri", "split")),
        ),
        check_vma=False,
    )
```

```python
import functools
import math

import jax
import jax.numpy as jnp
from jax import lax
from jax.experimental import pallas as pl
from jax.experimental.pallas import tpu as pltpu
from jax.sharding import PartitionSpec as P

smooth_sq = 0.01
self_term = 1.0
inject = 3.0
f32 = jnp.float32
bf16 = jnp.bfloat16
LANES = 128
LOW = 64
FEATURES = 32
PAIRS = ((0, 0), (0, 1), (1, 0), (1, 1), (0, 2), (2, 0))
VMEM = pl.BlockSpec(memory_space=pltpu.VMEM)
SMEM = pl.BlockSpec(memory_space=pltpu.SMEM)
SMALL = pl.CostEstimate(flops=1024, bytes_accessed=1024, transcendentals=0)


def dot(a, b, ca, cb, precision=None):
    return lax.dot_general(
        a, b, (((ca,), (cb,)), ((), ())), precision=precision, preferred_element_type=f32
    )


def split(value):
    high = value.astype(bf16)
    return high, (value - high.astype(f32)).astype(bf16)


def close_dot(a, b, ca, cb):
    a_high, a_low = split(a)
    b_high, b_low = split(b)
    return (dot(a_low, b_high, ca, cb) + dot(a_high, b_low, ca, cb)) + dot(a_high, b_high, ca, cb)


def params(mebibytes=16):
    return pltpu.CompilerParams(vmem_limit_bytes=mebibytes * 1024 * 1024)


def pieces_of(value):
    high = value.astype(bf16).astype(f32)
    rest = value - high
    middle = rest.astype(bf16).astype(f32)
    return (high, middle, rest - middle)


def geometry_kernel(
    scale, near, blocks_ref, vertices_ref, corners_ref, layers_ref, a_ref, b_ref, diag_ref, plain, table, a_rows, b_rows
):
    count = corners_ref.shape[1]
    tops = plain.shape[0]

    @pl.when(pl.program_id(0) == 0)
    def _():
        for axis in range(3):
            for top in range(tops):
                plain[top : top + 1, axis * LANES : (axis + 1) * LANES] = vertices_ref[
                    axis : axis + 1, top * LANES : (top + 1) * LANES
                ]
        for axis in range(3):
            for side in range(2):
                begin = axis * LANES + side * LOW
                value = plain[:, begin : begin + LOW]
                high = value.astype(bf16)
                low = (value - high.astype(f32)).astype(bf16)
                for at, part in enumerate((high, low)):
                    row = (2 * at + side) * tops
                    table[row : row + tops, axis * LOW : (axis + 1) * LOW] = part

    top_iota = lax.broadcasted_iota(jnp.int32, (2 * tops, count), 0)
    low_iota = lax.broadcasted_iota(jnp.int32, (LOW, count), 0)
    points = []
    for corner in range(3):
        index = corners_ref[corner : corner + 1, :]
        place = (index >> 7) + tops * ((index >> 6) & 1)
        top = jnp.where(top_iota == place, 1.0, 0.0).astype(bf16)
        low = low_iota == (index & (LOW - 1))
        found = dot(table[...], jnp.concatenate([top, top], axis=0), 0, 0)
        points.append(
            [
                jnp.sum(jnp.where(low, found[axis * LOW : (axis + 1) * LOW], 0.0), axis=0, keepdims=True)
                for axis in range(3)
            ]
        )
    p0, p1, p2 = points
    centre = [(p0[k] + p1[k] + p2[k]) / 3.0 for k in range(3)]
    e1 = [p1[k] - p0[k] for k in range(3)]
    e2 = [p2[k] - p0[k] for k in range(3)]
    cross_x = e1[1] * e2[2] - e1[2] * e2[1]
    cross_y = e1[2] * e2[0] - e1[0] * e2[2]
    cross_z = e1[0] * e2[1] - e1[1] * e2[0]
    area_sq = cross_x * cross_x + cross_y * cross_y + cross_z * cross_z
    layers = layers_ref[...]
    factor = jnp.where(layers == 0, 1.0, jnp.where(layers == 1, 0.3, 0.8)).astype(f32)
    weight = factor * (0.5 + area_sq / (1.0 + area_sq))
    unit = 1.0 / (scale * (weight * weight))
    norm = centre[0] * centre[0] + centre[1] * centre[1] + centre[2] * centre[2]
    a_side = [unit * norm, unit] + [unit * c for c in centre]
    b_side = [unit, unit * (norm + smooth_sq)] + [-2.0 * unit * c for c in centre]
    block = pl.program_id(0)

    def store(values, which, rows, out_ref):
        parts = [pieces_of(value) for value in values]
        row = 0
        for pair in PAIRS:
            for term in range(5):
                rows[row : row + 1, :] = parts[term][pair[which]]
                row += 1
        rows[row:, :] = jnp.zeros((FEATURES - row, count), f32)
        out_ref[...] = rows[...].astype(bf16)

    @pl.when(block < near)
    def _():
        store(a_side, 0, a_rows, a_ref)

    @pl.when(block >= near - 1)
    def _():
        store(b_side, 1, b_rows, b_ref)

    diag_ref[...] = weight * weight * (lax.rsqrt(jnp.full_like(weight, smooth_sq)) * scale + self_term)


def geometry(blocks, near, vertices, corners, layers, count, scale):
    n = blocks.shape[0]
    points = vertices.shape[1]
    tops = points // LANES
    return pl.pallas_call(
        functools.partial(geometry_kernel, scale, near),
        grid_spec=pltpu.PrefetchScalarGridSpec(
            num_scalar_prefetch=1,
            grid=(n,),
            in_specs=[
                pl.BlockSpec((3, points), lambda g, blk: (0, 0)),
                pl.BlockSpec((3, count), lambda g, blk: (0, blk[g])),
                pl.BlockSpec((1, count), lambda g, blk: (0, blk[g])),
            ],
            out_specs=[
                pl.BlockSpec((None, FEATURES, count), lambda g, blk: (jnp.minimum(g, near - 1), 0, 0)),
                pl.BlockSpec((None, FEATURES, count), lambda g, blk: (jnp.maximum(g - near + 1, 0), 0, 0)),
                pl.BlockSpec((None, 1, count), lambda g, blk: (g, 0, 0)),
            ],
            scratch_shapes=[
                pltpu.VMEM((tops, 3 * LANES), f32),
                pltpu.VMEM((4 * tops, 3 * LOW), bf16),
                pltpu.VMEM((FEATURES, count), f32),
                pltpu.VMEM((FEATURES, count), f32),
            ],
        ),
        out_shape=(
            jax.ShapeDtypeStruct((near, FEATURES, count), bf16),
            jax.ShapeDtypeStruct((n - near + 1, FEATURES, count), bf16),
            jax.ShapeDtypeStruct((n, 1, count), f32),
        ),
        compiler_params=params(),
        name="geometry",
    )(blocks, vertices, corners, layers[None, :])


def image_kernel(sources, slots, targets, has_start, extras, first_ref, *refs):
    refs = list(refs)
    densities = [refs.pop(0) for _ in sources]
    sides = [refs.pop(0) for _ in range(1 + max(which for which, _ in [*slots, *[t[:2] for t in targets]]))]
    starts = [refs.pop(0) for _ in targets] if has_start else [None] * len(targets)
    more = [refs.pop(0) for _ in range(extras)]
    count = densities[0].shape[1]
    half = count // 2
    chunk = min(512, count)
    for at, (which, slot, part) in enumerate(targets):
        columns, width = refs[at].shape
        if part is None:
            lanes = slice(None)
        else:
            place = first_ref[0] if part == 0 else 1 - first_ref[0]
            lanes = pl.ds(pl.multiple_of(place * half, half), half)
        b = sides[which][slot, :, lanes]
        acc = starts[at][:, lanes] if has_start else jnp.zeros((columns, width), f32)
        for source, (density, (side, a_slot)) in enumerate(zip(densities, slots)):
            for begin in range(0, count, chunk):
                tile = lax.rsqrt(dot(sides[side][a_slot, :, begin : begin + chunk], b, 0, 0))
                acc = acc + dot(density[:, begin : begin + chunk], tile.astype(bf16), 1, 0)
        if at < extras:
            acc = acc + more[at][...].astype(f32)
        refs[at][...] = acc.astype(refs[at].dtype)


def image_part(first, densities, slots, sides, targets, starts=None, extras=(), kind=f32):
    columns, count = densities[0].shape
    sides = sides[: 1 + max(which for which, _ in [*slots, *[t[:2] for t in targets]])]
    operands = [first, *densities, *sides, *(starts or []), *extras]
    widths = [count if part is None else count // 2 for _, _, part in targets]
    return pl.pallas_call(
        functools.partial(image_kernel, range(len(densities)), slots, targets, bool(starts), len(extras)),
        in_specs=[SMEM] + [VMEM] * (len(operands) - 1),
        out_specs=[VMEM] * len(targets),
        out_shape=[jax.ShapeDtypeStruct((columns, width), kind) for width in widths],
        compiler_params=params(20),
        cost_estimate=SMALL,
        name="image_part",
    )(*operands)


def half_of(mine, other):
    return (mine > other).astype(jnp.int32)


def stack_kernel(near, *refs):
    a_ref, out_ref = refs[near:]
    columns = refs[0].shape[0]
    for source in range(near):
        out_ref[source * columns : (source + 1) * columns, :] = refs[source][...]
        side = near * columns + source * FEATURES
        out_ref[side : side + FEATURES, :] = a_ref[near - 1 - source]


def stack_rows(sources, a_side, near):
    columns, count = sources[0].shape
    return pl.pallas_call(
        functools.partial(stack_kernel, near),
        in_specs=[VMEM] * (near + 1),
        out_specs=VMEM,
        out_shape=jax.ShapeDtypeStruct((near * (columns + FEATURES), count), bf16),
        compiler_params=params(),
        cost_estimate=SMALL,
        name="stack_rows",
    )(*sources, a_side)


def own_kernel(near, mine_ref, theirs_ref, b_ref, out_ref):
    columns, count = out_ref.shape
    chunk = min(512, count)
    b = b_ref[0]
    acc = jnp.zeros((columns, count), f32)
    for ref in (mine_ref, theirs_ref):
        for source in range(near):
            side = near * columns + source * FEATURES
            for begin in range(0, count, chunk):
                lanes = slice(begin, begin + chunk)
                tile = lax.rsqrt(dot(ref[side : side + FEATURES, lanes], b, 0, 0))
                if ref is mine_ref and source == 0:
                    rows = begin + lax.broadcasted_iota(jnp.int32, tile.shape, 0)
                    cols = lax.broadcasted_iota(jnp.int32, tile.shape, 1)
                    tile = jnp.where(rows == cols, 0.0, tile)
                acc = acc + dot(ref[source * columns : (source + 1) * columns, lanes], tile.astype(bf16), 1, 0)
    out_ref[...] = acc


def own_image(mine, theirs, b_side, near):
    rows, count = mine.shape
    columns = rows // near - FEATURES
    return pl.pallas_call(
        functools.partial(own_kernel, near),
        in_specs=[VMEM] * 3,
        out_specs=VMEM,
        out_shape=jax.ShapeDtypeStruct((columns, count), f32),
        compiler_params=params(20),
        cost_estimate=SMALL,
        name="own_image",
    )(mine, theirs, b_side)


def combine_kernel(part, first_ref, own_ref, *refs):
    fars, (smooth_ref, low_ref) = refs[:-2], refs[-2:]
    width = smooth_ref.shape[1]
    place = first_ref[0] if part == 0 else 1 - first_ref[0]
    lanes = pl.ds(pl.multiple_of(place * width, width), width)
    smooth = own_ref[:, lanes]
    for far in fars:
        smooth = smooth + far[...].astype(f32)
    smooth_ref[...] = smooth
    low_ref[...] = smooth.astype(bf16)


def combine(part, first, own, fars):
    columns, count = own.shape
    return pl.pallas_call(
        functools.partial(combine_kernel, part),
        in_specs=[SMEM] + [VMEM] * (1 + len(fars)),
        out_specs=[VMEM] * 2,
        out_shape=[jax.ShapeDtypeStruct((columns, count // 2), kind) for kind in (f32, bf16)],
        compiler_params=params(),
        cost_estimate=SMALL,
        name="combine",
    )(first, own, *fars)


def full_image(first_ref, diag_ref, current_ref, smooth_refs, image_ref):
    half = smooth_refs[0].shape[1]
    for place, smooth in zip((first_ref[0], 1 - first_ref[0]), smooth_refs):
        lanes = pl.ds(pl.multiple_of(place * half, half), half)
        fixed = diag_ref[:, lanes].astype(bf16).astype(f32) * current_ref[:, lanes].astype(bf16).astype(f32)
        image_ref[:, lanes] = smooth[...] + fixed


def gram_kernel(ranks, first_ref, diag_ref, first_half, second_half, *refs):
    currents, (block, image) = refs[:ranks], refs[ranks:]
    columns = currents[0].shape[0]
    full_image(first_ref, diag_ref, currents[0], (first_half, second_half), image)
    for rank in range(ranks):
        current = currents[rank][...]
        block[rank, :columns] = close_dot(image[...], current, 1, 1)
        block[rank, columns : 2 * columns] = close_dot(currents[0][...], current, 1, 1)
    block[0, 2 * columns :] = close_dot(image[...], image[...], 1, 1)


def gram_sums(first, diag, smooths, currents):
    ranks = len(currents)
    columns, count = currents[0].shape
    return pl.pallas_call(
        functools.partial(gram_kernel, ranks),
        in_specs=[SMEM] + [VMEM] * (ranks + 3),
        out_specs=[VMEM] * 2,
        out_shape=(
            jax.ShapeDtypeStruct((ranks, 3 * columns, columns), f32),
            jax.ShapeDtypeStruct((columns, count), f32),
        ),
        compiler_params=params(),
        cost_estimate=SMALL,
        name="gram",
    )(first, diag, *smooths, *currents)


def cross_kernel(ranks, place_ref, core_ref, block_ref, image_ref, diag_ref, *refs):
    currents, gots = refs[: ranks - 1], refs[ranks - 1 : 2 * ranks - 2]
    keep_ref, give_ref, sums, block = refs[2 * ranks - 2 :]
    columns, count = image_ref.shape
    half = count // 2
    block[...] = block_ref[...]
    for rank in range(1, ranks):
        which = half_of(place_ref[0], place_ref[rank])
        lanes = pl.ds(pl.multiple_of(which * half, half), half)
        current = currents[rank - 1][:, lanes].astype(bf16).astype(f32)
        other = gots[rank - 1][...].astype(f32) + diag_ref[:, lanes].astype(bf16).astype(f32) * current
        block[rank, 2 * columns :] = close_dot(image_ref[:, lanes], other, 1, 1)
    for place in range(ranks):
        rank = jnp.bitwise_xor(place_ref[0], place)
        sums[:, place * columns : (place + 1) * columns] = block[rank]
    rows = keep_ref.shape[0]
    keep_ref[...] = sums[pl.ds(pl.multiple_of(core_ref[0] * rows, rows), rows), :]
    give_ref[...] = sums[pl.ds(pl.multiple_of((1 - core_ref[0]) * rows, rows), rows), :]


def cross_sums(places, core, blocks, image, diag, currents, gots):
    ranks = len(currents)
    columns, count = image.shape
    total = ranks * columns
    half = jax.ShapeDtypeStruct((3 * columns // 2, total), f32)
    return pl.pallas_call(
        functools.partial(cross_kernel, ranks),
        in_specs=[SMEM, SMEM] + [VMEM] * (2 * ranks + 1),
        out_specs=[VMEM] * 2,
        out_shape=(half, half),
        scratch_shapes=[
            pltpu.VMEM((3 * columns, total), f32),
            pltpu.VMEM((ranks, 3 * columns, columns), f32),
        ],
        compiler_params=params(),
        cost_estimate=SMALL,
        name="cross",
    )(places, core, blocks, image, diag, *currents[1:], *gots)


def shares_kernel(place_ref, keep_ref, got_ref, *shares):
    size = shares[0].shape[0]
    for at, share in enumerate(shares):
        rows = pl.ds(pl.multiple_of(place_ref[at] * size, size), size)
        share[...] = keep_ref[rows, :] + got_ref[rows, :]


def cut(places, keep, got):
    rows, lanes = keep.shape
    cuts = places.shape[0]
    return pl.pallas_call(
        shares_kernel,
        in_specs=[SMEM, VMEM, VMEM],
        out_specs=[VMEM] * cuts,
        out_shape=[jax.ShapeDtypeStruct((rows // cuts, lanes), f32)] * cuts,
        compiler_params=params(),
        name="shares",
    )(places, keep, got)


def reciprocal(value):
    guess = pl.reciprocal(value, approx=True)
    return guess * (2.0 - value * guess)


def eliminate(panel, begin, window):
    size, total = panel.shape
    parts = [panel[:, at : at + LANES] for at in range(0, total, LANES)]
    row_at = lax.broadcasted_iota(jnp.int32, (size, LANES), 0)
    col_at = lax.broadcasted_iota(jnp.int32, (1, LANES), 1)

    def spread(pivot):
        place = (begin + pivot) % LANES
        return jnp.broadcast_to(parts[(begin + pivot) // LANES][:, place : place + 1], (size, LANES))

    cols = [spread(pivot) for pivot in range(window)]
    for pivot in range(size):
        col = cols.pop(0)
        inverse = reciprocal(col[pivot : pivot + 1, :])
        col = col - jnp.where(row_at == pivot, 1.0, 0.0)
        for part in range(len(parts)):
            row = parts[part][pivot : pivot + 1, :]
            if part == (begin + pivot) // LANES:
                row = row + jnp.where(col_at == (begin + pivot) % LANES, 1.0, 0.0)
            parts[part] = parts[part] - col * (row * inverse)
        cols = [later - col * (later[pivot : pivot + 1, :] * inverse) for later in cols]
        if pivot + window < size:
            cols.append(spread(pivot + window))
    return jnp.concatenate(parts, axis=1)


def sweep(ref, begin, size):
    total = ref.shape[0]
    panel = ref[begin : begin + size, :]
    row = eliminate(panel, begin, 6)
    col_at = lax.broadcasted_iota(jnp.int32, panel.shape, 1)
    left = [part.astype(bf16) for part in pieces_of(jnp.where(col_at < begin, -panel, panel))]
    right = [part.astype(bf16) for part in pieces_of(row)]
    update = dot(
        jnp.concatenate([left[at] for at, _ in PAIRS], axis=0),
        jnp.concatenate([right[at] for _, at in PAIRS], axis=0),
        0,
        0,
    )
    lanes = lax.broadcasted_iota(jnp.int32, (total, total), 1)
    ref[...] = jnp.where((lanes >= begin) & (lanes < begin + size), 0.0, ref[...]) - update
    ref[begin : begin + size, :] = row


def solve_kernel(columns, size, place_ref, share_ref, *refs):
    shares = refs[:-7]
    step_ref, turn_ref, sums, grams, gram_inv, square_inv, step_all = refs[-7:]
    rows, total = shares[0].shape
    for at, share in enumerate(shares):
        sums[pl.ds(pl.multiple_of(share_ref[at] * rows, rows), rows), :] = share[...]
    for rank in range(total // columns):
        for which in range(3):
            begin = (rank * 3 + which) * columns
            grams[which, rank * columns : (rank + 1) * columns, :] = sums[begin : begin + columns, :]
    cross = grams[0]
    gram = 0.5 * (cross + cross.T)
    gram_scale = 1.0 / jnp.max(gram, keepdims=True)
    square_scale = 1.0 / jnp.max(grams[1], keepdims=True)
    gram_inv[...] = gram * gram_scale
    square_inv[...] = grams[1] * square_scale
    for begin in range(0, total, size):
        sweep(gram_inv, begin, size)
        sweep(square_inv, begin, size)
    mine = pl.ds(pl.multiple_of(place_ref[0] * columns, columns), columns)
    step_all[...] = close_dot(grams[1], gram_inv[...] * gram_scale, 1, 0)
    step = step_all[mine, :]
    step_ref[...] = step
    row_at = lax.broadcasted_iota(jnp.int32, (total, total), 0) // columns
    col_at = lax.broadcasted_iota(jnp.int32, (total, total), 1) // columns
    pairs = grams[2]
    images = pairs + jnp.where(row_at == col_at, 0.0, pairs.T)
    left = close_dot(step, images, 1, 0)
    across = close_dot(step, grams[0], 1, 0)
    grams[0] = grams[0].T
    left = left - grams[0, mine, :]
    following = grams[1, mine, :] - across + close_dot(left, step_all[...], 1, 1)
    turn_ref[...] = close_dot(following, square_inv[...] * square_scale, 1, 0)


def solve(places, share_places, shares, columns):
    total = shares[0].shape[1]
    square = pltpu.VMEM((total, total), f32)
    rows = jax.ShapeDtypeStruct((columns, total), f32)
    return pl.pallas_call(
        functools.partial(solve_kernel, columns, 32),
        in_specs=[SMEM, SMEM] + [VMEM] * len(shares),
        out_specs=[VMEM] * 2,
        out_shape=(rows, rows),
        scratch_shapes=[
            pltpu.VMEM((3 * total, total), f32),
            pltpu.VMEM((3, total, total), f32),
            square,
            square,
            square,
        ],
        compiler_params=params(),
        name="solve",
    )(places, share_places, *shares)


def others_kernel(ranks, place_ref, diag_ref, *refs):
    currents, gots, rests, outs = (refs[at * (ranks - 1) : (at + 1) * (ranks - 1)] for at in range(4))
    half = diag_ref.shape[1] // 2
    for at in range(ranks - 1):
        which = half_of(place_ref[0], place_ref[at + 1])
        for place, smooth in ((which, gots[at]), (1 - which, rests[at])):
            lanes = pl.ds(pl.multiple_of(place * half, half), half)
            fixed = diag_ref[:, lanes].astype(bf16).astype(f32) * currents[at][:, lanes].astype(bf16).astype(f32)
            outs[at][:, lanes] = smooth[...].astype(f32) + fixed


def other_images(places, diag, currents, gots, rests):
    ranks = len(currents)
    return pl.pallas_call(
        functools.partial(others_kernel, ranks),
        in_specs=[SMEM] + [VMEM] * (3 * ranks - 2),
        out_specs=[VMEM] * (ranks - 1),
        out_shape=[jax.ShapeDtypeStruct(currents[0].shape, f32)] * (ranks - 1),
        compiler_params=params(),
        cost_estimate=SMALL,
        name="other_images",
    )(places, diag, *currents[1:], *gots, *rests)


def finish_kernel(ranks, chunks, place_ref, step_ref, turn_ref, *refs):
    currents, images, refs = refs[:ranks], refs[ranks : 2 * ranks], refs[2 * ranks :]
    outs, made, (current_all, image_all, sems) = refs[:3], refs[3:6], refs[6:]
    columns, count = currents[0].shape
    for rank in range(ranks):
        at = pl.ds(pl.multiple_of(place_ref[rank] * columns, columns), columns)
        current_all[at, :] = currents[rank][...]
        image_all[at, :] = images[rank][...]
    step_high, step_low = split(step_ref[...])
    turn_high, turn_low = split(turn_ref[...])
    both = jnp.concatenate([step_high, step_low, turn_high, turn_low], axis=0)
    highs = jnp.concatenate([step_high, turn_high], axis=0)
    steps = jnp.concatenate([step_high, step_low], axis=0)
    width = count // chunks
    copies = []
    for chunk in range(chunks):
        lanes = pl.ds(chunk * width, width)
        current_high, current_low = split(current_all[:, lanes])
        image_high, image_low = split(image_all[:, lanes])
        every = dot(both, current_high, 1, 0)
        rest = dot(highs, current_low, 1, 0)
        away = dot(steps, image_high, 1, 0)
        step_part, step_more, turn_part, turn_more = (every[at * columns : (at + 1) * columns] for at in range(4))
        away = away[:columns] + (away[columns:] + dot(step_high, image_low, 1, 0))
        remainder = currents[0][:, lanes] - away
        made[0][:, lanes] = step_part + (step_more + rest[:columns])
        made[1][:, lanes] = remainder
        made[2][:, lanes] = remainder + (turn_part + (turn_more + rest[columns:]))
        for at in range(3):
            copy = pltpu.make_async_copy(made[at].at[:, lanes], outs[at].at[:, lanes], sems.at[at, chunk])
            copy.start()
            copies.append(copy)
    for copy in copies:
        copy.wait()


def finish(places, step, turn, currents, images):
    ranks = len(currents)
    columns, count = currents[0].shape
    total = ranks * columns
    chunks = 2
    return pl.pallas_call(
        functools.partial(finish_kernel, ranks, chunks),
        in_specs=[SMEM] + [VMEM] * (2 * ranks + 2),
        out_specs=[pl.BlockSpec(memory_space=pl.ANY)] * 3,
        out_shape=[jax.ShapeDtypeStruct((columns, count), f32)] * 3,
        scratch_shapes=[pltpu.VMEM((columns, count), f32)] * 3
        + [pltpu.VMEM((total, count), f32)] * 2
        + [pltpu.SemaphoreType.DMA((3, chunks))],
        compiler_params=params(),
        cost_estimate=SMALL,
        name="finish",
    )(places, step, turn, *currents, *images)


def swap(value, axis, bits):
    size = lax.axis_size(axis)
    return lax.ppermute(value, axis, [(at, at ^ bits) for at in range(size)])


def pair_swap(value, bits, ranks):
    rank_bits, tri_bit = bits % ranks, bits // ranks
    if tri_bit == 0:
        return swap(value, "rhs", rank_bits)
    if rank_bits == 0:
        return swap(value, "tri", 1)
    count = lax.axis_size("tri")
    perm = [
        (tri * ranks + rank, (tri ^ 1) * ranks + (rank ^ rank_bits)) for tri in range(count) for rank in range(ranks)
    ]
    return lax.ppermute(value, ("tri", "rhs"), perm)


def indices(*values):
    return jnp.stack(values).astype(jnp.int32)


def all_sum(keep, give, beside, ranks, tris, tri, rank, core):
    low = tri & 1
    value, give = cut(indices(low, 1 - low), keep, swap(give, "split", 1))
    value = value + swap(give, "tri", 1)
    parts = [swap(value, "tri", 2 * far) for far in range(1, tris // 2)]
    parts, beside = lax.optimization_barrier((parts, beside))
    value = sum(parts, value)
    shares = [value] + [pair_swap(value, bits, ranks) for bits in range(1, 2 * ranks)]
    shares += [swap(share, "split", 1) for share in shares]
    places = [
        (rank ^ (bits % ranks)) * 4 + (core ^ other) * 2 + (low ^ (bits // ranks))
        for other in range(2)
        for bits in range(2 * ranks)
    ]
    return shares, indices(*places), beside


def body(residual, attach, vertices, corners, layers):
    columns, count = residual.shape
    tris, ranks, cores = lax.axis_size("tri"), lax.axis_size("rhs"), lax.axis_size("split")
    tri, rank, core = lax.axis_index("tri"), lax.axis_index("rhs"), lax.axis_index("split")
    near = min(4, tris)
    groups = tris // near
    scale = 1.0 / math.sqrt(corners.shape[1])

    my_ids = (tri * cores + core) * count + jnp.arange(count, dtype=jnp.int32)
    current = residual + inject * (attach[:, None] == my_ids[None, :]).astype(f32)
    packed = current.astype(bf16)
    currents = [current] + [swap(current, "rhs", bits) for bits in range(1, ranks)]
    sources = [packed] + [swap(packed, "tri", bits) for bits in range(1, near)]

    own_blocks = [(tri ^ (near * far)) * cores + core for far in range(groups)]
    near_blocks = [(tri ^ bits) * cores + core for bits in range(1, near)]
    vertices, packed = lax.optimization_barrier((vertices, packed))
    blocks = indices(*reversed(near_blocks), *own_blocks)
    a_side, b_side, diag = geometry(blocks, near, vertices, corners, layers, count, scale)
    diag = diag[near - 1]
    slots = list(reversed(range(near)))
    sides = [a_side, b_side, swap(b_side, "split", 1)]
    half_place = half_of(rank ^ 1, rank) if ranks > 1 else jnp.int32(0)
    first = indices(half_place)

    def part(which, targets, starts=None, **more):
        return image_part(
            first, sources[which], [(0, slot) for slot in slots[which]], sides, targets, starts, **more
        )

    fars = range(1, groups)
    arrived = [[], []]
    last = slice(near - 1, near)
    far_sum = []
    if groups > 1:
        own_at, other_at = ([(side, far, None) for far in fars] for side in (1, 2))
        far_own = part(slice(0, 1), own_at)
        sides, far_own = lax.optimization_barrier((sides, far_own))
        far_other = part(slice(0, 1), other_at)
        for at in range(1, near - 1):
            both = part(slice(at, at + 1), other_at + own_at, [*far_other, *far_own])
            far_other, far_own = both[: len(other_at)], both[len(other_at) :]
        ready = []
        sides, currents = lax.optimization_barrier((sides, currents))
        for half in range(2):
            ready.append(part(last, [(*at[:2], half) for at in other_at], far_other, kind=bf16))
            sides, _ = lax.optimization_barrier((sides, ready))
        sent = [[swap(value, "split", 1) for value in values] for values in ready]
        for half in range(2):
            far_sum.append(
                part(last, [(*at[:2], half) for at in own_at], far_own, extras=sent[half], kind=bf16)
            )
            arrived[half] = [swap(value, "tri", near * far) for far, value in zip(fars, far_sum[half])]
            sides, _ = lax.optimization_barrier((sides, far_sum))
        sources, _ = lax.optimization_barrier((sources, far_sum[0]))
    mine = stack_rows(sources, a_side, near)
    theirs = swap(mine, "split", 1)
    theirs, _ = lax.optimization_barrier((theirs, far_sum))
    own = own_image(mine, theirs, b_side, near)

    places = indices(*[rank ^ bits for bits in range(ranks)])
    smooth_first, low_first = combine(0, first, own, arrived[0])
    smooth_second, low_second = combine(1, first, own, arrived[1])
    gots, rests = [], []
    for bits in range(1, ranks):
        if bits == 1:
            give, rest = low_first, low_second
        else:
            is_first = half_of(rank ^ bits, rank) == half_place
            give = jnp.where(is_first, low_first, low_second)
            rest = jnp.where(is_first, low_second, low_first)
        gots.append(swap(give, "rhs", bits))
        rests.append(rest)
    blocks, image = gram_sums(first, diag, [smooth_first, smooth_second], currents)
    keep, give = cross_sums(places, indices(core), blocks, image, diag, currents, gots)
    rests, _ = lax.optimization_barrier((rests, gots))
    rests = [swap(rest, "rhs", bits) for bits, rest in enumerate(rests, 1)]
    beside = other_images(places, diag, currents, gots, rests)
    shares, share_places, beside = all_sum(keep, give, beside, ranks, tris, tri, rank, core)
    step, turn = solve(places, share_places, shares, columns)
    return finish(places, step, turn, currents, [image, *beside])


def solution(mesh):
    return jax.shard_map(
        body,
        mesh=mesh,
        in_specs=(P("rhs", ("tri", "split")), P("rhs"), P(), P(), P()),
        out_specs=(
            P("rhs", ("tri", "split")),
            P("rhs", ("tri", "split")),
            P("rhs", ("tri", "split")),
        ),
        check_vma=False,
    )
```

```python
import functools
import math

import jax
import jax.numpy as jnp
from jax import lax
from jax.experimental import pallas as pl
from jax.experimental.pallas import tpu as pltpu
from jax.sharding import PartitionSpec as P

smooth_sq = 0.01
self_term = 1.0
inject = 3.0
f32 = jnp.float32
bf16 = jnp.bfloat16
LANES = 128
LOW = 64
FEATURES = 32
TILE = 512 * 1024
PAIRS = ((0, 0), (0, 1), (1, 0), (1, 1), (0, 2), (2, 0))
VMEM = pl.BlockSpec(memory_space=pltpu.VMEM)
SMEM = pl.BlockSpec(memory_space=pltpu.SMEM)
SMALL = pl.CostEstimate(flops=1024, bytes_accessed=1024, transcendentals=0)


def dot(a, b, ca, cb, precision=None):
    return lax.dot_general(
        a, b, (((ca,), (cb,)), ((), ())), precision=precision, preferred_element_type=f32
    )


def split(value):
    high = value.astype(bf16)
    return high, (value - high.astype(f32)).astype(bf16)


def close_dot(a, b, ca, cb):
    a_high, a_low = split(a)
    b_high, b_low = split(b)
    return (dot(a_low, b_high, ca, cb) + dot(a_high, b_low, ca, cb)) + dot(a_high, b_high, ca, cb)


def params(mebibytes=12):
    return pltpu.CompilerParams(vmem_limit_bytes=mebibytes * 1024 * 1024)


def pieces_of(value):
    high = value.astype(bf16).astype(f32)
    rest = value - high
    middle = rest.astype(bf16).astype(f32)
    return (high, middle, rest - middle)


def geometry_kernel(
    scale, near, blocks_ref, vertices_ref, corners_ref, layers_ref, a_ref, b_ref, diag_ref, plain, table, a_rows, b_rows
):
    count = corners_ref.shape[1]
    tops = plain.shape[0]

    @pl.when(pl.program_id(0) == 0)
    def _():
        for axis in range(3):
            for top in range(tops):
                plain[top : top + 1, axis * LANES : (axis + 1) * LANES] = vertices_ref[
                    axis : axis + 1, top * LANES : (top + 1) * LANES
                ]
        for axis in range(3):
            for side in range(2):
                begin = axis * LANES + side * LOW
                value = plain[:, begin : begin + LOW]
                high = value.astype(bf16)
                low = (value - high.astype(f32)).astype(bf16)
                for at, part in enumerate((high, low)):
                    row = (2 * at + side) * tops
                    table[row : row + tops, axis * LOW : (axis + 1) * LOW] = part

    top_iota = lax.broadcasted_iota(jnp.int32, (2 * tops, count), 0)
    low_iota = lax.broadcasted_iota(jnp.int32, (LOW, count), 0)
    points = []
    for corner in range(3):
        index = corners_ref[corner : corner + 1, :]
        place = (index >> 7) + tops * ((index >> 6) & 1)
        top = jnp.where(top_iota == place, 1.0, 0.0).astype(bf16)
        low = low_iota == (index & (LOW - 1))
        found = dot(table[...], jnp.concatenate([top, top], axis=0), 0, 0)
        points.append(
            [
                jnp.sum(jnp.where(low, found[axis * LOW : (axis + 1) * LOW], 0.0), axis=0, keepdims=True)
                for axis in range(3)
            ]
        )
    p0, p1, p2 = points
    centre = [(p0[k] + p1[k] + p2[k]) / 3.0 for k in range(3)]
    e1 = [p1[k] - p0[k] for k in range(3)]
    e2 = [p2[k] - p0[k] for k in range(3)]
    cross_x = e1[1] * e2[2] - e1[2] * e2[1]
    cross_y = e1[2] * e2[0] - e1[0] * e2[2]
    cross_z = e1[0] * e2[1] - e1[1] * e2[0]
    area_sq = cross_x * cross_x + cross_y * cross_y + cross_z * cross_z
    layers = layers_ref[...]
    factor = jnp.where(layers == 0, 1.0, jnp.where(layers == 1, 0.3, 0.8)).astype(f32)
    weight = factor * (0.5 + area_sq / (1.0 + area_sq))
    unit = 1.0 / (scale * (weight * weight))
    norm = centre[0] * centre[0] + centre[1] * centre[1] + centre[2] * centre[2]
    a_side = [unit * norm, unit] + [unit * c for c in centre]
    b_side = [unit, unit * (norm + smooth_sq)] + [-2.0 * unit * c for c in centre]
    block = pl.program_id(0)

    def store(values, which, rows, out_ref):
        parts = [pieces_of(value) for value in values]
        row = 0
        for pair in PAIRS:
            for term in range(5):
                rows[row : row + 1, :] = parts[term][pair[which]]
                row += 1
        rows[row:, :] = jnp.zeros((FEATURES - row, count), f32)
        out_ref[...] = rows[...].astype(bf16)

    @pl.when(block < near)
    def _():
        store(a_side, 0, a_rows, a_ref)

    @pl.when(block >= near - 1)
    def _():
        store(b_side, 1, b_rows, b_ref)

    @pl.when(block == near - 1)
    def _():
        diag_ref[...] = weight * weight * (lax.rsqrt(jnp.full_like(weight, smooth_sq)) * scale + self_term)


def geometry(blocks, near, vertices, corners, layers, count, scale):
    n = blocks.shape[0]
    points = vertices.shape[1]
    tops = points // LANES
    return pl.pallas_call(
        functools.partial(geometry_kernel, scale, near),
        grid_spec=pltpu.PrefetchScalarGridSpec(
            num_scalar_prefetch=1,
            grid=(n,),
            in_specs=[
                pl.BlockSpec((3, points), lambda g, blk: (0, 0)),
                pl.BlockSpec((3, count), lambda g, blk: (0, blk[g])),
                pl.BlockSpec((1, count), lambda g, blk: (0, blk[g])),
            ],
            out_specs=[
                pl.BlockSpec((None, FEATURES, count), lambda g, blk: (jnp.minimum(g, near - 1), 0, 0)),
                pl.BlockSpec((None, FEATURES, count), lambda g, blk: (jnp.maximum(g - near + 1, 0), 0, 0)),
                pl.BlockSpec((1, count), lambda g, blk: (0, 0)),
            ],
            scratch_shapes=[
                pltpu.VMEM((tops, 3 * LANES), f32),
                pltpu.VMEM((4 * tops, 3 * LOW), bf16),
                pltpu.VMEM((FEATURES, count), f32),
                pltpu.VMEM((FEATURES, count), f32),
            ],
        ),
        out_shape=(
            jax.ShapeDtypeStruct((near, FEATURES, count), bf16),
            jax.ShapeDtypeStruct((n - near + 1, FEATURES, count), bf16),
            jax.ShapeDtypeStruct((1, count), f32),
        ),
        compiler_params=params(),
        name="geometry",
    )(blocks, vertices, corners, layers[None, :])


def image_kernel(sources, slots, targets, has_start, extras, first_ref, *refs):
    refs = list(refs)
    densities = [refs.pop(0) for _ in sources]
    sides = [refs.pop(0) for _ in range(1 + max(which for which, _ in [*slots, *[t[:2] for t in targets]]))]
    starts = [refs.pop(0) for _ in targets] if has_start else [None] * len(targets)
    more = [refs.pop(0) for _ in range(extras)]
    count = densities[0].shape[1]
    half = count // 2
    for at, (which, slot, part) in enumerate(targets):
        columns, width = refs[at].shape
        chunk = min(TILE // width, count)
        if part is None:
            lanes = slice(None)
        else:
            place = first_ref[0] if part == 0 else 1 - first_ref[0]
            lanes = pl.ds(pl.multiple_of(place * half, half), half)
        b = sides[which][slot, :, lanes]
        acc = starts[at][:, lanes] if has_start else jnp.zeros((columns, width), f32)
        for source, (density, (side, a_slot)) in enumerate(zip(densities, slots)):
            for begin in range(0, count, chunk):
                tile = lax.rsqrt(dot(sides[side][a_slot, :, begin : begin + chunk], b, 0, 0))
                acc = acc + dot(density[:, begin : begin + chunk], tile.astype(bf16), 1, 0)
        if at < extras:
            acc = acc + more[at][...].astype(f32)
        refs[at][...] = acc.astype(refs[at].dtype)


def image_part(first, densities, slots, sides, targets, starts=None, extras=(), kind=f32):
    columns, count = densities[0].shape
    sides = sides[: 1 + max(which for which, _ in [*slots, *[t[:2] for t in targets]])]
    operands = [first, *densities, *sides, *(starts or []), *extras]
    widths = [count if part is None else count // 2 for _, _, part in targets]
    return pl.pallas_call(
        functools.partial(image_kernel, range(len(densities)), slots, targets, bool(starts), len(extras)),
        in_specs=[SMEM] + [VMEM] * (len(operands) - 1),
        out_specs=[VMEM] * len(targets),
        out_shape=[jax.ShapeDtypeStruct((columns, width), kind) for width in widths],
        compiler_params=params(12),
        cost_estimate=SMALL,
        name="image_part",
    )(*operands)


def half_of(mine, other):
    return (mine > other).astype(jnp.int32)


def stack_kernel(near, *refs):
    a_ref, out_ref = refs[near:]
    columns = refs[0].shape[0]
    for source in range(near):
        out_ref[source * columns : (source + 1) * columns, :] = refs[source][...]
        side = near * columns + source * FEATURES
        out_ref[side : side + FEATURES, :] = a_ref[near - 1 - source]


def stack_rows(sources, a_side, near):
    columns, count = sources[0].shape
    return pl.pallas_call(
        functools.partial(stack_kernel, near),
        in_specs=[VMEM] * (near + 1),
        out_specs=VMEM,
        out_shape=jax.ShapeDtypeStruct((near * (columns + FEATURES), count), bf16),
        compiler_params=params(),
        cost_estimate=SMALL,
        name="stack_rows",
    )(*sources, a_side)


def own_kernel(near, part, diagonal, stacks, first_ref, b_ref, *refs):
    out_ref = refs[-1]
    columns, width = out_ref.shape
    count = b_ref.shape[2]
    chunk = min(TILE // width, count)
    place = first_ref[0] if part == 0 else 1 - first_ref[0]
    b = b_ref[0, :, pl.ds(pl.multiple_of(place * width, width), width)]
    acc = refs[stacks][...] if len(refs) > stacks + 1 else jnp.zeros((columns, width), f32)
    for at, ref in enumerate(refs[:stacks]):
        for source in range(near):
            side = near * columns + source * FEATURES
            for begin in range(0, count, chunk):
                lanes = slice(begin, begin + chunk)
                tile = lax.rsqrt(dot(ref[side : side + FEATURES, lanes], b, 0, 0))
                if diagonal and at == 0 and source == 0:
                    rows = begin + lax.broadcasted_iota(jnp.int32, tile.shape, 0)
                    cols = place * width + lax.broadcasted_iota(jnp.int32, tile.shape, 1)
                    tile = jnp.where(rows == cols, 0.0, tile)
                acc = acc + dot(ref[source * columns : (source + 1) * columns, lanes], tile.astype(bf16), 1, 0)
    out_ref[...] = acc


def own_image(part, first, stacks, b_side, near, diagonal, start=()):
    rows, count = stacks[0].shape
    columns = rows // near - FEATURES
    operands = [b_side, *stacks, *start]
    return pl.pallas_call(
        functools.partial(own_kernel, near, part, diagonal, len(stacks)),
        in_specs=[SMEM] + [VMEM] * len(operands),
        out_specs=VMEM,
        out_shape=jax.ShapeDtypeStruct((columns, count // 2), f32),
        compiler_params=params(12),
        cost_estimate=SMALL,
        name="own_image",
    )(first, *operands)


def add_parts(refs):
    total = refs[0][...].astype(f32)
    for ref in refs[1:]:
        total = total + ref[...].astype(f32)
    return total


def combine_kernel(*refs):
    smooth = add_parts(refs[:-2])
    refs[-2][...] = smooth
    refs[-1][...] = smooth.astype(bf16)


def combine(parts):
    return pl.pallas_call(
        combine_kernel,
        in_specs=[VMEM] * len(parts),
        out_specs=[VMEM] * 2,
        out_shape=[jax.ShapeDtypeStruct(parts[0].shape, kind) for kind in (f32, bf16)],
        compiler_params=params(),
        cost_estimate=SMALL,
        name="combine",
    )(*parts)


def full_image(first_ref, diag_ref, current_ref, smooths, image_ref):
    half = smooths[0].shape[1]
    for place, smooth in zip((first_ref[0], 1 - first_ref[0]), smooths):
        lanes = pl.ds(pl.multiple_of(place * half, half), half)
        fixed = diag_ref[:, lanes].astype(bf16).astype(f32) * current_ref[:, lanes].astype(bf16).astype(f32)
        image_ref[:, lanes] = smooth + fixed


def gram_kernel(ranks, first_ref, diag_ref, first_half, *refs):
    currents, parts, (block, image, low) = refs[:ranks], refs[ranks:-3], refs[-3:]
    columns = currents[0].shape[0]
    second_half = add_parts(parts)
    low[...] = second_half.astype(bf16)
    full_image(first_ref, diag_ref, currents[0], (first_half[...], second_half), image)
    for rank in range(ranks):
        current = currents[rank][...]
        block[rank, :columns] = close_dot(image[...], current, 1, 1)
        block[rank, columns : 2 * columns] = close_dot(currents[0][...], current, 1, 1)
    block[0, 2 * columns :] = close_dot(image[...], image[...], 1, 1)


def gram_sums(first, diag, smooth, parts, currents):
    ranks = len(currents)
    columns, count = currents[0].shape
    return pl.pallas_call(
        functools.partial(gram_kernel, ranks),
        in_specs=[SMEM] + [VMEM] * (ranks + len(parts) + 2),
        out_specs=[VMEM] * 3,
        out_shape=(
            jax.ShapeDtypeStruct((ranks, 3 * columns, columns), f32),
            jax.ShapeDtypeStruct((columns, count), f32),
            jax.ShapeDtypeStruct((columns, count // 2), bf16),
        ),
        compiler_params=params(),
        cost_estimate=SMALL,
        name="gram",
    )(first, diag, smooth, *currents, *parts)


def cross_kernel(ranks, place_ref, cut_ref, block_ref, image_ref, diag_ref, *refs):
    currents, gots = refs[: ranks - 1], refs[ranks - 1 : 2 * ranks - 2]
    keep_ref, give_ref, sums, block = refs[2 * ranks - 2 :]
    columns, count = image_ref.shape
    half = count // 2
    block[...] = block_ref[...]
    for rank in range(1, ranks):
        which = half_of(place_ref[0], place_ref[rank])
        lanes = pl.ds(pl.multiple_of(which * half, half), half)
        current = currents[rank - 1][:, lanes].astype(bf16).astype(f32)
        other = gots[rank - 1][...].astype(f32) + diag_ref[:, lanes].astype(bf16).astype(f32) * current
        block[rank, 2 * columns :] = close_dot(image_ref[:, lanes], other, 1, 1)
    for place in range(ranks):
        rank = jnp.bitwise_xor(place_ref[0], place)
        sums[:, place * columns : (place + 1) * columns] = block[rank]
    rows = keep_ref.shape[0] // 2
    for at, ref in enumerate((keep_ref, keep_ref, give_ref, give_ref)):
        begin = pl.multiple_of(cut_ref[at] * rows, rows)
        ref[at % 2 * rows : (at % 2 + 1) * rows, :] = sums[pl.ds(begin, rows), :]


def cross_sums(places, cuts, blocks, image, diag, currents, gots):
    ranks = len(currents)
    columns, count = image.shape
    total = ranks * columns
    half = jax.ShapeDtypeStruct((3 * columns // 2, total), f32)
    return pl.pallas_call(
        functools.partial(cross_kernel, ranks),
        in_specs=[SMEM, SMEM] + [VMEM] * (2 * ranks + 1),
        out_specs=[VMEM] * 2,
        out_shape=(half, half),
        scratch_shapes=[
            pltpu.VMEM((3 * columns, total), f32),
            pltpu.VMEM((ranks, 3 * columns, columns), f32),
        ],
        compiler_params=params(),
        cost_estimate=SMALL,
        name="cross",
    )(places, cuts, blocks, image, diag, *currents[1:], *gots)


def reciprocal(value):
    guess = pl.reciprocal(value, approx=True)
    return guess * (2.0 - value * guess)


def eliminate(panel, begin, window):
    size, total = panel.shape
    parts = [panel[:, at : at + LANES] for at in range(0, total, LANES)]
    row_at = lax.broadcasted_iota(jnp.int32, (size, LANES), 0)
    col_at = lax.broadcasted_iota(jnp.int32, (1, LANES), 1)

    def spread(pivot):
        place = (begin + pivot) % LANES
        return jnp.broadcast_to(parts[(begin + pivot) // LANES][:, place : place + 1], (size, LANES))

    cols = [spread(pivot) for pivot in range(window)]
    for pivot in range(size):
        col = cols.pop(0)
        inverse = reciprocal(col[pivot : pivot + 1, :])
        col = col - jnp.where(row_at == pivot, 1.0, 0.0)
        for part in range(len(parts)):
            row = parts[part][pivot : pivot + 1, :]
            if part == (begin + pivot) // LANES:
                row = row + jnp.where(col_at == (begin + pivot) % LANES, 1.0, 0.0)
            parts[part] = parts[part] - col * (row * inverse)
        cols = [later - col * (later[pivot : pivot + 1, :] * inverse) for later in cols]
        if pivot + window < size:
            cols.append(spread(pivot + window))
    return jnp.concatenate(parts, axis=1)


def sweep(ref, begin, size):
    total = ref.shape[0]
    panel = ref[begin : begin + size, :]
    row = eliminate(panel, begin, 6)
    col_at = lax.broadcasted_iota(jnp.int32, panel.shape, 1)
    left = [part.astype(bf16) for part in pieces_of(jnp.where(col_at < begin, -panel, panel))]
    right = [part.astype(bf16) for part in pieces_of(row)]
    update = dot(
        jnp.concatenate([left[at] for at, _ in PAIRS], axis=0),
        jnp.concatenate([right[at] for _, at in PAIRS], axis=0),
        0,
        0,
    )
    lanes = lax.broadcasted_iota(jnp.int32, (total, total), 1)
    ref[...] = jnp.where((lanes >= begin) & (lanes < begin + size), 0.0, ref[...]) - update
    ref[begin : begin + size, :] = row


def solve_kernel(columns, size, place_ref, share_ref, *refs):
    shares = refs[:-7]
    step_ref, turn_ref, sums, grams, gram_inv, square_inv, step_all = refs[-7:]
    rows, total = shares[0].shape
    for at, share in enumerate(shares):
        sums[pl.ds(pl.multiple_of(share_ref[at] * rows, rows), rows), :] = share[...]
    for rank in range(total // columns):
        for which in range(3):
            begin = (rank * 3 + which) * columns
            grams[which, rank * columns : (rank + 1) * columns, :] = sums[begin : begin + columns, :]
    cross = grams[0]
    gram = 0.5 * (cross + cross.T)
    gram_scale = 1.0 / jnp.max(gram, keepdims=True)
    square_scale = 1.0 / jnp.max(grams[1], keepdims=True)
    gram_inv[...] = gram * gram_scale
    square_inv[...] = grams[1] * square_scale
    for begin in range(0, total, size):
        sweep(gram_inv, begin, size)
        sweep(square_inv, begin, size)
    mine = pl.ds(pl.multiple_of(place_ref[0] * columns, columns), columns)
    step_all[...] = close_dot(grams[1], gram_inv[...] * gram_scale, 1, 0)
    step = step_all[mine, :]
    step_ref[...] = step
    row_at = lax.broadcasted_iota(jnp.int32, (total, total), 0) // columns
    col_at = lax.broadcasted_iota(jnp.int32, (total, total), 1) // columns
    pairs = grams[2]
    images = pairs + jnp.where(row_at == col_at, 0.0, pairs.T)
    left = close_dot(step, images, 1, 0)
    across = close_dot(step, grams[0], 1, 0)
    grams[0] = grams[0].T
    left = left - grams[0, mine, :]
    following = grams[1, mine, :] - across + close_dot(left, step_all[...], 1, 1)
    turn_ref[...] = close_dot(following, square_inv[...] * square_scale, 1, 0)


def solve(places, share_places, shares, columns):
    total = shares[0].shape[1]
    square = pltpu.VMEM((total, total), f32)
    rows = jax.ShapeDtypeStruct((columns, total), f32)
    return pl.pallas_call(
        functools.partial(solve_kernel, columns, 32),
        in_specs=[SMEM, SMEM] + [VMEM] * len(shares),
        out_specs=[VMEM] * 2,
        out_shape=(rows, rows),
        scratch_shapes=[
            pltpu.VMEM((3 * total, total), f32),
            pltpu.VMEM((3, total, total), f32),
            square,
            square,
            square,
        ],
        compiler_params=params(),
        name="solve",
    )(places, share_places, *shares)


def others_kernel(ranks, place_ref, diag_ref, *refs):
    currents, gots, rests, outs = (refs[at * (ranks - 1) : (at + 1) * (ranks - 1)] for at in range(4))
    half = diag_ref.shape[1] // 2
    for at in range(ranks - 1):
        which = half_of(place_ref[0], place_ref[at + 1])
        for place, smooth in ((which, gots[at]), (1 - which, rests[at])):
            lanes = pl.ds(pl.multiple_of(place * half, half), half)
            fixed = diag_ref[:, lanes].astype(bf16).astype(f32) * currents[at][:, lanes].astype(bf16).astype(f32)
            outs[at][:, lanes] = smooth[...].astype(f32) + fixed


def other_images(places, diag, currents, gots, rests):
    ranks = len(currents)
    return pl.pallas_call(
        functools.partial(others_kernel, ranks),
        in_specs=[SMEM] + [VMEM] * (3 * ranks - 2),
        out_specs=[VMEM] * (ranks - 1),
        out_shape=[jax.ShapeDtypeStruct(currents[0].shape, f32)] * (ranks - 1),
        compiler_params=params(),
        cost_estimate=SMALL,
        name="other_images",
    )(places, diag, *currents[1:], *gots, *rests)


def finish_kernel(ranks, chunks, place_ref, step_ref, turn_ref, *refs):
    currents, images, refs = refs[:ranks], refs[ranks : 2 * ranks], refs[2 * ranks :]
    outs, made, (current_all, image_all, sems) = refs[:3], refs[3:6], refs[6:]
    columns, count = currents[0].shape
    for rank in range(ranks):
        at = pl.ds(pl.multiple_of(place_ref[rank] * columns, columns), columns)
        current_all[at, :] = currents[rank][...]
        image_all[at, :] = images[rank][...]
    step_high, step_low = split(step_ref[...])
    turn_high, turn_low = split(turn_ref[...])
    both = jnp.concatenate([step_high, step_low, turn_high, turn_low], axis=0)
    highs = jnp.concatenate([step_high, turn_high], axis=0)
    steps = jnp.concatenate([step_high, step_low], axis=0)
    width = count // chunks
    copies = []
    for chunk in range(chunks):
        lanes = pl.ds(chunk * width, width)
        current_high, current_low = split(current_all[:, lanes])
        image_high, image_low = split(image_all[:, lanes])
        every = dot(both, current_high, 1, 0)
        rest = dot(highs, current_low, 1, 0)
        away = dot(steps, image_high, 1, 0)
        step_part, step_more, turn_part, turn_more = (every[at * columns : (at + 1) * columns] for at in range(4))
        away = away[:columns] + (away[columns:] + dot(step_high, image_low, 1, 0))
        remainder = currents[0][:, lanes] - away
        made[0][:, lanes] = step_part + (step_more + rest[:columns])
        made[1][:, lanes] = remainder
        made[2][:, lanes] = remainder + (turn_part + (turn_more + rest[columns:]))
        for at in range(3):
            copy = pltpu.make_async_copy(made[at].at[:, lanes], outs[at].at[:, lanes], sems.at[at, chunk])
            copy.start()
            copies.append(copy)
    for copy in copies:
        copy.wait()


def finish(places, step, turn, currents, images):
    ranks = len(currents)
    columns, count = currents[0].shape
    total = ranks * columns
    chunks = 2
    return pl.pallas_call(
        functools.partial(finish_kernel, ranks, chunks),
        in_specs=[SMEM] + [VMEM] * (2 * ranks + 2),
        out_specs=[pl.BlockSpec(memory_space=pl.ANY)] * 3,
        out_shape=[jax.ShapeDtypeStruct((columns, count), f32)] * 3,
        scratch_shapes=[pltpu.VMEM((columns, count), f32)] * 3
        + [pltpu.VMEM((total, count), f32)] * 2
        + [pltpu.SemaphoreType.DMA((3, chunks))],
        compiler_params=params(),
        cost_estimate=SMALL,
        name="finish",
    )(places, step, turn, *currents, *images)


def swap(value, axis, bits):
    size = lax.axis_size(axis)
    return lax.ppermute(value, axis, [(at, at ^ bits) for at in range(size)])


def pair_swap(value, bits, ranks):
    rank_bits, tri_bit = bits % ranks, bits // ranks
    if tri_bit == 0:
        return swap(value, "rhs", rank_bits)
    if rank_bits == 0:
        return swap(value, "tri", 1)
    count = lax.axis_size("tri")
    perm = [
        (tri * ranks + rank, (tri ^ 1) * ranks + (rank ^ rank_bits)) for tri in range(count) for rank in range(ranks)
    ]
    return lax.ppermute(value, ("tri", "rhs"), perm)


def indices(*values):
    return jnp.stack(values).astype(jnp.int32)


def all_sum(keep, give, beside, ranks, tris):
    value = keep + swap(give, "split", 1)
    value, give = jnp.split(value, 2)
    value = value + swap(give, "tri", 1)
    parts = [swap(value, "tri", 2 * far) for far in range(1, tris // 2)]
    parts, beside = lax.optimization_barrier((parts, beside))
    value = sum(parts, value)
    shares = [value] + [pair_swap(value, bits, ranks) for bits in range(1, 2 * ranks)]
    shares += [swap(share, "split", 1) for share in shares]
    return shares, beside


def body(residual, attach, vertices, corners, layers):
    columns, count = residual.shape
    tris, ranks, cores = lax.axis_size("tri"), lax.axis_size("rhs"), lax.axis_size("split")
    tri, rank, core = lax.axis_index("tri"), lax.axis_index("rhs"), lax.axis_index("split")
    near = min(4, tris)
    groups = tris // near
    scale = 1.0 / math.sqrt(corners.shape[1])

    my_ids = (tri * cores + core) * count + jnp.arange(count, dtype=jnp.int32)
    current = residual + inject * (attach[:, None] == my_ids[None, :]).astype(f32)
    packed = current.astype(bf16)
    currents = [current] + [swap(current, "rhs", bits) for bits in range(1, ranks)]
    sources = [packed] + [swap(packed, "tri", bits) for bits in range(1, near)]

    own_blocks = [(tri ^ (near * far)) * cores + core for far in range(groups)]
    near_blocks = [(tri ^ bits) * cores + core for bits in range(1, near)]
    blocks = indices(*reversed(near_blocks), *own_blocks)
    half_place = half_of(rank ^ 1, rank) if ranks > 1 else jnp.int32(0)
    first = indices(half_place)
    places = indices(*[rank ^ bits for bits in range(ranks)])
    low = tri & 1
    cuts = indices(2 * core + low, 2 * core + 1 - low, 2 - 2 * core + low, 3 - 2 * core - low)
    share_places = indices(
        *[
            (rank ^ (bits % ranks)) * 4 + (core ^ other) * 2 + (low ^ (bits // ranks))
            for other in range(2)
            for bits in range(2 * ranks)
        ]
    )
    vertices, packed, blocks, first, places, cuts, share_places = lax.optimization_barrier(
        (vertices, packed, blocks, first, places, cuts, share_places)
    )
    a_side, b_side, diag = geometry(blocks, near, vertices, corners, layers, count, scale)
    slots = list(reversed(range(near)))
    sides = [a_side, b_side, swap(b_side, "split", 1)]

    def part(which, targets, starts=None, **more):
        return image_part(
            first, sources[which], [(0, slot) for slot in slots[which]], sides, targets, starts, **more
        )

    fars = range(1, groups)
    arrived = [[], []]
    last = slice(near - 1, near)
    far_sum = []
    if groups > 1:
        own_at, other_at = ([(side, far, None) for far in fars] for side in (1, 2))
        far_own = part(slice(0, 1), own_at)
        sides, far_own = lax.optimization_barrier((sides, far_own))
        far_other = part(slice(0, 1), other_at)
        for at in range(1, near - 1):
            both = part(slice(at, at + 1), other_at + own_at, [*far_other, *far_own])
            far_other, far_own = both[: len(other_at)], both[len(other_at) :]
        ready = []
        sides, currents = lax.optimization_barrier((sides, currents))
        for half in range(2):
            ready.append(part(last, [(*at[:2], half) for at in other_at], far_other, kind=bf16))
            sides, _ = lax.optimization_barrier((sides, ready))
        sent = [[swap(value, "split", 1) for value in values] for values in ready]
        for half in range(2):
            far_sum.append(
                part(last, [(*at[:2], half) for at in own_at], far_own, extras=sent[half], kind=bf16)
            )
            arrived[half] = [swap(value, "tri", near * far) for far, value in zip(fars, far_sum[half])]
            sides, _ = lax.optimization_barrier((sides, far_sum))
        sources, _ = lax.optimization_barrier((sources, far_sum[0]))
    mine = stack_rows(sources, a_side, near)
    theirs = swap(mine, "split", 1)
    after, _ = lax.optimization_barrier((first, far_sum))
    own_first = own_image(0, after, [mine, theirs], b_side, near, True)
    after, _ = lax.optimization_barrier((first, own_first))
    own_second = own_image(1, after, [mine], b_side, near, True)
    own_first, own_second = lax.optimization_barrier((own_first, own_second))
    smooth, low_first = combine([own_first, *arrived[0]])
    after, _ = lax.optimization_barrier((first, low_first))
    own_second = own_image(1, after, [theirs], b_side, near, False, [own_second])
    blocks, image, low_second = gram_sums(first, diag, smooth, [own_second, *arrived[1]], currents)
    gots, rests = [], []
    for bits in range(1, ranks):
        if bits == 1:
            give, rest = low_first, low_second
        else:
            is_first = half_of(rank ^ bits, rank) == half_place
            give = jnp.where(is_first, low_first, low_second)
            rest = jnp.where(is_first, low_second, low_first)
        gots.append(swap(give, "rhs", bits))
        rests.append(rest)
    keep, give = cross_sums(places, cuts, blocks, image, diag, currents, gots)
    rests, _ = lax.optimization_barrier((rests, gots))
    rests = [swap(rest, "rhs", bits) for bits, rest in enumerate(rests, 1)]
    beside = other_images(places, diag, currents, gots, rests)
    shares, beside = all_sum(keep, give, beside, ranks, tris)
    step, turn = solve(places, share_places, shares, columns)
    return finish(places, step, turn, currents, [image, *beside])


def solution(mesh):
    return jax.shard_map(
        body,
        mesh=mesh,
        in_specs=(P("rhs", ("tri", "split")), P("rhs"), P(), P(), P()),
        out_specs=(
            P("rhs", ("tri", "split")),
            P("rhs", ("tri", "split")),
            P("rhs", ("tri", "split")),
        ),
        check_vma=False,
    )
```

```python
import functools
import math

import jax
import jax.numpy as jnp
from jax import lax
from jax.experimental import pallas as pl
from jax.experimental.pallas import tpu as pltpu
from jax.sharding import PartitionSpec as P

smooth_sq = 0.01
self_term = 1.0
inject = 3.0
f32 = jnp.float32
bf16 = jnp.bfloat16
LANES = 128
LOW = 64
FEATURES = 32
TILE = 512 * 1024
PAIRS = ((0, 0), (0, 1), (1, 0), (1, 1), (0, 2), (2, 0))
VMEM = pl.BlockSpec(memory_space=pltpu.VMEM)
SMEM = pl.BlockSpec(memory_space=pltpu.SMEM)
SMALL = pl.CostEstimate(flops=1024, bytes_accessed=1024, transcendentals=0)


def dot(a, b, ca, cb, precision=None):
    return lax.dot_general(
        a, b, (((ca,), (cb,)), ((), ())), precision=precision, preferred_element_type=f32
    )


def split(value):
    high = value.astype(bf16)
    return high, (value - high.astype(f32)).astype(bf16)


def close_dot(a, b, ca, cb):
    a_high, a_low = split(a)
    b_high, b_low = split(b)
    return (dot(a_low, b_high, ca, cb) + dot(a_high, b_low, ca, cb)) + dot(a_high, b_high, ca, cb)


def params(mebibytes=12):
    return pltpu.CompilerParams(vmem_limit_bytes=mebibytes * 1024 * 1024)


def pieces_of(value):
    high = value.astype(bf16).astype(f32)
    rest = value - high
    middle = rest.astype(bf16).astype(f32)
    return (high, middle, rest - middle)


def geometry_kernel(
    scale, near, blocks_ref, vertices_ref, corners_ref, layers_ref, a_ref, b_ref, diag_ref, plain, table, a_rows, b_rows
):
    count = corners_ref.shape[1]
    tops = plain.shape[0]

    @pl.when(pl.program_id(0) == 0)
    def _():
        for axis in range(3):
            for top in range(tops):
                plain[top : top + 1, axis * LANES : (axis + 1) * LANES] = vertices_ref[
                    axis : axis + 1, top * LANES : (top + 1) * LANES
                ]
        for axis in range(3):
            for side in range(2):
                begin = axis * LANES + side * LOW
                value = plain[:, begin : begin + LOW]
                high = value.astype(bf16)
                low = (value - high.astype(f32)).astype(bf16)
                for at, part in enumerate((high, low)):
                    row = (2 * at + side) * tops
                    table[row : row + tops, axis * LOW : (axis + 1) * LOW] = part

    top_iota = lax.broadcasted_iota(jnp.int32, (2 * tops, count), 0)
    low_iota = lax.broadcasted_iota(jnp.int32, (LOW, count), 0)
    points = []
    for corner in range(3):
        index = corners_ref[corner : corner + 1, :]
        place = (index >> 7) + tops * ((index >> 6) & 1)
        top = jnp.where(top_iota == place, 1.0, 0.0).astype(bf16)
        low = low_iota == (index & (LOW - 1))
        found = dot(table[...], jnp.concatenate([top, top], axis=0), 0, 0)
        points.append(
            [
                jnp.sum(jnp.where(low, found[axis * LOW : (axis + 1) * LOW], 0.0), axis=0, keepdims=True)
                for axis in range(3)
            ]
        )
    p0, p1, p2 = points
    centre = [(p0[k] + p1[k] + p2[k]) / 3.0 for k in range(3)]
    e1 = [p1[k] - p0[k] for k in range(3)]
    e2 = [p2[k] - p0[k] for k in range(3)]
    cross_x = e1[1] * e2[2] - e1[2] * e2[1]
    cross_y = e1[2] * e2[0] - e1[0] * e2[2]
    cross_z = e1[0] * e2[1] - e1[1] * e2[0]
    area_sq = cross_x * cross_x + cross_y * cross_y + cross_z * cross_z
    layers = layers_ref[...]
    factor = jnp.where(layers == 0, 1.0, jnp.where(layers == 1, 0.3, 0.8)).astype(f32)
    weight = factor * (0.5 + area_sq / (1.0 + area_sq))
    unit = 1.0 / (scale * (weight * weight))
    norm = centre[0] * centre[0] + centre[1] * centre[1] + centre[2] * centre[2]
    a_side = [unit * norm, unit] + [unit * c for c in centre]
    b_side = [unit, unit * (norm + smooth_sq)] + [-2.0 * unit * c for c in centre]
    block = pl.program_id(0)

    def store(values, which, rows, out_ref):
        parts = [pieces_of(value) for value in values]
        row = 0
        for pair in PAIRS:
            for term in range(5):
                rows[row : row + 1, :] = parts[term][pair[which]]
                row += 1
        rows[row:, :] = jnp.zeros((FEATURES - row, count), f32)
        out_ref[...] = rows[...].astype(bf16)

    @pl.when(block < near)
    def _():
        store(a_side, 0, a_rows, a_ref)

    @pl.when(block >= near - 1)
    def _():
        store(b_side, 1, b_rows, b_ref)

    @pl.when(block == near - 1)
    def _():
        diag_ref[...] = weight * weight * (lax.rsqrt(jnp.full_like(weight, smooth_sq)) * scale + self_term)


def geometry(blocks, near, vertices, corners, layers, count, scale):
    n = blocks.shape[0]
    points = vertices.shape[1]
    tops = points // LANES
    return pl.pallas_call(
        functools.partial(geometry_kernel, scale, near),
        grid_spec=pltpu.PrefetchScalarGridSpec(
            num_scalar_prefetch=1,
            grid=(n,),
            in_specs=[
                pl.BlockSpec((3, points), lambda g, blk: (0, 0)),
                pl.BlockSpec((3, count), lambda g, blk: (0, blk[g])),
                pl.BlockSpec((1, count), lambda g, blk: (0, blk[g])),
            ],
            out_specs=[
                pl.BlockSpec((None, FEATURES, count), lambda g, blk: (jnp.minimum(g, near - 1), 0, 0)),
                pl.BlockSpec((None, FEATURES, count), lambda g, blk: (jnp.maximum(g - near + 1, 0), 0, 0)),
                pl.BlockSpec((1, count), lambda g, blk: (0, 0)),
            ],
            scratch_shapes=[
                pltpu.VMEM((tops, 3 * LANES), f32),
                pltpu.VMEM((4 * tops, 3 * LOW), bf16),
                pltpu.VMEM((FEATURES, count), f32),
                pltpu.VMEM((FEATURES, count), f32),
            ],
        ),
        out_shape=(
            jax.ShapeDtypeStruct((near, FEATURES, count), bf16),
            jax.ShapeDtypeStruct((n - near + 1, FEATURES, count), bf16),
            jax.ShapeDtypeStruct((1, count), f32),
        ),
        compiler_params=params(),
        name="geometry",
    )(blocks, vertices, corners, layers[None, :])


def image_kernel(sources, slots, targets, has_start, extras, first_ref, *refs):
    refs = list(refs)
    densities = [refs.pop(0) for _ in sources]
    sides = [refs.pop(0) for _ in range(1 + max(which for which, _ in [*slots, *[t[:2] for t in targets]]))]
    starts = [refs.pop(0) for _ in targets] if has_start else [None] * len(targets)
    more = [refs.pop(0) for _ in range(extras)]
    count = densities[0].shape[1]
    half = count // 2
    for at, (which, slot, part) in enumerate(targets):
        columns, width = refs[at].shape
        chunk = min(TILE // width, count)
        if part is None:
            lanes = slice(None)
        else:
            place = first_ref[0] if part == 0 else 1 - first_ref[0]
            lanes = pl.ds(pl.multiple_of(place * half, half), half)
        b = sides[which][slot, :, lanes]
        acc = starts[at][:, lanes] if has_start else jnp.zeros((columns, width), f32)
        for source, (density, (side, a_slot)) in enumerate(zip(densities, slots)):
            for begin in range(0, count, chunk):
                tile = lax.rsqrt(dot(sides[side][a_slot, :, begin : begin + chunk], b, 0, 0))
                acc = acc + dot(density[:, begin : begin + chunk], tile.astype(bf16), 1, 0)
        if at < extras:
            acc = acc + more[at][...].astype(f32)
        refs[at][...] = acc.astype(refs[at].dtype)


def image_part(first, densities, slots, sides, targets, starts=None, extras=(), kind=f32):
    columns, count = densities[0].shape
    sides = sides[: 1 + max(which for which, _ in [*slots, *[t[:2] for t in targets]])]
    operands = [first, *densities, *sides, *(starts or []), *extras]
    widths = [count if part is None else count // 2 for _, _, part in targets]
    return pl.pallas_call(
        functools.partial(image_kernel, range(len(densities)), slots, targets, bool(starts), len(extras)),
        in_specs=[SMEM] + [VMEM] * (len(operands) - 1),
        out_specs=[VMEM] * len(targets),
        out_shape=[jax.ShapeDtypeStruct((columns, width), kind) for width in widths],
        compiler_params=params(12),
        cost_estimate=SMALL,
        name="image_part",
    )(*operands)


def half_of(mine, other):
    return (mine > other).astype(jnp.int32)


def stack_kernel(near, *refs):
    a_ref, out_ref = refs[near:]
    columns = refs[0].shape[0]
    for source in range(near):
        out_ref[source * columns : (source + 1) * columns, :] = refs[source][...]
        side = near * columns + source * FEATURES
        out_ref[side : side + FEATURES, :] = a_ref[near - 1 - source]


def stack_rows(sources, a_side, near):
    columns, count = sources[0].shape
    return pl.pallas_call(
        functools.partial(stack_kernel, near),
        in_specs=[VMEM] * (near + 1),
        out_specs=VMEM,
        out_shape=jax.ShapeDtypeStruct((near * (columns + FEATURES), count), bf16),
        compiler_params=params(),
        cost_estimate=SMALL,
        name="stack_rows",
    )(*sources, a_side)


def own_kernel(near, part, diagonal, stacks, first_ref, b_ref, *refs):
    out_ref = refs[-1]
    columns, width = out_ref.shape
    count = b_ref.shape[2]
    chunk = min(TILE // width, count)
    place = first_ref[0] if part == 0 else 1 - first_ref[0]
    b = b_ref[0, :, pl.ds(pl.multiple_of(place * width, width), width)]
    acc = refs[stacks][...] if len(refs) > stacks + 1 else jnp.zeros((columns, width), f32)
    for at, ref in enumerate(refs[:stacks]):
        for source in range(near):
            side = near * columns + source * FEATURES
            for begin in range(0, count, chunk):
                lanes = slice(begin, begin + chunk)
                tile = lax.rsqrt(dot(ref[side : side + FEATURES, lanes], b, 0, 0))
                if diagonal and at == 0 and source == 0:
                    rows = begin + lax.broadcasted_iota(jnp.int32, tile.shape, 0)
                    cols = place * width + lax.broadcasted_iota(jnp.int32, tile.shape, 1)
                    tile = jnp.where(rows == cols, 0.0, tile)
                acc = acc + dot(ref[source * columns : (source + 1) * columns, lanes], tile.astype(bf16), 1, 0)
    out_ref[...] = acc


def own_image(part, first, stacks, b_side, near, diagonal, start=()):
    rows, count = stacks[0].shape
    columns = rows // near - FEATURES
    operands = [b_side, *stacks, *start]
    return pl.pallas_call(
        functools.partial(own_kernel, near, part, diagonal, len(stacks)),
        in_specs=[SMEM] + [VMEM] * len(operands),
        out_specs=VMEM,
        out_shape=jax.ShapeDtypeStruct((columns, count // 2), f32),
        compiler_params=params(12),
        cost_estimate=SMALL,
        name="own_image",
    )(first, *operands)


def add_parts(refs):
    total = refs[0][...].astype(f32)
    for ref in refs[1:]:
        total = total + ref[...].astype(f32)
    return total


def combine_kernel(*refs):
    smooth = add_parts(refs[:-2])
    refs[-2][...] = smooth
    refs[-1][...] = smooth.astype(bf16)


def combine(parts):
    return pl.pallas_call(
        combine_kernel,
        in_specs=[VMEM] * len(parts),
        out_specs=[VMEM] * 2,
        out_shape=[jax.ShapeDtypeStruct(parts[0].shape, kind) for kind in (f32, bf16)],
        compiler_params=params(),
        cost_estimate=SMALL,
        name="combine",
    )(*parts)


def full_image(first_ref, diag_ref, current_ref, smooths, image_ref):
    half = smooths[0].shape[1]
    for place, smooth in zip((first_ref[0], 1 - first_ref[0]), smooths):
        lanes = pl.ds(pl.multiple_of(place * half, half), half)
        fixed = diag_ref[:, lanes].astype(bf16).astype(f32) * current_ref[:, lanes].astype(bf16).astype(f32)
        image_ref[:, lanes] = smooth + fixed


def gram_kernel(ranks, place_ref, first_ref, diag_ref, first_half, *refs):
    currents, parts, (block, image, low) = refs[:ranks], refs[ranks:-3], refs[-3:]
    columns = currents[0].shape[0]
    second_half = add_parts(parts)
    low[...] = second_half.astype(bf16)
    full_image(first_ref, diag_ref, currents[0], (first_half[...], second_half), image)
    mine = currents[0][...]
    half = columns // 2
    for rank in range(ranks):
        current = currents[rank][...]
        block[rank, :columns] = close_dot(image[...], current, 1, 1)
        if rank > 0:
            ahead = place_ref[0] < place_ref[rank]
            left = jnp.where(ahead, mine[:half], current[half:])
            block[rank, 2 * columns : 2 * columns + half] = close_dot(left, jnp.where(ahead, current, mine), 1, 1)
    square = close_dot(mine, mine, 1, 1)
    row_at = lax.broadcasted_iota(jnp.int32, square.shape, 0)
    col_at = lax.broadcasted_iota(jnp.int32, square.shape, 1)
    block[0, columns : 2 * columns] = jnp.where(row_at > col_at, square, close_dot(image[...], image[...], 1, 1))
    diagonal = jnp.sum(jnp.where(row_at == col_at, square, 0.0), axis=0, keepdims=True)
    block[0, 2 * columns : 2 * columns + half] = jnp.broadcast_to(diagonal, (half, columns))
    spare = block.shape[1] - 2 * columns - half
    if spare > 0:
        block[:, 2 * columns + half :] = jnp.zeros((ranks, spare, columns), f32)


def sum_rows(columns):
    return -(-5 * columns // 64) * 32


def gram_sums(places, first, diag, smooth, parts, currents):
    ranks = len(currents)
    columns, count = currents[0].shape
    return pl.pallas_call(
        functools.partial(gram_kernel, ranks),
        in_specs=[SMEM] * 2 + [VMEM] * (ranks + len(parts) + 2),
        out_specs=[VMEM] * 3,
        out_shape=(
            jax.ShapeDtypeStruct((ranks, sum_rows(columns), columns), f32),
            jax.ShapeDtypeStruct((columns, count), f32),
            jax.ShapeDtypeStruct((columns, count // 2), bf16),
        ),
        compiler_params=params(),
        cost_estimate=SMALL,
        name="gram",
    )(places, first, diag, smooth, *currents, *parts)


def cross_kernel(ranks, place_ref, cut_ref, block_ref, image_ref, diag_ref, *refs):
    currents, gots = refs[: ranks - 1], refs[ranks - 1 : 2 * ranks - 2]
    keep_ref, give_ref, sums, block = refs[2 * ranks - 2 :]
    columns, count = image_ref.shape
    half = count // 2
    block[...] = block_ref[...]
    for rank in range(1, ranks):
        which = half_of(place_ref[0], place_ref[rank])
        lanes = pl.ds(pl.multiple_of(which * half, half), half)
        current = currents[rank - 1][:, lanes].astype(bf16).astype(f32)
        other = gots[rank - 1][...].astype(f32) + diag_ref[:, lanes].astype(bf16).astype(f32) * current
        block[rank, columns : 2 * columns] = close_dot(image_ref[:, lanes], other, 1, 1)
    for place in range(ranks):
        rank = jnp.bitwise_xor(place_ref[0], place)
        sums[:, place * columns : (place + 1) * columns] = block[rank]
    rows = keep_ref.shape[0] // 2
    for at, ref in enumerate((keep_ref, keep_ref, give_ref, give_ref)):
        begin = pl.multiple_of(cut_ref[at] * rows, rows)
        ref[at % 2 * rows : (at % 2 + 1) * rows, :] = sums[pl.ds(begin, rows), :]


def cross_sums(places, cuts, blocks, image, diag, currents, gots):
    ranks = len(currents)
    columns, count = image.shape
    total = ranks * columns
    rows = sum_rows(columns)
    half = jax.ShapeDtypeStruct((rows // 2, total), f32)
    return pl.pallas_call(
        functools.partial(cross_kernel, ranks),
        in_specs=[SMEM, SMEM] + [VMEM] * (2 * ranks + 1),
        out_specs=[VMEM] * 2,
        out_shape=(half, half),
        scratch_shapes=[
            pltpu.VMEM((rows, total), f32),
            pltpu.VMEM((ranks, rows, columns), f32),
        ],
        compiler_params=params(),
        cost_estimate=SMALL,
        name="cross",
    )(places, cuts, blocks, image, diag, *currents[1:], *gots)


def reciprocal(value):
    guess = pl.reciprocal(value, approx=True)
    return guess * (2.0 - value * guess)


def eliminate(panel, begin, window):
    size, total = panel.shape
    parts = [panel[:, at : at + LANES] for at in range(0, total, LANES)]
    row_at = lax.broadcasted_iota(jnp.int32, (size, LANES), 0)
    col_at = lax.broadcasted_iota(jnp.int32, (1, LANES), 1)

    def spread(pivot):
        place = (begin + pivot) % LANES
        return jnp.broadcast_to(parts[(begin + pivot) // LANES][:, place : place + 1], (size, LANES))

    cols = [spread(pivot) for pivot in range(window)]
    for pivot in range(size):
        col = cols.pop(0)
        inverse = reciprocal(col[pivot : pivot + 1, :])
        col = col - jnp.where(row_at == pivot, 1.0, 0.0)
        for part in range(len(parts)):
            row = parts[part][pivot : pivot + 1, :]
            if part == (begin + pivot) // LANES:
                row = row + jnp.where(col_at == (begin + pivot) % LANES, 1.0, 0.0)
            parts[part] = parts[part] - col * (row * inverse)
        cols = [later - col * (later[pivot : pivot + 1, :] * inverse) for later in cols]
        if pivot + window < size:
            cols.append(spread(pivot + window))
    return jnp.concatenate(parts, axis=1)


def sweep(ref, begin, size):
    total = ref.shape[0]
    panel = ref[begin : begin + size, :]
    row = eliminate(panel, begin, 6)
    col_at = lax.broadcasted_iota(jnp.int32, panel.shape, 1)
    left = [part.astype(bf16) for part in pieces_of(jnp.where(col_at < begin, -panel, panel))]
    right = [part.astype(bf16) for part in pieces_of(row)]
    update = dot(
        jnp.concatenate([left[at] for at, _ in PAIRS], axis=0),
        jnp.concatenate([right[at] for _, at in PAIRS], axis=0),
        0,
        0,
    )
    lanes = lax.broadcasted_iota(jnp.int32, (total, total), 1)
    ref[...] = jnp.where((lanes >= begin) & (lanes < begin + size), 0.0, ref[...]) - update
    ref[begin : begin + size, :] = row


def solve_kernel(columns, size, place_ref, share_ref, *refs):
    shares = refs[:-7]
    step_ref, turn_ref, sums, grams, gram_inv, square_inv, step_all = refs[-7:]
    rows, total = shares[0].shape
    for at, share in enumerate(shares):
        sums[pl.ds(pl.multiple_of(share_ref[at] * rows, rows), rows), :] = share[...]
    ranks = total // columns
    height = sums.shape[0] // ranks
    half = columns // 2
    row_at = lax.broadcasted_iota(jnp.int32, (total, total), 0)
    col_at = lax.broadcasted_iota(jnp.int32, (total, total), 1)
    same = row_at // columns == col_at // columns
    lanes = col_at[:1] // columns
    diagonal = jnp.zeros((1, total), f32)
    grams[1] = jnp.zeros((total, total), f32)
    for rank in range(ranks):
        mine = slice(rank * columns, (rank + 1) * columns)
        base = rank * height
        grams[0, mine, :] = sums[base : base + columns, :]
        grams[2, mine, :] = sums[base + columns : base + 2 * columns, :]
        base += 2 * columns
        diagonal = jnp.where(lanes == rank, sums[base : base + 1, :], diagonal)
        for other in range(ranks):
            block = sums[base : base + half, other * columns : (other + 1) * columns]
            if other > rank:
                grams[1, rank * columns : rank * columns + half, other * columns : (other + 1) * columns] = block
            if other < rank:
                grams[1, other * columns + half : (other + 1) * columns, mine] = block
    pairs = grams[2]
    flipped = pairs.T
    across = grams[1]
    own = jnp.where(row_at > col_at, pairs, jnp.where(row_at < col_at, flipped, diagonal))
    grams[1] = jnp.where(same, own, across + across.T)
    grams[2] = jnp.where(same, jnp.where(row_at > col_at, flipped, pairs), pairs + flipped)
    cross = grams[0]
    gram = 0.5 * (cross + cross.T)
    gram_scale = 1.0 / jnp.max(gram, keepdims=True)
    square_scale = 1.0 / jnp.max(grams[1], keepdims=True)
    gram_inv[...] = gram * gram_scale
    square_inv[...] = grams[1] * square_scale
    for begin in range(0, total, size):
        sweep(gram_inv, begin, size)
        sweep(square_inv, begin, size)
    mine = pl.ds(pl.multiple_of(place_ref[0] * columns, columns), columns)
    step_all[...] = close_dot(grams[1], gram_inv[...] * gram_scale, 1, 0)
    step = step_all[mine, :]
    step_ref[...] = step
    left = close_dot(step, grams[2], 1, 0)
    across = close_dot(step, grams[0], 1, 0)
    grams[0] = grams[0].T
    left = left - grams[0, mine, :]
    following = grams[1, mine, :] - across + close_dot(left, step_all[...], 1, 1)
    turn_ref[...] = close_dot(following, square_inv[...] * square_scale, 1, 0)


def solve(places, share_places, shares, columns):
    total = shares[0].shape[1]
    square = pltpu.VMEM((total, total), f32)
    rows = jax.ShapeDtypeStruct((columns, total), f32)
    return pl.pallas_call(
        functools.partial(solve_kernel, columns, 32),
        in_specs=[SMEM, SMEM] + [VMEM] * len(shares),
        out_specs=[VMEM] * 2,
        out_shape=(rows, rows),
        scratch_shapes=[
            pltpu.VMEM((total // columns * sum_rows(columns), total), f32),
            pltpu.VMEM((3, total, total), f32),
            square,
            square,
            square,
        ],
        compiler_params=params(),
        name="solve",
    )(places, share_places, *shares)


def others_kernel(ranks, place_ref, diag_ref, *refs):
    currents, gots, rests, outs = (refs[at * (ranks - 1) : (at + 1) * (ranks - 1)] for at in range(4))
    half = diag_ref.shape[1] // 2
    for at in range(ranks - 1):
        which = half_of(place_ref[0], place_ref[at + 1])
        for place, smooth in ((which, gots[at]), (1 - which, rests[at])):
            lanes = pl.ds(pl.multiple_of(place * half, half), half)
            fixed = diag_ref[:, lanes].astype(bf16).astype(f32) * currents[at][:, lanes].astype(bf16).astype(f32)
            outs[at][:, lanes] = smooth[...].astype(f32) + fixed


def other_images(places, diag, currents, gots, rests):
    ranks = len(currents)
    return pl.pallas_call(
        functools.partial(others_kernel, ranks),
        in_specs=[SMEM] + [VMEM] * (3 * ranks - 2),
        out_specs=[VMEM] * (ranks - 1),
        out_shape=[jax.ShapeDtypeStruct(currents[0].shape, f32)] * (ranks - 1),
        compiler_params=params(),
        cost_estimate=SMALL,
        name="other_images",
    )(places, diag, *currents[1:], *gots, *rests)


def finish_kernel(ranks, chunks, place_ref, step_ref, turn_ref, *refs):
    currents, images, refs = refs[:ranks], refs[ranks : 2 * ranks], refs[2 * ranks :]
    outs, made, (current_all, image_all, sems) = refs[:3], refs[3:6], refs[6:]
    columns, count = currents[0].shape
    for rank in range(ranks):
        at = pl.ds(pl.multiple_of(place_ref[rank] * columns, columns), columns)
        current_all[at, :] = currents[rank][...]
        image_all[at, :] = images[rank][...]
    step_high, step_low = split(step_ref[...])
    turn_high, turn_low = split(turn_ref[...])
    both = jnp.concatenate([step_high, step_low, turn_high, turn_low], axis=0)
    highs = jnp.concatenate([step_high, turn_high], axis=0)
    steps = jnp.concatenate([step_high, step_low], axis=0)
    width = count // chunks
    copies = []
    for chunk in range(chunks):
        lanes = pl.ds(chunk * width, width)
        current_high, current_low = split(current_all[:, lanes])
        image_high, image_low = split(image_all[:, lanes])
        every = dot(both, current_high, 1, 0)
        rest = dot(highs, current_low, 1, 0)
        away = dot(steps, image_high, 1, 0)
        step_part, step_more, turn_part, turn_more = (every[at * columns : (at + 1) * columns] for at in range(4))
        away = away[:columns] + (away[columns:] + dot(step_high, image_low, 1, 0))
        remainder = currents[0][:, lanes] - away
        made[0][:, lanes] = step_part + (step_more + rest[:columns])
        made[1][:, lanes] = remainder
        made[2][:, lanes] = remainder + (turn_part + (turn_more + rest[columns:]))
        for at in range(3):
            copy = pltpu.make_async_copy(made[at].at[:, lanes], outs[at].at[:, lanes], sems.at[at, chunk])
            copy.start()
            copies.append(copy)
    for copy in copies:
        copy.wait()


def finish(places, step, turn, currents, images):
    ranks = len(currents)
    columns, count = currents[0].shape
    total = ranks * columns
    chunks = 2
    return pl.pallas_call(
        functools.partial(finish_kernel, ranks, chunks),
        in_specs=[SMEM] + [VMEM] * (2 * ranks + 2),
        out_specs=[pl.BlockSpec(memory_space=pl.ANY)] * 3,
        out_shape=[jax.ShapeDtypeStruct((columns, count), f32)] * 3,
        scratch_shapes=[pltpu.VMEM((columns, count), f32)] * 3
        + [pltpu.VMEM((total, count), f32)] * 2
        + [pltpu.SemaphoreType.DMA((3, chunks))],
        compiler_params=params(),
        cost_estimate=SMALL,
        name="finish",
    )(places, step, turn, *currents, *images)


def swap(value, axis, bits):
    size = lax.axis_size(axis)
    return lax.ppermute(value, axis, [(at, at ^ bits) for at in range(size)])


def pair_swap(value, bits, ranks):
    rank_bits, tri_bit = bits % ranks, bits // ranks
    if tri_bit == 0:
        return swap(value, "rhs", rank_bits)
    if rank_bits == 0:
        return swap(value, "tri", 1)
    count = lax.axis_size("tri")
    perm = [
        (tri * ranks + rank, (tri ^ 1) * ranks + (rank ^ rank_bits)) for tri in range(count) for rank in range(ranks)
    ]
    return lax.ppermute(value, ("tri", "rhs"), perm)


def indices(*values):
    return jnp.stack(values).astype(jnp.int32)


def all_sum(keep, give, beside, ranks, tris):
    value = keep + swap(give, "split", 1)
    value, give = jnp.split(value, 2)
    value = value + swap(give, "tri", 1)
    parts = [swap(value, "tri", 2 * far) for far in range(1, tris // 2)]
    parts, beside = lax.optimization_barrier((parts, beside))
    value = sum(parts, value)
    shares = [value] + [pair_swap(value, bits, ranks) for bits in range(1, 2 * ranks)]
    shares += [swap(share, "split", 1) for share in shares]
    return shares, beside


def body(residual, attach, vertices, corners, layers):
    columns, count = residual.shape
    tris, ranks, cores = lax.axis_size("tri"), lax.axis_size("rhs"), lax.axis_size("split")
    tri, rank, core = lax.axis_index("tri"), lax.axis_index("rhs"), lax.axis_index("split")
    near = min(4, tris)
    groups = tris // near
    scale = 1.0 / math.sqrt(corners.shape[1])

    my_ids = (tri * cores + core) * count + jnp.arange(count, dtype=jnp.int32)
    current = residual + inject * (attach[:, None] == my_ids[None, :]).astype(f32)
    packed = current.astype(bf16)
    currents = [current] + [swap(current, "rhs", bits) for bits in range(1, ranks)]
    sources = [packed] + [swap(packed, "tri", bits) for bits in range(1, near)]

    own_blocks = [(tri ^ (near * far)) * cores + core for far in range(groups)]
    near_blocks = [(tri ^ bits) * cores + core for bits in range(1, near)]
    blocks = indices(*reversed(near_blocks), *own_blocks)
    half_place = half_of(rank ^ 1, rank) if ranks > 1 else jnp.int32(0)
    first = indices(half_place)
    places = indices(*[rank ^ bits for bits in range(ranks)])
    low = tri & 1
    cuts = indices(2 * core + low, 2 * core + 1 - low, 2 - 2 * core + low, 3 - 2 * core - low)
    share_places = indices(
        *[
            (rank ^ (bits % ranks)) * 4 + (core ^ other) * 2 + (low ^ (bits // ranks))
            for other in range(2)
            for bits in range(2 * ranks)
        ]
    )
    vertices, packed, blocks, first, places, cuts, share_places = lax.optimization_barrier(
        (vertices, packed, blocks, first, places, cuts, share_places)
    )
    a_side, b_side, diag = geometry(blocks, near, vertices, corners, layers, count, scale)
    slots = list(reversed(range(near)))
    sides = [a_side, b_side, swap(b_side, "split", 1)]

    def part(which, targets, starts=None, **more):
        return image_part(
            first, sources[which], [(0, slot) for slot in slots[which]], sides, targets, starts, **more
        )

    fars = range(1, groups)
    arrived = [[], []]
    last = slice(near - 1, near)
    far_sum = []
    if groups > 1:
        own_at, other_at = ([(side, far, None) for far in fars] for side in (1, 2))
        far_own = part(slice(0, 1), own_at)
        sides, far_own = lax.optimization_barrier((sides, far_own))
        far_other = part(slice(0, 1), other_at)
        for at in range(1, near - 1):
            both = part(slice(at, at + 1), other_at + own_at, [*far_other, *far_own])
            far_other, far_own = both[: len(other_at)], both[len(other_at) :]
        ready = []
        sides, currents = lax.optimization_barrier((sides, currents))
        for half in range(2):
            ready.append(part(last, [(*at[:2], half) for at in other_at], far_other, kind=bf16))
            sides, _ = lax.optimization_barrier((sides, ready))
        sent = [[swap(value, "split", 1) for value in values] for values in ready]
        for half in range(2):
            far_sum.append(
                part(last, [(*at[:2], half) for at in own_at], far_own, extras=sent[half], kind=bf16)
            )
            arrived[half] = [swap(value, "tri", near * far) for far, value in zip(fars, far_sum[half])]
            sides, _ = lax.optimization_barrier((sides, far_sum))
        sources, _ = lax.optimization_barrier((sources, far_sum[0]))
    mine = stack_rows(sources, a_side, near)
    theirs = swap(mine, "split", 1)
    after, _ = lax.optimization_barrier((first, far_sum))
    own_first = own_image(0, after, [mine, theirs], b_side, near, True)
    after, _ = lax.optimization_barrier((first, own_first))
    own_second = own_image(1, after, [mine], b_side, near, True)
    own_first, own_second = lax.optimization_barrier((own_first, own_second))
    smooth, low_first = combine([own_first, *arrived[0]])
    after, _ = lax.optimization_barrier((first, low_first))
    own_second = own_image(1, after, [theirs], b_side, near, False, [own_second])
    blocks, image, low_second = gram_sums(places, first, diag, smooth, [own_second, *arrived[1]], currents)
    gots, rests = [], []
    for bits in range(1, ranks):
        if bits == 1:
            give, rest = low_first, low_second
        else:
            is_first = half_of(rank ^ bits, rank) == half_place
            give = jnp.where(is_first, low_first, low_second)
            rest = jnp.where(is_first, low_second, low_first)
        gots.append(swap(give, "rhs", bits))
        rests.append(rest)
    keep, give = cross_sums(places, cuts, blocks, image, diag, currents, gots)
    rests, _ = lax.optimization_barrier((rests, gots))
    rests = [swap(rest, "rhs", bits) for bits, rest in enumerate(rests, 1)]
    beside = other_images(places, diag, currents, gots, rests)
    shares, beside = all_sum(keep, give, beside, ranks, tris)
    step, turn = solve(places, share_places, shares, columns)
    return finish(places, step, turn, currents, [image, *beside])


def solution(mesh):
    return jax.shard_map(
        body,
        mesh=mesh,
        in_specs=(P("rhs", ("tri", "split")), P("rhs"), P(), P(), P()),
        out_specs=(
            P("rhs", ("tri", "split")),
            P("rhs", ("tri", "split")),
            P("rhs", ("tri", "split")),
        ),
        check_vma=False,
    )
```

```python
import functools
import math

import jax
import jax.numpy as jnp
from jax import lax
from jax.experimental import pallas as pl
from jax.experimental.pallas import tpu as pltpu
from jax.sharding import PartitionSpec as P

smooth_sq = 0.01
self_term = 1.0
inject = 3.0
f32 = jnp.float32
bf16 = jnp.bfloat16
LANES = 128
LOW = 64
FEATURES = 32
TILE = 512 * 1024
PAIRS = ((0, 0), (0, 1), (1, 0), (1, 1), (0, 2), (2, 0))
VMEM = pl.BlockSpec(memory_space=pltpu.VMEM)
SMEM = pl.BlockSpec(memory_space=pltpu.SMEM)
SMALL = pl.CostEstimate(flops=1024, bytes_accessed=1024, transcendentals=0)


def dot(a, b, ca, cb, precision=None):
    return lax.dot_general(
        a, b, (((ca,), (cb,)), ((), ())), precision=precision, preferred_element_type=f32
    )


def split(value):
    high = value.astype(bf16)
    return high, (value - high.astype(f32)).astype(bf16)


def close_dot(a, b, ca, cb):
    a_high, a_low = split(a)
    b_high, b_low = split(b)
    return (dot(a_low, b_high, ca, cb) + dot(a_high, b_low, ca, cb)) + dot(a_high, b_high, ca, cb)


def params(mebibytes=12):
    return pltpu.CompilerParams(vmem_limit_bytes=mebibytes * 1024 * 1024)


def pieces_of(value):
    high = value.astype(bf16).astype(f32)
    rest = value - high
    middle = rest.astype(bf16).astype(f32)
    return (high, middle, rest - middle)


def geometry_kernel(
    scale, near, blocks_ref, vertices_ref, corners_ref, layers_ref, a_ref, b_ref, diag_ref, plain, table, a_rows, b_rows
):
    count = corners_ref.shape[1]
    tops = plain.shape[0]

    @pl.when(pl.program_id(0) == 0)
    def _():
        for axis in range(3):
            for top in range(tops):
                plain[top : top + 1, axis * LANES : (axis + 1) * LANES] = vertices_ref[
                    axis : axis + 1, top * LANES : (top + 1) * LANES
                ]
        for axis in range(3):
            for side in range(2):
                begin = axis * LANES + side * LOW
                value = plain[:, begin : begin + LOW]
                high = value.astype(bf16)
                low = (value - high.astype(f32)).astype(bf16)
                for at, part in enumerate((high, low)):
                    row = (2 * at + side) * tops
                    table[row : row + tops, axis * LOW : (axis + 1) * LOW] = part

    top_iota = lax.broadcasted_iota(jnp.int32, (2 * tops, count), 0)
    low_iota = lax.broadcasted_iota(jnp.int32, (LOW, count), 0)
    points = []
    for corner in range(3):
        index = corners_ref[corner : corner + 1, :]
        place = (index >> 7) + tops * ((index >> 6) & 1)
        top = jnp.where(top_iota == place, 1.0, 0.0).astype(bf16)
        low = low_iota == (index & (LOW - 1))
        found = dot(table[...], jnp.concatenate([top, top], axis=0), 0, 0)
        points.append(
            [
                jnp.sum(jnp.where(low, found[axis * LOW : (axis + 1) * LOW], 0.0), axis=0, keepdims=True)
                for axis in range(3)
            ]
        )
    p0, p1, p2 = points
    centre = [(p0[k] + p1[k] + p2[k]) / 3.0 for k in range(3)]
    e1 = [p1[k] - p0[k] for k in range(3)]
    e2 = [p2[k] - p0[k] for k in range(3)]
    cross_x = e1[1] * e2[2] - e1[2] * e2[1]
    cross_y = e1[2] * e2[0] - e1[0] * e2[2]
    cross_z = e1[0] * e2[1] - e1[1] * e2[0]
    area_sq = cross_x * cross_x + cross_y * cross_y + cross_z * cross_z
    layers = layers_ref[...]
    factor = jnp.where(layers == 0, 1.0, jnp.where(layers == 1, 0.3, 0.8)).astype(f32)
    weight = factor * (0.5 + area_sq / (1.0 + area_sq))
    unit = 1.0 / (scale * (weight * weight))
    norm = centre[0] * centre[0] + centre[1] * centre[1] + centre[2] * centre[2]
    a_side = [unit * norm, unit] + [unit * c for c in centre]
    b_side = [unit, unit * (norm + smooth_sq)] + [-2.0 * unit * c for c in centre]
    block = pl.program_id(0)

    def store(values, which, rows, out_ref):
        parts = [pieces_of(value) for value in values]
        row = 0
        for pair in PAIRS:
            for term in range(5):
                rows[row : row + 1, :] = parts[term][pair[which]]
                row += 1
        rows[row:, :] = jnp.zeros((FEATURES - row, count), f32)
        out_ref[...] = rows[...].astype(bf16)

    @pl.when(block < near)
    def _():
        store(a_side, 0, a_rows, a_ref)

    @pl.when(block >= near - 1)
    def _():
        store(b_side, 1, b_rows, b_ref)

    @pl.when(block == near - 1)
    def _():
        diag_ref[...] = weight * weight * (lax.rsqrt(jnp.full_like(weight, smooth_sq)) * scale + self_term)


def geometry(blocks, near, vertices, corners, layers, count, scale):
    n = blocks.shape[0]
    points = vertices.shape[1]
    tops = points // LANES
    return pl.pallas_call(
        functools.partial(geometry_kernel, scale, near),
        grid_spec=pltpu.PrefetchScalarGridSpec(
            num_scalar_prefetch=1,
            grid=(n,),
            in_specs=[
                pl.BlockSpec((3, points), lambda g, blk: (0, 0)),
                pl.BlockSpec((3, count), lambda g, blk: (0, blk[g])),
                pl.BlockSpec((1, count), lambda g, blk: (0, blk[g])),
            ],
            out_specs=[
                pl.BlockSpec((None, FEATURES, count), lambda g, blk: (jnp.minimum(g, near - 1), 0, 0)),
                pl.BlockSpec((None, FEATURES, count), lambda g, blk: (jnp.maximum(g - near + 1, 0), 0, 0)),
                pl.BlockSpec((1, count), lambda g, blk: (0, 0)),
            ],
            scratch_shapes=[
                pltpu.VMEM((tops, 3 * LANES), f32),
                pltpu.VMEM((4 * tops, 3 * LOW), bf16),
                pltpu.VMEM((FEATURES, count), f32),
                pltpu.VMEM((FEATURES, count), f32),
            ],
        ),
        out_shape=(
            jax.ShapeDtypeStruct((near, FEATURES, count), bf16),
            jax.ShapeDtypeStruct((n - near + 1, FEATURES, count), bf16),
            jax.ShapeDtypeStruct((1, count), f32),
        ),
        compiler_params=params(),
        name="geometry",
    )(blocks, vertices, corners, layers[None, :])


def image_kernel(sources, slots, targets, has_start, extras, first_ref, *refs):
    refs = list(refs)
    densities = [refs.pop(0) for _ in sources]
    sides = [refs.pop(0) for _ in range(1 + max(which for which, _ in [*slots, *[t[:2] for t in targets]]))]
    starts = [refs.pop(0) for _ in targets] if has_start else [None] * len(targets)
    more = [refs.pop(0) for _ in range(extras)]
    count = densities[0].shape[1]
    half = count // 2
    for at, (which, slot, part) in enumerate(targets):
        columns, width = refs[at].shape
        chunk = min(TILE // width, count)
        if part is None:
            lanes = slice(None)
        else:
            place = first_ref[0] if part == 0 else 1 - first_ref[0]
            lanes = pl.ds(pl.multiple_of(place * half, half), half)
        b = sides[which][slot, :, lanes]
        acc = starts[at][:, lanes] if has_start else jnp.zeros((columns, width), f32)
        for source, (density, (side, a_slot)) in enumerate(zip(densities, slots)):
            for begin in range(0, count, chunk):
                tile = lax.rsqrt(dot(sides[side][a_slot, :, begin : begin + chunk], b, 0, 0))
                acc = acc + dot(density[:, begin : begin + chunk], tile.astype(bf16), 1, 0)
        if at < extras:
            acc = acc + more[at][...].astype(f32)
        refs[at][...] = acc.astype(refs[at].dtype)


def image_part(first, densities, slots, sides, targets, starts=None, extras=(), kind=f32):
    columns, count = densities[0].shape
    sides = sides[: 1 + max(which for which, _ in [*slots, *[t[:2] for t in targets]])]
    operands = [first, *densities, *sides, *(starts or []), *extras]
    widths = [count if part is None else count // 2 for _, _, part in targets]
    return pl.pallas_call(
        functools.partial(image_kernel, range(len(densities)), slots, targets, bool(starts), len(extras)),
        in_specs=[SMEM] + [VMEM] * (len(operands) - 1),
        out_specs=[VMEM] * len(targets),
        out_shape=[jax.ShapeDtypeStruct((columns, width), kind) for width in widths],
        compiler_params=params(12),
        cost_estimate=SMALL,
        name="image_part",
    )(*operands)


def half_of(mine, other):
    return (mine > other).astype(jnp.int32)


def stack_kernel(near, *refs):
    a_ref, out_ref = refs[near:]
    columns = refs[0].shape[0]
    for source in range(near):
        out_ref[source * columns : (source + 1) * columns, :] = refs[source][...]
        side = near * columns + source * FEATURES
        out_ref[side : side + FEATURES, :] = a_ref[near - 1 - source]


def stack_rows(sources, a_side, near):
    columns, count = sources[0].shape
    return pl.pallas_call(
        functools.partial(stack_kernel, near),
        in_specs=[VMEM] * (near + 1),
        out_specs=VMEM,
        out_shape=jax.ShapeDtypeStruct((near * (columns + FEATURES), count), bf16),
        compiler_params=params(),
        cost_estimate=SMALL,
        name="stack_rows",
    )(*sources, a_side)


def own_kernel(near, part, diagonal, stacks, first_ref, b_ref, *refs):
    out_ref = refs[-1]
    columns, width = out_ref.shape
    count = b_ref.shape[2]
    chunk = min(TILE // width, count)
    place = first_ref[0] if part == 0 else 1 - first_ref[0]
    b = b_ref[0, :, pl.ds(pl.multiple_of(place * width, width), width)]
    acc = refs[stacks][...] if len(refs) > stacks + 1 else jnp.zeros((columns, width), f32)
    for at, ref in enumerate(refs[:stacks]):
        for source in range(near):
            side = near * columns + source * FEATURES
            for begin in range(0, count, chunk):
                lanes = slice(begin, begin + chunk)
                tile = lax.rsqrt(dot(ref[side : side + FEATURES, lanes], b, 0, 0))
                if diagonal and at == 0 and source == 0:
                    rows = begin + lax.broadcasted_iota(jnp.int32, tile.shape, 0)
                    cols = place * width + lax.broadcasted_iota(jnp.int32, tile.shape, 1)
                    tile = jnp.where(rows == cols, 0.0, tile)
                acc = acc + dot(ref[source * columns : (source + 1) * columns, lanes], tile.astype(bf16), 1, 0)
    out_ref[...] = acc


def own_image(part, first, stacks, b_side, near, diagonal, start=()):
    rows, count = stacks[0].shape
    columns = rows // near - FEATURES
    operands = [b_side, *stacks, *start]
    return pl.pallas_call(
        functools.partial(own_kernel, near, part, diagonal, len(stacks)),
        in_specs=[SMEM] + [VMEM] * len(operands),
        out_specs=VMEM,
        out_shape=jax.ShapeDtypeStruct((columns, count // 2), f32),
        compiler_params=params(12),
        cost_estimate=SMALL,
        name="own_image",
    )(first, *operands)


def add_parts(refs):
    total = refs[0][...].astype(f32)
    for ref in refs[1:]:
        total = total + ref[...].astype(f32)
    return total


def combine_kernel(*refs):
    smooth = add_parts(refs[:-2])
    refs[-2][...] = smooth
    refs[-1][...] = smooth.astype(bf16)


def combine(parts):
    return pl.pallas_call(
        combine_kernel,
        in_specs=[VMEM] * len(parts),
        out_specs=[VMEM] * 2,
        out_shape=[jax.ShapeDtypeStruct(parts[0].shape, kind) for kind in (f32, bf16)],
        compiler_params=params(),
        cost_estimate=SMALL,
        name="combine",
    )(*parts)


def full_image(first_ref, diag_ref, current_ref, smooths, image_ref):
    half = smooths[0].shape[1]
    for place, smooth in zip((first_ref[0], 1 - first_ref[0]), smooths):
        lanes = pl.ds(pl.multiple_of(place * half, half), half)
        fixed = diag_ref[:, lanes].astype(bf16).astype(f32) * current_ref[:, lanes].astype(bf16).astype(f32)
        image_ref[:, lanes] = smooth + fixed


def gram_kernel(ranks, place_ref, first_ref, diag_ref, first_half, *refs):
    currents, parts, (block, image, low) = refs[:ranks], refs[ranks:-3], refs[-3:]
    columns = currents[0].shape[0]
    second_half = add_parts(parts)
    low[...] = second_half.astype(bf16)
    full_image(first_ref, diag_ref, currents[0], (first_half[...], second_half), image)
    mine = currents[0][...]
    half = columns // 2
    for rank in range(ranks):
        current = currents[rank][...]
        block[rank, :columns] = close_dot(image[...], current, 1, 1)
        if rank > 0:
            ahead = place_ref[0] < place_ref[rank]
            left = jnp.where(ahead, mine[:half], current[half:])
            block[rank, 2 * columns : 2 * columns + half] = close_dot(left, jnp.where(ahead, current, mine), 1, 1)
    square = close_dot(mine, mine, 1, 1)
    row_at = lax.broadcasted_iota(jnp.int32, square.shape, 0)
    col_at = lax.broadcasted_iota(jnp.int32, square.shape, 1)
    block[0, columns : 2 * columns] = jnp.where(row_at > col_at, square, close_dot(image[...], image[...], 1, 1))
    diagonal = jnp.sum(jnp.where(row_at == col_at, square, 0.0), axis=0, keepdims=True)
    block[0, 2 * columns : 2 * columns + half] = jnp.broadcast_to(diagonal, (half, columns))
    spare = block.shape[1] - 2 * columns - half
    if spare > 0:
        block[:, 2 * columns + half :] = jnp.zeros((ranks, spare, columns), f32)


def sum_rows(columns):
    return -(-5 * columns // 64) * 32


def gram_sums(places, first, diag, smooth, parts, currents):
    ranks = len(currents)
    columns, count = currents[0].shape
    return pl.pallas_call(
        functools.partial(gram_kernel, ranks),
        in_specs=[SMEM] * 2 + [VMEM] * (ranks + len(parts) + 2),
        out_specs=[VMEM] * 3,
        out_shape=(
            jax.ShapeDtypeStruct((ranks, sum_rows(columns), columns), f32),
            jax.ShapeDtypeStruct((columns, count), f32),
            jax.ShapeDtypeStruct((columns, count // 2), bf16),
        ),
        compiler_params=params(),
        cost_estimate=SMALL,
        name="gram",
    )(places, first, diag, smooth, *currents, *parts)


def cross_kernel(ranks, place_ref, cut_ref, block_ref, image_ref, diag_ref, *refs):
    currents, gots = refs[: ranks - 1], refs[ranks - 1 : 2 * ranks - 2]
    keep_ref, give_ref, sums, block = refs[2 * ranks - 2 :]
    columns, count = image_ref.shape
    half = count // 2
    block[...] = block_ref[...]
    for rank in range(1, ranks):
        which = half_of(place_ref[0], place_ref[rank])
        lanes = pl.ds(pl.multiple_of(which * half, half), half)
        current = currents[rank - 1][:, lanes].astype(bf16).astype(f32)
        other = gots[rank - 1][...].astype(f32) + diag_ref[:, lanes].astype(bf16).astype(f32) * current
        block[rank, columns : 2 * columns] = close_dot(image_ref[:, lanes], other, 1, 1)
    for place in range(ranks):
        rank = jnp.bitwise_xor(place_ref[0], place)
        sums[:, place * columns : (place + 1) * columns] = block[rank]
    rows = keep_ref.shape[0] // 2
    for at, ref in enumerate((keep_ref, keep_ref, give_ref, give_ref)):
        begin = pl.multiple_of(cut_ref[at] * rows, rows)
        ref[at % 2 * rows : (at % 2 + 1) * rows, :] = sums[pl.ds(begin, rows), :]


def cross_sums(places, cuts, blocks, image, diag, currents, gots):
    ranks = len(currents)
    columns, count = image.shape
    total = ranks * columns
    rows = sum_rows(columns)
    half = jax.ShapeDtypeStruct((rows // 2, total), f32)
    return pl.pallas_call(
        functools.partial(cross_kernel, ranks),
        in_specs=[SMEM, SMEM] + [VMEM] * (2 * ranks + 1),
        out_specs=[VMEM] * 2,
        out_shape=(half, half),
        scratch_shapes=[
            pltpu.VMEM((rows, total), f32),
            pltpu.VMEM((ranks, rows, columns), f32),
        ],
        compiler_params=params(),
        cost_estimate=SMALL,
        name="cross",
    )(places, cuts, blocks, image, diag, *currents[1:], *gots)


def reciprocal(value):
    guess = pl.reciprocal(value, approx=True)
    return guess * (2.0 - value * guess)


def eliminate(panel, begin, window):
    size, total = panel.shape
    parts = [panel[:, at : at + LANES] for at in range(0, total, LANES)]
    row_at = lax.broadcasted_iota(jnp.int32, (size, LANES), 0)
    col_at = lax.broadcasted_iota(jnp.int32, (1, LANES), 1)

    def spread(pivot):
        place = (begin + pivot) % LANES
        return jnp.broadcast_to(parts[(begin + pivot) // LANES][:, place : place + 1], (size, LANES))

    cols = [spread(pivot) for pivot in range(window)]
    for pivot in range(size):
        col = cols.pop(0)
        inverse = reciprocal(col[pivot : pivot + 1, :])
        col = col - jnp.where(row_at == pivot, 1.0, 0.0)
        for part in range(len(parts)):
            row = parts[part][pivot : pivot + 1, :]
            if part == (begin + pivot) // LANES:
                row = row + jnp.where(col_at == (begin + pivot) % LANES, 1.0, 0.0)
            parts[part] = parts[part] - col * (row * inverse)
        cols = [later - col * (later[pivot : pivot + 1, :] * inverse) for later in cols]
        if pivot + window < size:
            cols.append(spread(pivot + window))
    return jnp.concatenate(parts, axis=1)


def sweep(ref, begin, size):
    total = ref.shape[0]
    panel = ref[begin : begin + size, :]
    row = eliminate(panel, begin, 6)
    col_at = lax.broadcasted_iota(jnp.int32, panel.shape, 1)
    left = [part.astype(bf16) for part in pieces_of(jnp.where(col_at < begin, -panel, panel))]
    right = [part.astype(bf16) for part in pieces_of(row)]
    update = dot(
        jnp.concatenate([left[at] for at, _ in PAIRS], axis=0),
        jnp.concatenate([right[at] for _, at in PAIRS], axis=0),
        0,
        0,
    )
    lanes = lax.broadcasted_iota(jnp.int32, (total, total), 1)
    ref[...] = jnp.where((lanes >= begin) & (lanes < begin + size), 0.0, ref[...]) - update
    ref[begin : begin + size, :] = row


def solve_kernel(columns, size, place_ref, share_ref, *refs):
    shares = refs[:-7]
    step_ref, turn_ref, sums, grams, gram_inv, square_inv, step_all = refs[-7:]
    rows, total = shares[0].shape
    for at, share in enumerate(shares):
        sums[pl.ds(pl.multiple_of(share_ref[at] * rows, rows), rows), :] = share[...]
    ranks = total // columns
    height = sums.shape[0] // ranks
    half = columns // 2
    row_at = lax.broadcasted_iota(jnp.int32, (total, total), 0)
    col_at = lax.broadcasted_iota(jnp.int32, (total, total), 1)
    same = row_at // columns == col_at // columns
    lanes = col_at[:1] // columns
    diagonal = jnp.zeros((1, total), f32)
    grams[1] = jnp.zeros((total, total), f32)
    for rank in range(ranks):
        mine = slice(rank * columns, (rank + 1) * columns)
        base = rank * height
        grams[0, mine, :] = sums[base : base + columns, :]
        grams[2, mine, :] = sums[base + columns : base + 2 * columns, :]
        base += 2 * columns
        diagonal = jnp.where(lanes == rank, sums[base : base + 1, :], diagonal)
        for other in range(ranks):
            block = sums[base : base + half, other * columns : (other + 1) * columns]
            if other > rank:
                grams[1, rank * columns : rank * columns + half, other * columns : (other + 1) * columns] = block
            if other < rank:
                grams[1, other * columns + half : (other + 1) * columns, mine] = block
    pairs = grams[2]
    flipped = pairs.T
    across = grams[1]
    own = jnp.where(row_at > col_at, pairs, jnp.where(row_at < col_at, flipped, diagonal))
    grams[1] = jnp.where(same, own, across + across.T)
    grams[2] = jnp.where(same, jnp.where(row_at > col_at, flipped, pairs), pairs + flipped)
    cross = grams[0]
    gram = 0.5 * (cross + cross.T)
    gram_scale = 1.0 / jnp.max(gram, keepdims=True)
    square_scale = 1.0 / jnp.max(grams[1], keepdims=True)
    gram_inv[...] = gram * gram_scale
    square_inv[...] = grams[1] * square_scale
    for begin in range(0, total, size):
        sweep(gram_inv, begin, size)
        sweep(square_inv, begin, size)
    mine = pl.ds(pl.multiple_of(place_ref[0] * columns, columns), columns)
    step_all[...] = close_dot(grams[1], gram_inv[...] * gram_scale, 1, 0)
    step = step_all[mine, :]
    step_ref[...] = step
    left = close_dot(step, grams[2], 1, 0)
    across = close_dot(step, grams[0], 1, 0)
    grams[0] = grams[0].T
    left = left - grams[0, mine, :]
    following = grams[1, mine, :] - across + close_dot(left, step_all[...], 1, 1)
    turn_ref[...] = close_dot(following, square_inv[...] * square_scale, 1, 0)


def solve(places, share_places, shares, columns):
    total = shares[0].shape[1]
    square = pltpu.VMEM((total, total), f32)
    rows = jax.ShapeDtypeStruct((columns, total), f32)
    return pl.pallas_call(
        functools.partial(solve_kernel, columns, 32),
        in_specs=[SMEM, SMEM] + [VMEM] * len(shares),
        out_specs=[VMEM] * 2,
        out_shape=(rows, rows),
        scratch_shapes=[
            pltpu.VMEM((total // columns * sum_rows(columns), total), f32),
            pltpu.VMEM((3, total, total), f32),
            square,
            square,
            square,
        ],
        compiler_params=params(),
        name="solve",
    )(places, share_places, *shares)


def others_kernel(ranks, place_ref, diag_ref, *refs):
    currents, gots, rests, outs = (refs[at * (ranks - 1) : (at + 1) * (ranks - 1)] for at in range(4))
    half = diag_ref.shape[1] // 2
    for at in range(ranks - 1):
        which = half_of(place_ref[0], place_ref[at + 1])
        for place, smooth in ((which, gots[at]), (1 - which, rests[at])):
            lanes = pl.ds(pl.multiple_of(place * half, half), half)
            fixed = diag_ref[:, lanes].astype(bf16).astype(f32) * currents[at][:, lanes].astype(bf16).astype(f32)
            outs[at][:, lanes] = smooth[...].astype(f32) + fixed


def other_images(places, diag, currents, gots, rests):
    ranks = len(currents)
    return pl.pallas_call(
        functools.partial(others_kernel, ranks),
        in_specs=[SMEM] + [VMEM] * (3 * ranks - 2),
        out_specs=[VMEM] * (ranks - 1),
        out_shape=[jax.ShapeDtypeStruct(currents[0].shape, f32)] * (ranks - 1),
        compiler_params=params(),
        cost_estimate=SMALL,
        name="other_images",
    )(places, diag, *currents[1:], *gots, *rests)


def finish_kernel(ranks, chunks, place_ref, step_ref, turn_ref, *refs):
    currents, images, refs = refs[:ranks], refs[ranks : 2 * ranks], refs[2 * ranks :]
    outs, made, (current_all, image_all, sems) = refs[:3], refs[3:6], refs[6:]
    columns, count = currents[0].shape
    for rank in range(ranks):
        at = pl.ds(pl.multiple_of(place_ref[rank] * columns, columns), columns)
        current_all[at, :] = currents[rank][...]
        image_all[at, :] = images[rank][...]
    step_high, step_low = split(step_ref[...])
    turn_high, turn_low = split(turn_ref[...])
    both = jnp.concatenate([step_high, step_low, turn_high, turn_low], axis=0)
    highs = jnp.concatenate([step_high, turn_high], axis=0)
    steps = jnp.concatenate([step_high, step_low], axis=0)
    width = count // chunks
    copies = []
    for chunk in range(chunks):
        lanes = pl.ds(chunk * width, width)
        current_high, current_low = split(current_all[:, lanes])
        image_high, image_low = split(image_all[:, lanes])
        every = dot(both, current_high, 1, 0)
        rest = dot(highs, current_low, 1, 0)
        away = dot(steps, image_high, 1, 0)
        step_part, step_more, turn_part, turn_more = (every[at * columns : (at + 1) * columns] for at in range(4))
        away = away[:columns] + (away[columns:] + dot(step_high, image_low, 1, 0))
        remainder = currents[0][:, lanes] - away
        made[0][:, lanes] = step_part + (step_more + rest[:columns])
        made[1][:, lanes] = remainder
        made[2][:, lanes] = remainder + (turn_part + (turn_more + rest[columns:]))
        for at in range(3):
            copy = pltpu.make_async_copy(made[at].at[:, lanes], outs[at].at[:, lanes], sems.at[at, chunk])
            copy.start()
            copies.append(copy)
    for copy in copies:
        copy.wait()


def finish(places, step, turn, currents, images):
    ranks = len(currents)
    columns, count = currents[0].shape
    total = ranks * columns
    chunks = 2
    return pl.pallas_call(
        functools.partial(finish_kernel, ranks, chunks),
        in_specs=[SMEM] + [VMEM] * (2 * ranks + 2),
        out_specs=[pl.BlockSpec(memory_space=pl.ANY)] * 3,
        out_shape=[jax.ShapeDtypeStruct((columns, count), f32)] * 3,
        scratch_shapes=[pltpu.VMEM((columns, count), f32)] * 3
        + [pltpu.VMEM((total, count), f32)] * 2
        + [pltpu.SemaphoreType.DMA((3, chunks))],
        compiler_params=params(),
        cost_estimate=SMALL,
        name="finish",
    )(places, step, turn, *currents, *images)


def swap(value, axis, bits):
    size = lax.axis_size(axis)
    return lax.ppermute(value, axis, [(at, at ^ bits) for at in range(size)])


def pair_swap(value, bits, ranks):
    rank_bits, tri_bit = bits % ranks, bits // ranks
    if tri_bit == 0:
        return swap(value, "rhs", rank_bits)
    if rank_bits == 0:
        return swap(value, "tri", 1)
    count = lax.axis_size("tri")
    perm = [
        (tri * ranks + rank, (tri ^ 1) * ranks + (rank ^ rank_bits)) for tri in range(count) for rank in range(ranks)
    ]
    return lax.ppermute(value, ("tri", "rhs"), perm)


def indices(*values):
    return jnp.stack(values).astype(jnp.int32)


def all_sum(keep, give, beside, ranks, tris):
    value = keep + swap(give, "split", 1)
    value, give = jnp.split(value, 2)
    value = value + swap(give, "tri", 1)
    parts = [swap(value, "tri", 2 * far) for far in range(1, tris // 2)]
    parts, beside = lax.optimization_barrier((parts, beside))
    value = sum(parts, value)
    shares = [value] + [pair_swap(value, bits, ranks) for bits in range(1, 2 * ranks)]
    shares += [swap(share, "split", 1) for share in shares]
    return shares, beside


def body(residual, attach, vertices, corners, layers):
    columns, count = residual.shape
    tris, ranks, cores = lax.axis_size("tri"), lax.axis_size("rhs"), lax.axis_size("split")
    tri, rank, core = lax.axis_index("tri"), lax.axis_index("rhs"), lax.axis_index("split")
    near = min(4, tris)
    groups = tris // near
    scale = 1.0 / math.sqrt(corners.shape[1])

    my_ids = (tri * cores + core) * count + jnp.arange(count, dtype=jnp.int32)
    current = residual + inject * (attach[:, None] == my_ids[None, :]).astype(f32)
    packed = current.astype(bf16)
    currents = [current] + [swap(current, "rhs", bits) for bits in range(1, ranks)]
    sources = [packed] + [swap(packed, "tri", bits) for bits in range(1, near)]

    own_blocks = [(tri ^ (near * far)) * cores + core for far in range(groups)]
    near_blocks = [(tri ^ bits) * cores + core for bits in range(1, near)]
    blocks = indices(*reversed(near_blocks), *own_blocks)
    half_place = half_of(rank ^ 1, rank) if ranks > 1 else jnp.int32(0)
    first = indices(half_place)
    places = indices(*[rank ^ bits for bits in range(ranks)])
    low = tri & 1
    cuts = indices(2 * core + low, 2 * core + 1 - low, 2 - 2 * core + low, 3 - 2 * core - low)
    share_places = indices(
        *[
            (rank ^ (bits % ranks)) * 4 + (core ^ other) * 2 + (low ^ (bits // ranks))
            for other in range(2)
            for bits in range(2 * ranks)
        ]
    )
    vertices, packed, blocks, first, places, cuts, share_places = lax.optimization_barrier(
        (vertices, packed, blocks, first, places, cuts, share_places)
    )
    a_side, b_side, diag = geometry(blocks, near, vertices, corners, layers, count, scale)
    slots = list(reversed(range(near)))
    sides = [a_side, b_side, swap(b_side, "split", 1)]

    def part(which, targets, starts=None, **more):
        return image_part(
            first, sources[which], [(0, slot) for slot in slots[which]], sides, targets, starts, **more
        )

    fars = range(1, groups)
    arrived = [[], []]
    last = slice(near - 1, near)
    far_sum = []
    if groups > 1:
        own_at, other_at = ([(side, far, None) for far in fars] for side in (1, 2))
        far_own = part(slice(0, 1), own_at)
        sides, far_own = lax.optimization_barrier((sides, far_own))
        far_other = part(slice(0, 1), other_at)
        for at in range(1, near - 1):
            both = part(slice(at, at + 1), other_at + own_at, [*far_other, *far_own])
            far_other, far_own = both[: len(other_at)], both[len(other_at) :]
        ready = []
        sides, currents = lax.optimization_barrier((sides, currents))
        for half in range(2):
            ready.append(part(last, [(*at[:2], half) for at in other_at], far_other, kind=bf16))
            sides, _ = lax.optimization_barrier((sides, ready))
        sent = [[swap(value, "split", 1) for value in values] for values in ready]
        for half in range(2):
            far_sum.append(
                part(last, [(*at[:2], half) for at in own_at], far_own, extras=sent[half], kind=bf16)
            )
            arrived[half] = [swap(value, "tri", near * far) for far, value in zip(fars, far_sum[half])]
            if half == 0:
                sources, _ = lax.optimization_barrier((sources, far_sum[0]))
                mine = stack_rows(sources, a_side, near)
                theirs = swap(mine, "split", 1)
                after, _ = lax.optimization_barrier((first, far_sum[0]))
                own_first = own_image(0, after, [mine], b_side, near, True)
                sides, _ = lax.optimization_barrier((sides, own_first))
    else:
        mine = stack_rows(sources, a_side, near)
        theirs = swap(mine, "split", 1)
        own_first = own_image(0, first, [mine], b_side, near, True)
    after, _, _ = lax.optimization_barrier((first, far_sum, own_first))
    own_first = own_image(0, after, [theirs], b_side, near, False, [own_first])
    after, _ = lax.optimization_barrier((first, own_first))
    own_second = own_image(1, after, [mine], b_side, near, True)
    own_first, own_second = lax.optimization_barrier((own_first, own_second))
    smooth, low_first = combine([own_first, *arrived[0]])
    after, _ = lax.optimization_barrier((first, low_first))
    own_second = own_image(1, after, [theirs], b_side, near, False, [own_second])
    blocks, image, low_second = gram_sums(places, first, diag, smooth, [own_second, *arrived[1]], currents)
    gots, rests = [], []
    for bits in range(1, ranks):
        if bits == 1:
            give, rest = low_first, low_second
        else:
            is_first = half_of(rank ^ bits, rank) == half_place
            give = jnp.where(is_first, low_first, low_second)
            rest = jnp.where(is_first, low_second, low_first)
        gots.append(swap(give, "rhs", bits))
        rests.append(rest)
    keep, give = cross_sums(places, cuts, blocks, image, diag, currents, gots)
    rests, _ = lax.optimization_barrier((rests, gots))
    rests = [swap(rest, "rhs", bits) for bits, rest in enumerate(rests, 1)]
    beside = other_images(places, diag, currents, gots, rests)
    shares, beside = all_sum(keep, give, beside, ranks, tris)
    step, turn = solve(places, share_places, shares, columns)
    return finish(places, step, turn, currents, [image, *beside])


def solution(mesh):
    return jax.shard_map(
        body,
        mesh=mesh,
        in_specs=(P("rhs", ("tri", "split")), P("rhs"), P(), P(), P()),
        out_specs=(
            P("rhs", ("tri", "split")),
            P("rhs", ("tri", "split")),
            P("rhs", ("tri", "split")),
        ),
        check_vma=False,
    )
```
